32 devices in a mesh: row: 4 (over x, core), col: 8 (over z, y).
Axes of the slice: x: 2, y: 2, z: 4, core: 2. Of those that a mesh axis runs over, the one named last changes fastest.
Arguments:
- grad: bfloat16 [2048, 7168], P('row', 'col'), may hold values from -18 to 18
- weight: float32 [2048, 7168], P('row', 'col'), may hold values from -6 to 6
- moment: float32 [2048, 7168], P('row', 'col'), may hold values from -18 to 18
- second: float32 [2048, 7168], P('row', 'col'), may hold values from 1 to 30
- gram_left: float32 [4, 512, 512], P('row', 'col'), may hold values from -1.2 to 12, as said below
- basis_left: float32 [4, 512, 512], P('row', 'col'), may hold values from -0.5 to 1.5, as said below
- gram_right: float32 [8, 896, 896], P('col', 'row'), may hold values from -1.2 to 12, as said below
- basis_right: float32 [8, 896, 896], P('col', 'row'), may hold values from -0.5 to 1.5, as said below
Outputs:
- new_weight: float32 [2048, 7168], P('row', 'col')
- new_moment: float32 [2048, 7168], P('row', 'col')
- new_second: float32 [2048, 7168], P('row', 'col')
- new_gram_left: float32 [4, 512, 512], P('row', 'col')
- new_basis_left: float32 [4, 512, 512], P('row', 'col')
- new_gram_right: float32 [8, 896, 896], P('col', 'row')
- new_basis_right: float32 [8, 896, 896], P('col', 'row')
The draws below stay inside these ranges and needn't reach their ends.
Inputs may be any that keep to these rules, and one draw needn't show every extreme that they name: `gram_left`: every block is symmetric and positive definite. `basis_left`: every block is invertible. `gram_right`: every block is symmetric and positive definite. `basis_right`: every block is invertible.
All inputs are finite; a program needn't handle non-finite values.
Results may differ from the reference program's by a relative error of at most 0.0012.
Values may be sent and summed in bfloat16 or wider, within the bound.
No kernel may reach another device: no remote copies, remote signals or barrier semaphores. Data moves between devices by JAX's collectives and lax.ppermute only.
A program may use at most 128 MiB of HBM per device.

```python
import math
import jax
import jax.numpy as jnp
from jax import lax

BL = 512
BR = 896
D_OUT = 2048
D_IN = 7168
N_ROW = 4
N_COL = 8


def symmetric_blocks(noise, diagonal):
    eye = jnp.eye(noise.shape[-1], dtype=jnp.float32)
    mixed = 0.5 * (noise + jnp.swapaxes(noise, 1, 2))
    return mixed * (1.0 - eye) + eye * diagonal[:, :, None]


def draw_gram_left(key, part):
    key = jax.random.fold_in(key, 11)
    noise_key, diag_key = jax.random.split(key)
    noise = jax.random.uniform(noise_key, (N_ROW, BL, BL), jnp.float32, -3.5, 3.5) / math.sqrt(BL)
    diagonal = jnp.exp(jax.random.uniform(diag_key, (N_ROW, BL), jnp.float32, math.log(4.0), math.log(12.0)))
    return symmetric_blocks(noise, diagonal)


def draw_gram_right(key, part):
    key = jax.random.fold_in(key, 17)
    noise_key, diag_key = jax.random.split(key)
    noise = jax.random.uniform(noise_key, (N_COL, BR, BR), jnp.float32, -3.5, 3.5) / math.sqrt(BR)
    diagonal = jnp.exp(jax.random.uniform(diag_key, (N_COL, BR), jnp.float32, math.log(4.0), math.log(12.0)))
    return symmetric_blocks(noise, diagonal)


def draw_basis_left(key, part):
    key = jax.random.fold_in(key, 13)
    noise = jnp.clip(jax.random.normal(key, (N_ROW, BL, BL), jnp.float32), -4.0, 4.0) * (0.3 / math.sqrt(BL))
    return jnp.eye(BL, dtype=jnp.float32)[None] + noise


def draw_basis_right(key, part):
    key = jax.random.fold_in(key, 19)
    noise = jnp.clip(jax.random.normal(key, (N_COL, BR, BR), jnp.float32), -4.0, 4.0) * (0.3 / math.sqrt(BR))
    return jnp.eye(BR, dtype=jnp.float32)[None] + noise


def block_scale(own_key, extent, cuts, least, high):
    gain, own = 1.0, jax.random.fold_in(own_key, 6)
    for axis_at, shards_of in cuts:
        heights = jnp.exp(jax.random.uniform(jax.random.fold_in(own, axis_at), (shards_of,), jnp.float32, least / len(cuts), high / len(cuts)))
        gain = gain * jnp.repeat(heights, extent[axis_at] // shards_of).reshape([-1 if axis == axis_at else 1 for axis in range(len(extent))])
    return gain


def centred(rng, shape, deviation, most, cuts=(), kind=jnp.bfloat16):
    array = jax.random.normal(rng, shape, jnp.float32) * deviation
    if len(cuts) > 0:
        array = block_scale(rng, shape, cuts, -0.22, 0.18) * array
    return jnp.clip(array, min=-most, max=most).astype(kind)


def setup_inputs(seed: int = 0) -> dict:
    key_of = jax.random.split(jax.random.key(seed), 9)
    return {
        "grad": centred(key_of[0], (D_OUT, D_IN), 3.0, 18.0, ((0, 4), (1, 8))),
        "weight": centred(key_of[1], (D_OUT, D_IN), 1.0, 6.0, ((0, 4), (1, 8)), jnp.float32),
        "moment": centred(key_of[2], (D_OUT, D_IN), 3.0, 18.0, ((0, 4), (1, 8)), jnp.float32),
        "second": jnp.clip(jnp.exp(math.log(30.0) - 3.4011974 * jax.random.uniform(key_of[3], (D_OUT, D_IN), jnp.float32) ** block_scale(key_of[3], (D_OUT, D_IN), ((0, 4), (1, 8)), -0.2, 0.2)), 1.0, 30.0),
        "gram_left": draw_gram_left(jax.random.fold_in(key_of[8], 71), 0),
        "basis_left": draw_basis_left(jax.random.fold_in(key_of[8], 71), 0),
        "gram_right": draw_gram_right(jax.random.fold_in(key_of[8], 71), 0),
        "basis_right": draw_basis_right(jax.random.fold_in(key_of[8], 71), 0),
    }


STAT_DECAY = 0.95
FIRST_DECAY = 0.9
SECOND_DECAY = 0.95
EPSILON = 1e-08
STEP_SIZE = 0.02
WEIGHT_DECAY = 0.01
HIGHEST = lax.Precision.HIGHEST

def orthonormal_rows(rows, cross):
    lower = jnp.linalg.cholesky(cross)
    return lax.linalg.triangular_solve(lower, rows, left_side=False, lower=True, transpose_a=True)

def orthonormal(matrix):
    cross = jnp.dot(matrix.T.astype(jnp.float32), matrix.astype(jnp.float32), precision=HIGHEST, preferred_element_type=jnp.float32)
    return orthonormal_rows(matrix, cross)

def left_gram(block):
    return jnp.dot(block.astype(jnp.float32), block.T.astype(jnp.float32), preferred_element_type=jnp.float32)

def right_gram(block):
    return jnp.dot(block.T.astype(jnp.float32), block.astype(jnp.float32), preferred_element_type=jnp.float32)

def left_turn(pair):
    return jnp.dot(pair[0].T.astype(jnp.float32), pair[1].astype(jnp.float32), preferred_element_type=jnp.float32).astype(jnp.bfloat16)

def right_turn(pair):
    return jnp.dot(pair[0].astype(jnp.float32), pair[1].astype(jnp.float32), preferred_element_type=jnp.float32)

def left_back(pair):
    return jnp.dot(pair[0].astype(jnp.float32), pair[1].astype(jnp.float32), preferred_element_type=jnp.float32).astype(jnp.bfloat16)

def right_back(pair):
    return jnp.dot(pair[0].astype(jnp.float32), pair[1].T.astype(jnp.float32), preferred_element_type=jnp.float32)

def by_columns(matrix):
    return jnp.swapaxes(matrix.reshape(D_OUT, N_COL, BR), 0, 1)

def from_columns(blocks):
    return jnp.swapaxes(blocks, 0, 1).reshape(D_OUT, D_IN)

def rotate_in(matrix, left_half, right_half):
    inner = lax.map(left_turn, (left_half, matrix.reshape(N_ROW, BL, D_IN)))
    outer = lax.map(right_turn, (by_columns(inner.reshape(D_OUT, D_IN)), right_half))
    return from_columns(outer)

def rotate_out(matrix, left_half, right_half):
    inner = lax.map(left_back, (left_half, matrix.reshape(N_ROW, BL, D_IN)))
    outer = lax.map(right_back, (by_columns(inner.reshape(D_OUT, D_IN)), right_half))
    return from_columns(outer)

def reference(grad, weight, moment, second, gram_left, basis_left, gram_right, basis_right):
    part_left = lax.map(left_gram, grad.reshape(N_ROW, BL, D_IN)) / D_IN
    part_right = lax.map(right_gram, by_columns(grad)) / D_OUT
    new_gram_left = STAT_DECAY * gram_left + (1.0 - STAT_DECAY) * part_left
    new_gram_right = STAT_DECAY * gram_right + (1.0 - STAT_DECAY) * part_right
    image_left = jnp.matmul(new_gram_left, basis_left, precision=HIGHEST)
    image_right = jnp.matmul(new_gram_right, basis_right, precision=HIGHEST)
    new_basis_left = lax.map(orthonormal, image_left)
    new_basis_right = lax.map(orthonormal, image_right)
    left_half = new_basis_left.astype(jnp.bfloat16)
    right_half = new_basis_right.astype(jnp.bfloat16)
    rotated_grad = rotate_in(grad, left_half, right_half)
    new_moment = FIRST_DECAY * moment + (1.0 - FIRST_DECAY) * grad.astype(jnp.float32)
    new_second = SECOND_DECAY * second + (1.0 - SECOND_DECAY) * rotated_grad * rotated_grad
    rotated_moment = rotate_in(new_moment.astype(jnp.bfloat16), left_half, right_half)
    direction = (rotated_moment / (jnp.sqrt(new_second) + EPSILON)).astype(jnp.bfloat16)
    update = rotate_out(direction, left_half, right_half)
    new_weight = weight - STEP_SIZE * (update + WEIGHT_DECAY * weight)
    return (new_weight, new_moment, new_second, new_gram_left, new_basis_left, new_gram_right, new_basis_right)
```

```python
import functools
import jax
import jax.numpy as jnp
from jax import lax
from jax.experimental import pallas as pl
from jax.experimental.pallas import tpu as pltpu

LANES = 128
ROWS = 8


def lane_mask(step):
    lanes = lax.broadcasted_iota(jnp.int32, (ROWS, LANES), 1)
    return (lanes >= step * ROWS) & (lanes < (step + 1) * ROWS)


def sub_row(x, k):
    return jnp.broadcast_to(x[k : k + 1, :], (ROWS, LANES))


def lane_col(x, c):
    return jnp.broadcast_to(x[:, c : c + 1], (ROWS, LANES))


def reciprocal(p):
    guess = pl.reciprocal(p, approx=True)
    return guess * (2.0 - p * guess)


def inverse_factor(rows):
    count = LANES // ROWS
    rows = list(rows)
    subs = lax.broadcasted_iota(jnp.int32, (ROWS, LANES), 0)
    lanes = lax.broadcasted_iota(jnp.int32, (ROWS, LANES), 1)
    out = []
    for s in range(count):
        base = s * ROWS
        pivot = rows[s]
        here = (lanes >= base) & (lanes < base + ROWS)
        cols = [lane_col(pivot, base + k) for k in range(ROWS)]
        full = jnp.where(here, (lanes == subs + base).astype(jnp.float32), pivot)
        forward = full
        inverse = jnp.zeros((ROWS, LANES), jnp.float32)
        pivots = jnp.ones((ROWS, LANES), jnp.float32)
        for j in range(ROWS):
            value = sub_row(cols[j], j)
            inv = reciprocal(value)
            scaled = cols[j] * inv
            m_full = jnp.where(subs == j, 0.0, scaled)
            for k in range(j + 1, ROWS):
                cols[k] = cols[k] - m_full * sub_row(cols[k], j)
            row = sub_row(full, j)
            if j < ROWS - 1:
                forward = forward - jnp.where(subs > j, scaled, 0.0) * sub_row(forward, j)
            full = full - m_full * row
            inverse = jnp.where(subs == j, inv, inverse)
            pivots = jnp.where(subs == j, value, pivots)
        out.append(jnp.where(lanes < base + ROWS, forward * lax.rsqrt(pivots), 0.0))
        full = full * inverse
        if s < count - 1:
            spread = [sub_row(full, k) for k in range(ROWS)]
            for i in range(s + 1, count):
                coeffs = [lane_col(rows[i], base + k) for k in range(ROWS)]
                terms = [coeffs[k] * spread[k] for k in range(ROWS)]
                while len(terms) > 1:
                    terms = [a + b for a, b in zip(terms[::2], terms[1::2])]
                rows[i] = jnp.where(here, 0.0, rows[i]) - terms[0]
    return out


def split(x):
    hi = x.astype(jnp.bfloat16)
    return hi, (x - hi.astype(jnp.float32)).astype(jnp.bfloat16)


def stack_left(x, axis):
    hi, lo = split(x)
    return jnp.concatenate([hi, hi, lo], axis=axis)


def stack_right(x, axis):
    hi, lo = split(x)
    return jnp.concatenate([hi, lo, hi], axis=axis)


def mm(a, b, dims):
    return lax.dot_general(a, b, (dims, ((), ())), preferred_element_type=jnp.float32)


def mm_nn(a, b):
    return mm(stack_left(a, 1), stack_right(b, 0), ((1,), (0,)))


def mm_nt(a, b):
    return mm(stack_left(a, 1), stack_right(b, 1), ((1,), (1,)))


class Chain:
    def __init__(self, n, z_ref, d_ref, w_ref, q_ref):
        self.n, self.z, self.d, self.w, self.q = n, z_ref, d_ref, w_ref, q_ref
        self.blocks = n // LANES

    def block(self, i):
        if isinstance(i, int):
            return pl.ds(i * LANES, LANES)
        return pl.ds(pl.multiple_of(i * LANES, LANES), LANES)

    def start(self, cross_ref, image_ref):
        self.z[: self.n, :] = cross_ref[...]
        self.z[self.n :, :] = image_ref[...]
        self.w[...] = jnp.zeros_like(self.w)

    def step(self, j):
        at, before = self.block(j), self.block(lax.max(j - 1, 0))
        w = self.w[...]
        low = mm_nt(self.z[at, before], w)
        self.d[...] = self.z[at, at] - mm_nt(low, low)
        rows = [self.d[i * ROWS : (i + 1) * ROWS, :] for i in range(LANES // ROWS)]
        out = inverse_factor(rows)
        p = mm_nt(self.z[:, before], w)
        self.q[:, before] = p[self.n :, :]
        u = stack_right(mm_nn(w, self.z[before, :]), 0)
        self.z[...] -= mm(stack_left(p, 1), u, ((1,), (0,)))
        for i, row in enumerate(out):
            self.w[i * ROWS : (i + 1) * ROWS, :] = row

    def finish(self):
        last = self.block(self.blocks - 1)
        self.q[:, last] = mm_nt(self.z[self.n :, last], self.w[...])


from jax.sharding import PartitionSpec as P

STAT_DECAY = 0.95
FIRST_DECAY = 0.9
SECOND_DECAY = 0.95
EPSILON = 1e-08
STEP_SIZE = 0.02
WEIGHT_DECAY = 0.01
HIGH = lax.Precision.HIGH


def chains_kernel(cross_r, image_r, cross_l, image_l, q_r, q_l, z_r, d_r, w_r, z_l, d_l, w_l):
    right = Chain(cross_r.shape[0], z_r, d_r, w_r, q_r)
    left = Chain(cross_l.shape[0], z_l, d_l, w_l, q_l)
    right.start(cross_r, image_r)
    left.start(cross_l, image_l)
    alone = right.blocks - left.blocks

    def first(j, carry):
        right.step(j)
        return carry

    def second(j, carry):
        right.step(j)
        left.step(j - alone)
        return carry

    lax.fori_loop(0, alone, first, 0)
    lax.fori_loop(alone, right.blocks, second, 0)
    right.finish()
    left.finish()


def chains(cross_r, image_r, cross_l, image_l):
    right, left = cross_r.shape[0], cross_l.shape[0]
    scratch = []
    for n in (right, left):
        scratch += [
            pltpu.VMEM((2 * n, n), jnp.float32),
            pltpu.VMEM((LANES, LANES), jnp.float32),
            pltpu.VMEM((LANES, LANES), jnp.float32),
        ]
    return pl.pallas_call(
        chains_kernel,
        out_shape=[
            jax.ShapeDtypeStruct((right, right), jnp.float32),
            jax.ShapeDtypeStruct((left, left), jnp.float32),
        ],
        scratch_shapes=scratch,
        compiler_params=pltpu.CompilerParams(vmem_limit_bytes=56 * 2**20),
    )(cross_r, image_r, cross_l, image_l)


def swap(x, axis, distance):
    count = lax.axis_size(axis)
    return lax.ppermute(x, axis, [(i, i ^ distance) for i in range(count)])


def distances(axis):
    count = lax.axis_size(axis)
    return [1 << b for b in range(count.bit_length() - 1)]


def is_power(axis):
    count = lax.axis_size(axis)
    return count & (count - 1) == 0


def gather_rows(x, axis):
    if not is_power(axis):
        return lax.all_gather(x, axis, axis=0, tiled=True)
    me = lax.axis_index(axis)
    held = {0: x}
    for distance in reversed(distances(axis)):
        held.update({at ^ distance: swap(piece, axis, distance) for at, piece in list(held.items())})
    rows = x.shape[0]
    out = jnp.zeros((rows * lax.axis_size(axis), x.shape[1]), x.dtype)
    for at, piece in held.items():
        out = lax.dynamic_update_slice(out, piece, ((me ^ at) * rows, 0))
    return out


def scatter_sum(x, axis):
    if not is_power(axis):
        return lax.psum_scatter(x, axis, scatter_dimension=0, tiled=True).astype(jnp.float32)
    me = lax.axis_index(axis)
    count = lax.axis_size(axis)
    rows = x.shape[0] // count
    x = x.reshape(count, rows, x.shape[1])
    kind = x.dtype
    for bit, distance in enumerate(distances(axis)):
        own = lax.rem(me >> bit, 2)
        x = x.astype(kind).reshape(x.shape[0] // 2, 2, rows, x.shape[2])
        keep = lax.dynamic_index_in_dim(x, own, 1, keepdims=False)
        other = lax.dynamic_index_in_dim(x, 1 - own, 1, keepdims=False)
        x = keep.astype(jnp.float32) + swap(other, axis, distance).astype(jnp.float32)
    return x[0]


def self_cross(matrix):
    return lax.dot_general(
        matrix, matrix, (((0,), (0,)), ((), ())), precision=HIGH, preferred_element_type=jnp.float32
    )


def rotate_in(matrix, left_half, right_half):
    inner = lax.dot_general(
        left_half, matrix, (((0,), (0,)), ((), ())), preferred_element_type=jnp.float32
    )
    return jnp.dot(inner.astype(jnp.bfloat16), right_half, preferred_element_type=jnp.float32)


def body(grad, weight, moment, second, gram_left, basis_left, gram_right, basis_right):
    count_col = lax.axis_size("col")
    count_row = lax.axis_size("row")
    block_left, block_right = grad.shape
    rows_left, rows_right = gram_left.shape[1], gram_right.shape[1]
    at_left, at_right = lax.axis_index("col") * rows_left, lax.axis_index("row") * rows_right
    part_right = lax.dot_general(
        grad, grad, (((0,), (0,)), ((), ())), preferred_element_type=jnp.float32
    ) / (block_left * count_row)
    part_left = lax.dot_general(
        grad, grad, (((1,), (1,)), ((), ())), preferred_element_type=jnp.float32
    ) / (block_right * count_col)
    basis_r = gather_rows(basis_right[0], "row")
    gram_r = gather_rows(gram_right[0], "row")
    both_l = lax.all_gather(
        jnp.concatenate([gram_left[0], basis_left[0]], axis=1), "col", axis=0, tiled=True
    )
    gram_l, basis_l = both_l[:, :block_left], both_l[:, block_left:]
    sum_l = lax.psum(part_left.astype(jnp.bfloat16), "col").astype(jnp.float32)
    sum_right = scatter_sum(part_right.astype(jnp.bfloat16), "row")
    sum_r = gather_rows(sum_right.astype(jnp.bfloat16), "row").astype(jnp.float32)
    new_gram_r = STAT_DECAY * gram_r + (1.0 - STAT_DECAY) * sum_r
    new_gram_l = STAT_DECAY * gram_l + (1.0 - STAT_DECAY) * sum_l
    new_gram_left = lax.dynamic_slice_in_dim(new_gram_l, at_left, rows_left, 0)
    new_gram_right = STAT_DECAY * gram_right[0] + (1.0 - STAT_DECAY) * sum_right
    image_r = jnp.dot(new_gram_r, basis_r, precision=HIGH, preferred_element_type=jnp.float32)
    image_l = jnp.dot(new_gram_l, basis_l, precision=HIGH, preferred_element_type=jnp.float32)
    right, left = chains(self_cross(image_r), image_r, self_cross(image_l), image_l)
    basis_rows_left = lax.dynamic_slice_in_dim(left, at_left, rows_left, 0)
    basis_rows_right = lax.dynamic_slice_in_dim(right, at_right, rows_right, 0)
    left_half, right_half = left.astype(jnp.bfloat16), right.astype(jnp.bfloat16)
    rotated_grad = rotate_in(grad, left_half, right_half)
    new_moment = FIRST_DECAY * moment + (1.0 - FIRST_DECAY) * grad.astype(jnp.float32)
    new_second = SECOND_DECAY * second + (1.0 - SECOND_DECAY) * rotated_grad * rotated_grad
    rotated_moment = rotate_in(new_moment.astype(jnp.bfloat16), left_half, right_half)
    direction = (rotated_moment / (jnp.sqrt(new_second) + EPSILON)).astype(jnp.bfloat16)
    turned = jnp.dot(left_half, direction, preferred_element_type=jnp.float32).astype(jnp.bfloat16)
    update = lax.dot_general(
        turned, right_half, (((1,), (1,)), ((), ())), preferred_element_type=jnp.float32
    )
    new_weight = weight - STEP_SIZE * (update + WEIGHT_DECAY * weight)
    return (
        new_weight,
        new_moment,
        new_second,
        new_gram_left[None],
        basis_rows_left[None],
        new_gram_right[None],
        basis_rows_right[None],
    )


def solution(mesh):
    in_specs = (
        P("row", "col"),
        P("row", "col"),
        P("row", "col"),
        P("row", "col"),
        P("row", "col", None),
        P("row", "col", None),
        P("col", "row", None),
        P("col", "row", None),
    )
    out_specs = (
        P("row", "col"),
        P("row", "col"),
        P("row", "col"),
        P("row", "col", None),
        P("row", "col", None),
        P("col", "row", None),
        P("col", "row", None),
    )
    return jax.shard_map(body, mesh=mesh, in_specs=in_specs, out_specs=out_specs, check_vma=False)
```

```python
import functools
import jax
import jax.numpy as jnp
from jax import lax
from jax.experimental import pallas as pl
from jax.experimental.pallas import tpu as pltpu

LANES = 128
ROWS = 8


def lane_mask(step):
    lanes = lax.broadcasted_iota(jnp.int32, (ROWS, LANES), 1)
    return (lanes >= step * ROWS) & (lanes < (step + 1) * ROWS)


def sub_row(x, k):
    return jnp.broadcast_to(x[k : k + 1, :], (ROWS, LANES))


def lane_col(x, c):
    return jnp.broadcast_to(x[:, c : c + 1], (ROWS, LANES))


def reciprocal(p):
    guess = pl.reciprocal(p, approx=True)
    return guess * (2.0 - p * guess)


def inverse_factor(rows):
    count = LANES // ROWS
    rows = list(rows)
    subs = lax.broadcasted_iota(jnp.int32, (ROWS, LANES), 0)
    lanes = lax.broadcasted_iota(jnp.int32, (ROWS, LANES), 1)
    out = []
    for s in range(count):
        base = s * ROWS
        pivot = rows[s]
        here = (lanes >= base) & (lanes < base + ROWS)
        cols = [lane_col(pivot, base + k) for k in range(ROWS)]
        full = jnp.where(here, (lanes == subs + base).astype(jnp.float32), pivot)
        forward = full
        inverse = jnp.zeros((ROWS, LANES), jnp.float32)
        pivots = jnp.ones((ROWS, LANES), jnp.float32)
        for j in range(ROWS):
            value = sub_row(cols[j], j)
            inv = reciprocal(value)
            scaled = cols[j] * inv
            m_full = jnp.where(subs == j, 0.0, scaled)
            for k in range(j + 1, ROWS):
                cols[k] = cols[k] - m_full * sub_row(cols[k], j)
            row = sub_row(full, j)
            if j < ROWS - 1:
                forward = forward - jnp.where(subs > j, scaled, 0.0) * sub_row(forward, j)
            full = full - m_full * row
            inverse = jnp.where(subs == j, inv, inverse)
            pivots = jnp.where(subs == j, value, pivots)
        out.append(jnp.where(lanes < base + ROWS, forward * lax.rsqrt(pivots), 0.0))
        full = full * inverse
        if s < count - 1:
            spread = [sub_row(full, k) for k in range(ROWS)]
            for i in range(s + 1, count):
                coeffs = [lane_col(rows[i], base + k) for k in range(ROWS)]
                terms = [coeffs[k] * spread[k] for k in range(ROWS)]
                while len(terms) > 1:
                    terms = [a + b for a, b in zip(terms[::2], terms[1::2])]
                rows[i] = jnp.where(here, 0.0, rows[i]) - terms[0]
    return out


def split(x):
    hi = x.astype(jnp.bfloat16)
    return hi, (x - hi.astype(jnp.float32)).astype(jnp.bfloat16)


def stack_left(x, axis):
    hi, lo = split(x)
    return jnp.concatenate([hi, hi, lo], axis=axis)


def stack_right(x, axis):
    hi, lo = split(x)
    return jnp.concatenate([hi, lo, hi], axis=axis)


def mm(a, b, dims):
    return lax.dot_general(a, b, (dims, ((), ())), preferred_element_type=jnp.float32)


def mm_nn(a, b):
    return mm(stack_left(a, 1), stack_right(b, 0), ((1,), (0,)))


def mm_nt(a, b):
    return mm(stack_left(a, 1), stack_right(b, 1), ((1,), (1,)))


def product(ah, al, bh, bl, dims):
    return mm(ah, bh, dims) + (mm(ah, bl, dims) + mm(al, bh, dims))


def block(i):
    return pl.ds(i * LANES, LANES) if isinstance(i, int) else pl.ds(pl.multiple_of(i * LANES, LANES), LANES)


class Chain:
    def __init__(self, z_ref, d_ref, w_ref, q_ref):
        self.z, self.d, self.w, self.q = z_ref, d_ref, w_ref, q_ref
        self.width = z_ref.shape[1]
        self.blocks = self.width // LANES

    def cross(self):
        hi, lo = split(self.z[self.width :, :])
        dims = ((0,), (0,))
        self.z[: self.width, :] = product(hi, lo, hi, lo, dims)
        self.w[...] = jnp.zeros_like(self.w)

    def step(self, j):
        at, before = block(j), block(lax.max(j - 1, 0))
        w = self.w[...]
        low = mm_nt(self.z[at, before], w)
        self.d[...] = self.z[at, at] - mm_nt(low, low)
        rows = [self.d[i * ROWS : (i + 1) * ROWS, :] for i in range(LANES // ROWS)]
        out = inverse_factor(rows)
        p = mm_nt(self.z[:, before], w)
        self.q[:, before] = p[self.width :, :]
        u = stack_right(mm_nn(w, self.z[before, :]), 0)
        self.z[...] -= mm(stack_left(p, 1), u, ((1,), (0,)))
        for i, row in enumerate(out):
            self.w[i * ROWS : (i + 1) * ROWS, :] = row

    def finish(self):
        last = block(self.blocks - 1)
        self.q[:, last] = mm_nt(self.z[self.width :, last], self.w[...])


from jax.sharding import PartitionSpec as P

STAT_DECAY = 0.95
FIRST_DECAY = 0.9
SECOND_DECAY = 0.95
EPSILON = 1e-08
STEP_SIZE = 0.02
WEIGHT_DECAY = 0.01
HEAD_LIMIT = 34 * 2**20
VMEM_LIMIT = 44 * 2**20


def offsets(size):
    return size // LANES // 2 + 1


def pack_products(cols, out_ref, dims, scale):
    blocks = len(cols)
    for i in range(blocks):
        for o in range(offsets(blocks * LANES)):
            term = mm(cols[i], cols[(i + o) % blocks], dims)
            out_ref[block(i), block(o)] = (term * scale).astype(out_ref.dtype)


def terms_kernel(scale_left, scale_right, grad_ref, right_ref, left_ref):
    rows, columns = grad_ref.shape
    pack_products([grad_ref[:, block(i)] for i in range(columns // LANES)], right_ref, ((0,), (0,)), scale_right)
    pack_products([grad_ref[block(i), :] for i in range(rows // LANES)], left_ref, ((1,), (1,)), scale_left)


def terms(grad, scale_left, scale_right):
    rows, columns = grad.shape
    return pl.pallas_call(
        functools.partial(terms_kernel, scale_left, scale_right),
        out_shape=[
            jax.ShapeDtypeStruct((columns, offsets(columns) * LANES), jnp.bfloat16),
            jax.ShapeDtypeStruct((rows, offsets(rows) * LANES), jnp.bfloat16),
        ],
        compiler_params=pltpu.CompilerParams(vmem_limit_bytes=VMEM_LIMIT),
    )(grad)


def place(ref, me, pieces, scale):
    for distance, piece, first in pieces:
        rows = piece.shape[0]
        at = pl.ds(pl.multiple_of((me ^ distance) * rows, ROWS), rows)
        value = piece[:, first : first + ref.shape[1]].astype(jnp.float32)
        ref[at, :] = value * scale if scale != 1.0 else value


def add_packed(gram_ref, packed_ref):
    blocks = gram_ref.shape[0] // LANES
    count = offsets(gram_ref.shape[0])
    for i in range(blocks):
        for o in range(count):
            k = (i + o) % blocks
            term = packed_ref[block(i), block(o)]
            gram_ref[block(i), block(k)] += term
            if o > 0 and not (blocks % 2 == 0 and o == count - 1):
                gram_ref[block(k), block(i)] += term.T


def image(z_ref, gh_ref, gl_ref, basis_ref):
    width = z_ref.shape[1]
    bh, bl = split(basis_ref[...])
    for i in range(gh_ref.shape[0] // LANES):
        z_ref[pl.ds(width + i * LANES, LANES), :] = product(
            gh_ref[block(i), :], gl_ref[block(i), :], bh, bl, ((1,), (0,))
        )


def split_rows(ref, hi_ref, lo_ref):
    for i in range(ref.shape[0] // LANES):
        hi_ref[block(i), :], lo_ref[block(i), :] = split(ref[block(i), :])


def own_rows(ref, me, rows):
    return ref[pl.ds(pl.multiple_of(me * rows, ROWS), rows), :]


def half_window(size):
    return -(-size // 2 // LANES) * LANES


def fill_halves(gram, me, count, own_in, other_in):
    size = gram.shape[0]
    place(gram, me, own_in, STAT_DECAY)
    if not other_in:
        return
    half = lax.div(2 * me, count)
    window = half_window(size)
    rest = size - window
    for distance, piece, _ in other_in:
        rows = piece.shape[0]
        at = pl.ds(pl.multiple_of((me ^ distance) * rows, ROWS), rows)
        gram[at, pl.ds(pl.multiple_of((1 - half) * rest, LANES), window)] = piece[:, :window] * STAT_DECAY
    near = pl.multiple_of(half * window, LANES)
    far = pl.multiple_of((1 - half) * rest, LANES)
    for i in range(rest // LANES):
        at = pl.ds(pl.multiple_of(near + i * LANES, LANES), LANES)
        gram[pl.ds(far, window), at] = gram[at, pl.ds(far, window)].T


def head_kernel(count, owns, others, sums, *refs):
    me_ref, refs = refs[0], list(refs[1:])
    gram_in = [(d, refs.pop(0), 0) for d in owns]
    basis_in = [(d, refs.pop(0), 0) for d in owns]
    other_in = [(d, refs.pop(0), half_window(refs[-6].shape[0])) for d in others]
    sum_in = [(d, refs.pop(0), 0) for d in sums]
    rows_ref, gh_ref, gl_ref, q_ref, gram, packed, basis, z, d, w = refs
    me = me_ref[0]
    fill_halves(gram, me, count, gram_in, other_in)
    place(packed, lax.rem(me, 2) if len(sums) > 1 else 0, sum_in, 1.0 - STAT_DECAY)
    place(basis, me, basis_in + other_in, 1.0)
    add_packed(gram, packed)
    rows_ref[...] = own_rows(gram, me, rows_ref.shape[0])
    split_rows(gram, gh_ref, gl_ref)
    image(z, gh_ref, gl_ref, basis)
    chain = Chain(z, d, w, q_ref)
    chain.cross()

    def step(j, carry):
        chain.step(j)
        return carry

    lax.fori_loop(0, chain.blocks, step, 0)
    chain.finish()


def in_specs(count):
    return [pl.BlockSpec(memory_space=pltpu.SMEM)] + [pl.BlockSpec(memory_space=pltpu.VMEM)] * count


def chain_scratch(width, rows):
    return [
        pltpu.VMEM((width + rows, width), jnp.float32),
        pltpu.VMEM((LANES, LANES), jnp.float32),
        pltpu.VMEM((LANES, LANES), jnp.float32),
    ]


def head(me, count, grams, bases, others, sums, width):
    args = [p for group in (grams, bases, others, sums) for _, p in group]
    rows, size = grams[0][1].shape
    return pl.pallas_call(
        functools.partial(head_kernel, count, *[[d for d, _ in group] for group in (grams, others, sums)]),
        out_shape=[
            jax.ShapeDtypeStruct((rows, size), jnp.float32),
            jax.ShapeDtypeStruct((size, size), jnp.bfloat16),
            jax.ShapeDtypeStruct((size, size), jnp.bfloat16),
            jax.ShapeDtypeStruct((size, width), jnp.float32),
        ],
        in_specs=in_specs(len(args)),
        scratch_shapes=[
            pltpu.VMEM((size, size), jnp.float32),
            pltpu.VMEM((size, offsets(size) * LANES), jnp.float32),
            pltpu.VMEM((size, width), jnp.float32),
            *chain_scratch(width, size),
        ],
        compiler_params=pltpu.CompilerParams(vmem_limit_bytes=HEAD_LIMIT),
    )(me, *args)


def rest_kernel(bases, others, sums, *refs):
    me_ref, refs = refs[0], list(refs[1:])
    gh, gl, q_first = refs[:3]
    refs = refs[3:]
    basis_in = [(d, refs.pop(0), q_first.shape[1]) for d in bases]
    basis_in += [(d, refs.pop(0), 0) for d in others]
    left = refs.pop(0)
    sum_in = [(d, refs.pop(0), 0) for d in sums]
    right_half, right_rows, left_half, left_rows, gram_rows = refs[:5]
    basis, qr, ql, gram_l, packed_l, basis_l, glh, gll, zr, dr, wr, zl, dl, wl = refs[5:]
    row, col = me_ref[0], me_ref[1]
    size = gram_l.shape[0]
    first = q_first.shape[1]
    place(basis, row, basis_in, 1.0)
    gram_l[...] = left[:, :size] * STAT_DECAY
    basis_l[...] = left[:, size:]
    place(packed_l, lax.rem(col, 2) if len(sums) > 1 else 0, sum_in, 1.0 - STAT_DECAY)
    add_packed(gram_l, packed_l)
    gram_rows[...] = own_rows(gram_l, col, gram_rows.shape[0])
    image(zr, gh, gl, basis)
    width = zr.shape[1]
    qh, qo = split(q_first[...])
    xh, xl = split(zr[width:, :])
    sh, sl = split(product(qh, qo, xh, xl, ((0,), (0,))))
    zr[width:, :] -= product(qh, qo, sh, sl, ((1,), (0,)))
    split_rows(gram_l, glh, gll)
    image(zl, glh, gll, basis_l)
    right, left = Chain(zr, dr, wr, qr), Chain(zl, dl, wl, ql)
    right.cross()
    left.cross()

    def step(j, carry):
        right.step(j)
        left.step(j)
        return carry

    def short(j, carry):
        right.step(j)
        return carry

    lax.fori_loop(0, left.blocks, step, 0)
    lax.fori_loop(left.blocks, right.blocks, short, 0)
    right.finish()
    left.finish()
    right_half[:, :first] = q_first[...].astype(jnp.bfloat16)
    right_half[:, first:] = qr[...].astype(jnp.bfloat16)
    right_rows[:, :first] = own_rows(q_first, row, right_rows.shape[0])
    right_rows[:, first:] = own_rows(qr, row, right_rows.shape[0])
    left_half[...] = ql[...].astype(jnp.bfloat16)
    left_rows[...] = own_rows(ql, col, left_rows.shape[0])


def rest(me, gh, gl, q_first, bases, others, left, sums, rows_l):
    args = [gh, gl, q_first] + [p for _, p in bases + others] + [left] + [p for _, p in sums]
    rows_r, size_r = bases[0][1].shape
    width = size_r - q_first.shape[1]
    size_l = left.shape[0]
    f32, bf16 = jnp.float32, jnp.bfloat16
    return pl.pallas_call(
        functools.partial(rest_kernel, *[[d for d, _ in group] for group in (bases, others, sums)]),
        out_shape=[
            jax.ShapeDtypeStruct((size_r, size_r), bf16),
            jax.ShapeDtypeStruct((rows_r, size_r), f32),
            jax.ShapeDtypeStruct((size_l, size_l), bf16),
            jax.ShapeDtypeStruct((rows_l, size_l), f32),
            jax.ShapeDtypeStruct((rows_l, size_l), f32),
        ],
        in_specs=in_specs(len(args)),
        scratch_shapes=[
            pltpu.VMEM((size_r, width), f32),
            pltpu.VMEM((size_r, width), f32),
            pltpu.VMEM((size_l, size_l), f32),
            pltpu.VMEM((size_l, size_l), f32),
            pltpu.VMEM((size_l, offsets(size_l) * LANES), f32),
            pltpu.VMEM((size_l, size_l), f32),
            pltpu.VMEM((size_l, size_l), bf16),
            pltpu.VMEM((size_l, size_l), bf16),
            *chain_scratch(width, size_r),
            *chain_scratch(size_l, size_l),
        ],
        compiler_params=pltpu.CompilerParams(vmem_limit_bytes=VMEM_LIMIT),
    )(me, *args)


def swap(x, axis, distance):
    count = lax.axis_size(axis)
    return lax.ppermute(x, axis, [(i, i ^ distance) for i in range(count)])


def distances(axis):
    count = lax.axis_size(axis)
    return [1 << b for b in range(count.bit_length() - 1)]


def spread(held, axis, steps):
    for distance in steps:
        held = held + [(at ^ distance, swap(piece, axis, distance)) for at, piece in held]
    return held


def sum_pairs(x, axis):
    me, kind = lax.axis_index(axis), x.dtype
    if lax.axis_size(axis) == 1:
        return x, [(0, x)]
    rows = x.shape[0] // 2
    own = lax.rem(me, 2)
    keep = lax.dynamic_slice_in_dim(x, own * rows, rows, 0)
    other = lax.dynamic_slice_in_dim(x, (1 - own) * rows, rows, 0)
    total = keep.astype(jnp.float32) + swap(other, axis, 1).astype(jnp.float32)
    for distance in distances(axis)[1:]:
        total = total.astype(kind)
        total = total.astype(jnp.float32) + swap(total, axis, distance).astype(jnp.float32)
    total = total.astype(kind)
    return total, [(0, total), (1, swap(total, axis, 1))]


def gather_right(gram, basis, width):
    count = lax.axis_size("row")
    grams, bases = [(0, gram)], [(0, basis)]
    if count == 1:
        return grams, bases, []
    window = half_window(gram.shape[1])
    half = lax.div(2 * lax.axis_index("row"), count)
    mine = lax.dynamic_slice_in_dim(gram, half * (gram.shape[1] - window), window, 1)
    mine = jnp.concatenate([mine, basis[:, :width]], axis=1)
    others = [(count // 2, swap(mine, "row", count // 2))]
    near = distances("row")[-2::-1]
    return spread(grams, "row", near), spread(bases, "row", near), spread(others, "row", near)


def rotate_in(matrix, left_half, right_half):
    inner = lax.dot_general(
        left_half, matrix, (((0,), (0,)), ((), ())), preferred_element_type=jnp.float32
    )
    return jnp.dot(inner.astype(jnp.bfloat16), right_half, preferred_element_type=jnp.float32)


def body(grad, weight, moment, second, gram_left, basis_left, gram_right, basis_right):
    block_left, block_right = grad.shape
    first = max(block_right - block_left, LANES)
    count = lax.axis_size("row")
    me = jnp.stack([lax.axis_index("row"), lax.axis_index("col")])
    lefts = lax.all_gather(
        jnp.concatenate([gram_left[0], basis_left[0]], axis=1), "col", axis=0, tiled=True
    )
    grams, bases, others = gather_right(gram_right[0], basis_right[0], first)
    terms_right, terms_left = terms(
        grad, 1.0 / (block_right * lax.axis_size("col")), 1.0 / (block_left * count)
    )
    sent, sums_right = sum_pairs(terms_right, "row")
    _, sums_left = sum_pairs(terms_left, "col")
    last, _ = lax.optimization_barrier((basis_right[0][:, first:], sent))
    last = [(d, swap(last, "row", d)) for d in range(count // 2, count)] if count > 1 else []
    new_gram_right, gh, gl, q_first = head(me, count, grams, bases, others, sums_right, first)
    right_half, basis_rows_right, left_half, basis_rows_left, new_gram_left = rest(
        me, gh, gl, q_first, bases, last, lefts, sums_left, gram_left.shape[1]
    )
    rotated_grad = rotate_in(grad, left_half, right_half)
    new_moment = FIRST_DECAY * moment + (1.0 - FIRST_DECAY) * grad.astype(jnp.float32)
    new_second = SECOND_DECAY * second + (1.0 - SECOND_DECAY) * rotated_grad * rotated_grad
    rotated_moment = rotate_in(new_moment.astype(jnp.bfloat16), left_half, right_half)
    direction = (rotated_moment / (jnp.sqrt(new_second) + EPSILON)).astype(jnp.bfloat16)
    turned = jnp.dot(left_half, direction, preferred_element_type=jnp.float32).astype(jnp.bfloat16)
    update = lax.dot_general(
        turned, right_half, (((1,), (1,)), ((), ())), preferred_element_type=jnp.float32
    )
    new_weight = weight - STEP_SIZE * (update + WEIGHT_DECAY * weight)
    return (
        new_weight,
        new_moment,
        new_second,
        new_gram_left[None],
        basis_rows_left[None],
        new_gram_right[None],
        basis_rows_right[None],
    )


def solution(mesh):
    specs = (
        P("row", "col"),
        P("row", "col"),
        P("row", "col"),
        P("row", "col"),
        P("row", "col", None),
        P("row", "col", None),
        P("col", "row", None),
        P("col", "row", None),
    )
    out_specs = specs[:3] + specs[4:]
    return jax.shard_map(body, mesh=mesh, in_specs=specs, out_specs=out_specs, check_vma=False)
```

```python
import functools
import jax
import jax.numpy as jnp
from jax import lax
from jax.experimental import pallas as pl
from jax.experimental.pallas import tpu as pltpu
from jax.sharding import PartitionSpec as P

STAT_DECAY = 0.95
FIRST_DECAY = 0.9
SECOND_DECAY = 0.95
EPSILON = 1e-08
STEP_SIZE = 0.02
WEIGHT_DECAY = 0.01
LANES = 128
ROWS = 8
VMEM_LIMIT = 56 * 2**20


def sub_row(x, k):
    return jnp.broadcast_to(x[k : k + 1, :], (ROWS, LANES))


def lane_col(x, c):
    return jnp.broadcast_to(x[:, c : c + 1], (ROWS, LANES))


def reciprocal(p):
    guess = pl.reciprocal(p, approx=True)
    return guess * (2.0 - p * guess)


def inverse_factor(rows):
    count = LANES // ROWS
    rows = list(rows)
    subs = lax.broadcasted_iota(jnp.int32, (ROWS, LANES), 0)
    lanes = lax.broadcasted_iota(jnp.int32, (ROWS, LANES), 1)
    out = []
    for s in range(count):
        base = s * ROWS
        pivot = rows[s]
        here = (lanes >= base) & (lanes < base + ROWS)
        cols = [lane_col(pivot, base + k) for k in range(ROWS)]
        full = jnp.where(here, (lanes == subs + base).astype(jnp.float32), pivot)
        forward = full
        inverse = jnp.zeros((ROWS, LANES), jnp.float32)
        pivots = jnp.ones((ROWS, LANES), jnp.float32)
        yield
        for j in range(ROWS):
            value = sub_row(cols[j], j)
            inv = reciprocal(value)
            scaled = cols[j] * inv
            m_full = jnp.where(subs == j, 0.0, scaled)
            for k in range(j + 1, ROWS):
                cols[k] = cols[k] - m_full * sub_row(cols[k], j)
            row = sub_row(full, j)
            if j < ROWS - 1:
                forward = forward - jnp.where(subs > j, scaled, 0.0) * sub_row(forward, j)
            full = full - m_full * row
            inverse = jnp.where(subs == j, inv, inverse)
            pivots = jnp.where(subs == j, value, pivots)
            yield
        out.append(jnp.where(lanes < base + ROWS, forward * lax.rsqrt(pivots), 0.0))
        full = full * inverse
        if s < count - 1:
            spread = [sub_row(full, k) for k in range(ROWS)]
            for i in range(s + 1, count):
                coeffs = [lane_col(rows[i], base + k) for k in range(ROWS)]
                terms = [coeffs[k] * spread[k] for k in range(ROWS)]
                while len(terms) > 1:
                    terms = [a + b for a, b in zip(terms[::2], terms[1::2])]
                rows[i] = jnp.where(here, 0.0, rows[i]) - terms[0]
                yield
    return out


def in_turns(generators, fills):
    results = [None] * len(generators)
    live = list(enumerate(generators))
    fills = list(fills)
    total, turn, done = 250, 0, 0
    while live:
        for at, generator in list(live):
            try:
                next(generator)
            except StopIteration as stop:
                results[at] = stop.value
                live.remove((at, generator))
        turn += 1
        while done < len(fills) and done * total <= turn * len(fills):
            fills[done]()
            done += 1
    for fill in fills[done:]:
        fill()
    return results


def split(x):
    hi = x.astype(jnp.bfloat16)
    return hi, (x - hi.astype(jnp.float32)).astype(jnp.bfloat16)


def stack_left(x, axis):
    hi, lo = split(x)
    return jnp.concatenate([hi, hi, lo], axis=axis)


def stack_right(x, axis):
    hi, lo = split(x)
    return jnp.concatenate([hi, lo, hi], axis=axis)


def mm(a, b, dims):
    return lax.dot_general(a, b, (dims, ((), ())), preferred_element_type=jnp.float32)


def mm_nn(a, b):
    return mm(stack_left(a, 1), stack_right(b, 0), ((1,), (0,)))


def mm_nt(a, b):
    return mm(stack_left(a, 1), stack_right(b, 1), ((1,), (1,)))


def product(ah, al, bh, bl, dims):
    return mm(ah, bh, dims) + (mm(ah, bl, dims) + mm(al, bh, dims))


def block(i):
    return pl.ds(i * LANES, LANES) if isinstance(i, int) else pl.ds(pl.multiple_of(i * LANES, LANES), LANES)


class Chain:
    def __init__(self, z_ref, w_ref, q_ref):
        self.z, self.w, self.q = z_ref, w_ref, q_ref
        self.width = z_ref.shape[1]
        self.blocks = self.width // LANES

    def cross(self):
        hi, lo = split(self.z[self.width :, :])
        dims = ((0,), (0,))
        self.z[: self.width, :] = product(hi, lo, hi, lo, dims)
        self.w[...] = jnp.zeros_like(self.w)

    def look(self, j):
        self.before = block(lax.max(j - 1, 0))
        self.w_nt = stack_right(self.w[...], 1)
        at = block(j)
        low = mm(stack_left(self.z[at, self.before], 1), self.w_nt, ((1,), (1,)))
        diagonal = self.z[at, at] - mm_nt(low, low)
        return [diagonal[i * ROWS : (i + 1) * ROWS, :] for i in range(LANES // ROWS)]

    def fills(self):
        def rows_of_u():
            self.u = stack_right(mm_nn(self.w[...], self.z[self.before, :]), 0)

        def rows(i):
            at = block(i)
            p = mm(stack_left(self.z[at, self.before], 1), self.w_nt, ((1,), (1,)))
            if i >= self.blocks:
                self.q[block(i - self.blocks), self.before] = p
            self.z[at, :] -= mm(stack_left(p, 1), self.u, ((1,), (0,)))

        return [rows_of_u] + [functools.partial(rows, i) for i in range(self.z.shape[0] // LANES)]

    def store(self, out):
        for i, row in enumerate(out):
            self.w[i * ROWS : (i + 1) * ROWS, :] = row

    def finish(self):
        last = block(self.blocks - 1)
        self.q[:, last] = mm_nt(self.z[self.width :, last], self.w[...])


def run_chains(chains):
    def step_of(members):
        def step(j, carry):
            rows = [chain.look(j) for chain in members]
            fills = [fill for chain in members for fill in chain.fills()]
            for chain, out in zip(members, in_turns([inverse_factor(r) for r in rows], fills)):
                chain.store(out)
            return carry

        return step

    start = 0
    for end in sorted({chain.blocks for chain in chains}):
        lax.fori_loop(start, end, step_of([chain for chain in chains if chain.blocks >= end]), 0)
        start = end
    for chain in chains:
        chain.finish()


class Copies:
    def __init__(self, semaphores):
        self.semaphores, self.used = semaphores, 0

    def start(self, source, target):
        copy = pltpu.make_async_copy(source, target, self.semaphores.at[self.used])
        self.used += 1
        copy.start()
        return copy


def wait(copies):
    for copy in copies:
        copy.wait()


def offsets(size):
    return size // LANES // 2 + 1


def pack_products(cols, out_ref, dims, scale):
    blocks = len(cols)
    for i in range(blocks):
        for o in range(offsets(blocks * LANES)):
            term = mm(cols[i], cols[(i + o) % blocks], dims)
            out_ref[block(i), block(o)] = (term * scale).astype(out_ref.dtype)


def terms_kernel(scale_left, scale_right, grad_ref, right_ref, left_ref):
    rows, columns = grad_ref.shape
    pack_products([grad_ref[:, block(i)] for i in range(columns // LANES)], right_ref, ((0,), (0,)), scale_right)
    pack_products([grad_ref[block(i), :] for i in range(rows // LANES)], left_ref, ((1,), (1,)), scale_left)


def terms(grad, scale_left, scale_right):
    rows, columns = grad.shape
    return pl.pallas_call(
        functools.partial(terms_kernel, scale_left, scale_right),
        out_shape=[
            jax.ShapeDtypeStruct((columns, offsets(columns) * LANES), jnp.bfloat16),
            jax.ShapeDtypeStruct((rows, offsets(rows) * LANES), jnp.bfloat16),
        ],
        compiler_params=pltpu.CompilerParams(vmem_limit_bytes=VMEM_LIMIT),
    )(grad)


def rows_at(me, distance, rows):
    return pl.ds(pl.multiple_of((me ^ distance) * rows, ROWS), rows)


def new_gram(gram_ref, packed_ref, gh_ref, gl_ref):
    blocks = gram_ref.shape[0] // LANES
    count = offsets(gram_ref.shape[0])

    def put(i, k, term):
        value = gram_ref[block(i), block(k)] * STAT_DECAY + term
        gram_ref[block(i), block(k)] = value
        gh_ref[block(i), block(k)], gl_ref[block(i), block(k)] = split(value)

    for i in range(blocks):
        for o in range(count):
            k = (i + o) % blocks
            term = packed_ref[block(i), block(o)].astype(jnp.float32) * (1.0 - STAT_DECAY)
            put(i, k, term)
            if o > 0 and not (blocks % 2 == 0 and o == count - 1):
                put(k, i, term.T)


def image(z_ref, gh_ref, gl_ref, basis_ref):
    width = z_ref.shape[1]
    bh, bl = split(basis_ref[...])
    for i in range(gh_ref.shape[0] // LANES):
        z_ref[pl.ds(width + i * LANES, LANES), :] = product(
            gh_ref[block(i), :], gl_ref[block(i), :], bh, bl, ((1,), (0,))
        )


def own_rows(ref, me, rows):
    return ref[pl.ds(pl.multiple_of(me * rows, ROWS), rows), :]


def half_window(size):
    return -(-size // 2 // LANES) * LANES


def fill_halves(gram, half):
    size = gram.shape[0]
    window = half_window(size)
    rest = size - window
    near = half * window
    far = pl.ds(pl.multiple_of((1 - half) * rest, LANES), window)
    for i in range(rest // LANES):
        at = pl.ds(pl.multiple_of(near + i * LANES, LANES), LANES)
        gram[far, at] = gram[at, far].T


def packed_copies(copies, me, sums, packed):
    side = lax.rem(me, 2) if len(sums) > 1 else 0
    return [copies.start(piece, packed.at[rows_at(side, d, piece.shape[0]), :]) for d, piece in sums]


def take(refs, distances_of):
    return [(d, refs.pop(0)) for d in distances_of]


def head_kernel(count, owns, others, sums, *refs):
    me_ref, refs = refs[0], list(refs[1:])
    gram_in, basis_in, other_in, sum_in = take(refs, owns), take(refs, owns), take(refs, others), take(refs, sums)
    rows_ref, gh_ref, gl_ref, q_ref, gram, packed, basis, gh, gl, rows_own, z, w, semaphores = refs
    me = me_ref[0]
    copies = Copies(semaphores)
    width = basis.shape[1]
    half = lax.div(2 * me, count)
    window = half_window(gram.shape[0])
    others_at = pl.ds(pl.multiple_of((1 - half) * (gram.shape[0] - window), LANES), window)
    first, second = [], []
    for d, piece in gram_in:
        first.append(copies.start(piece, gram.at[rows_at(me, d, piece.shape[0]), :]))
    for d, piece in other_in:
        at = rows_at(me, d, piece.shape[0])
        first.append(copies.start(piece.at[:, pl.ds(0, window)], gram.at[at, others_at]))
    first += packed_copies(copies, me, sum_in, packed)
    for d, piece in basis_in:
        at = rows_at(me, d, piece.shape[0])
        second.append(copies.start(piece.at[:, pl.ds(0, width)], basis.at[at, :]))
    for d, piece in other_in:
        at = rows_at(me, d, piece.shape[0])
        second.append(copies.start(piece.at[:, pl.ds(window, width)], basis.at[at, :]))
    wait(first)
    if other_in:
        fill_halves(gram, half)
    new_gram(gram, packed, gh, gl)
    rows_own[...] = own_rows(gram, me, rows_own.shape[0])
    out = [copies.start(gh, gh_ref), copies.start(gl, gl_ref), copies.start(rows_own, rows_ref)]
    wait(second)
    image(z, gh, gl, basis)
    chain = Chain(z, w, q_ref)
    chain.cross()
    run_chains([chain])
    wait(out)


def any_specs(count):
    return [pl.BlockSpec(memory_space=pltpu.SMEM)] + [pl.BlockSpec(memory_space=pl.ANY)] * count


def chain_scratch(width, rows):
    return [pltpu.VMEM((width + rows, width), jnp.float32), pltpu.VMEM((LANES, LANES), jnp.float32)]


def head(me, count, grams, bases, others, sums, width):
    args = [p for group in (grams, bases, others, sums) for _, p in group]
    rows, size = grams[0][1].shape
    f32, bf16 = jnp.float32, jnp.bfloat16
    return pl.pallas_call(
        functools.partial(head_kernel, count, *[[d for d, _ in group] for group in (grams, others, sums)]),
        out_shape=[
            jax.ShapeDtypeStruct((rows, size), f32),
            jax.ShapeDtypeStruct((size, size), bf16),
            jax.ShapeDtypeStruct((size, size), bf16),
            jax.ShapeDtypeStruct((size, width), f32),
        ],
        in_specs=any_specs(len(args)),
        out_specs=[pl.BlockSpec(memory_space=pl.ANY)] * 3 + [pl.BlockSpec(memory_space=pltpu.VMEM)],
        scratch_shapes=[
            pltpu.VMEM((size, size), f32),
            pltpu.VMEM((size, offsets(size) * LANES), bf16),
            pltpu.VMEM((size, width), f32),
            pltpu.VMEM((size, size), bf16),
            pltpu.VMEM((size, size), bf16),
            pltpu.VMEM((rows, size), f32),
            *chain_scratch(width, size),
            pltpu.SemaphoreType.DMA((len(args) + len(others) + 3,)),
        ],
        compiler_params=pltpu.CompilerParams(vmem_limit_bytes=VMEM_LIMIT),
    )(me, *args)


def rest_kernel(bases, others, sums, *refs):
    me_ref, refs = refs[0], list(refs[1:])
    gh_in, gl_in, q_in, grad_in, weight_in, moment_in, second_in, gram_in, left_in = refs[:9]
    refs = refs[9:]
    basis_in, other_in, sum_in = take(refs, bases), take(refs, others), take(refs, sums)
    weight_out, moment_out, second_out, right_rows, left_rows, gram_rows = refs[:6]
    (gh, gl, q_first, basis, qr, ql, gram_l, packed_l, basis_l, glh, gll, zr, wr, zl, wl) = refs[6:21]
    (grad, weight, moment, second, inner, turn, right_half, left_half, semaphores) = refs[21:]
    row, col = me_ref[0], me_ref[1]
    copies = Copies(semaphores)
    first = q_first.shape[1]
    width = zr.shape[1]
    start = [copies.start(gh_in, gh), copies.start(gl_in, gl)]
    for d, piece in basis_in:
        at = rows_at(row, d, piece.shape[0])
        start.append(copies.start(piece.at[:, pl.ds(first, width)], basis.at[at, :]))
    for d, piece in other_in:
        start.append(copies.start(piece, basis.at[rows_at(row, d, piece.shape[0]), :]))
    project = [copies.start(q_in, q_first)]
    lefts = packed_copies(copies, col, sum_in, packed_l)
    lefts += [copies.start(gram_in, gram_l), copies.start(left_in, basis_l)]
    tail = [copies.start(grad_in, grad), copies.start(moment_in, moment)]
    late = [copies.start(second_in, second), copies.start(weight_in, weight)]

    wait(start)
    image(zr, gh, gl, basis)
    wait(project)
    qh, qo = split(q_first[...])
    xh, xl = split(zr[width:, :])
    sh, sl = split(product(qh, qo, xh, xl, ((0,), (0,))))
    zr[width:, :] -= product(qh, qo, sh, sl, ((1,), (0,)))
    wait(lefts)
    new_gram(gram_l, packed_l, glh, gll)
    gram_rows[...] = own_rows(gram_l, col, gram_rows.shape[0])
    image(zl, glh, gll, basis_l)
    right, left = Chain(zr, wr, qr), Chain(zl, wl, ql)
    right.cross()
    left.cross()
    right_half[:, :first] = q_first[...].astype(jnp.bfloat16)
    wait(tail)
    for i in range(grad.shape[0] // LANES):
        moment[block(i), :] = FIRST_DECAY * moment[block(i), :] + (1.0 - FIRST_DECAY) * grad[block(i), :].astype(
            jnp.float32
        )
    out = [copies.start(moment, moment_out)]
    run_chains([left, right] if left.blocks <= right.blocks else [right, left])
    left_half[...] = ql[...].astype(jnp.bfloat16)
    right_half[:, first:] = qr[...].astype(jnp.bfloat16)
    right_rows[:, :first] = own_rows(q_first, row, right_rows.shape[0])
    right_rows[:, first:] = own_rows(qr, row, right_rows.shape[0])
    left_rows[...] = own_rows(ql, col, left_rows.shape[0])

    wait(late)
    blocks = grad.shape[0] // LANES
    for i in range(blocks):
        part = left_half[:, block(i)]
        both = [grad[...], moment[...].astype(jnp.bfloat16)]
        for n, matrix in enumerate(both):
            inner[pl.ds(n * grad.shape[0] + i * LANES, LANES), :] = mm(part, matrix, ((0,), (0,))).astype(jnp.bfloat16)
    for i in range(blocks):
        rotated_grad = mm(inner[block(i), :], right_half[...], ((1,), (0,)))
        rotated_moment = mm(inner[pl.ds(grad.shape[0] + i * LANES, LANES), :], right_half[...], ((1,), (0,)))
        new_second = SECOND_DECAY * second[block(i), :] + (1.0 - SECOND_DECAY) * rotated_grad * rotated_grad
        second[block(i), :] = new_second
        out.append(copies.start(second.at[block(i), :], second_out.at[block(i), :]))
        turn[block(i), :] = (rotated_moment / (jnp.sqrt(new_second) + EPSILON)).astype(jnp.bfloat16)
    for i in range(blocks):
        turned = mm(left_half[block(i), :], turn[...], ((1,), (0,))).astype(jnp.bfloat16)
        update = mm(turned, right_half[...], ((1,), (1,)))
        old = weight[block(i), :]
        weight[block(i), :] = old - STEP_SIZE * (update + WEIGHT_DECAY * old)
        out.append(copies.start(weight.at[block(i), :], weight_out.at[block(i), :]))
    wait(out)


def rest(me, gh, gl, q_first, tiles, bases, others, left, sums, rows_l):
    args = [gh, gl, q_first, *tiles, *left] + [p for group in (bases, others, sums) for _, p in group]
    rows_r, size_r = bases[0][1].shape
    width = size_r - q_first.shape[1]
    size_l = left[0].shape[0]
    tile = tiles[0].shape
    f32, bf16 = jnp.float32, jnp.bfloat16
    vmem, anywhere = pl.BlockSpec(memory_space=pltpu.VMEM), pl.BlockSpec(memory_space=pl.ANY)
    return pl.pallas_call(
        functools.partial(rest_kernel, *[[d for d, _ in group] for group in (bases, others, sums)]),
        out_shape=[
            jax.ShapeDtypeStruct(tile, f32),
            jax.ShapeDtypeStruct(tile, f32),
            jax.ShapeDtypeStruct(tile, f32),
            jax.ShapeDtypeStruct((rows_r, size_r), f32),
            jax.ShapeDtypeStruct((rows_l, size_l), f32),
            jax.ShapeDtypeStruct((rows_l, size_l), f32),
        ],
        in_specs=any_specs(len(args)),
        out_specs=[anywhere] * 3 + [vmem] * 3,
        scratch_shapes=[
            pltpu.VMEM((size_r, size_r), bf16),
            pltpu.VMEM((size_r, size_r), bf16),
            pltpu.VMEM((size_r, size_r - width), f32),
            pltpu.VMEM((size_r, width), f32),
            pltpu.VMEM((size_r, width), f32),
            pltpu.VMEM((size_l, size_l), f32),
            pltpu.VMEM((size_l, size_l), f32),
            pltpu.VMEM((size_l, offsets(size_l) * LANES), bf16),
            pltpu.VMEM((size_l, size_l), f32),
            pltpu.VMEM((size_l, size_l), bf16),
            pltpu.VMEM((size_l, size_l), bf16),
            *chain_scratch(width, size_r),
            *chain_scratch(size_l, size_l),
            pltpu.VMEM(tile, bf16),
            pltpu.VMEM(tile, f32),
            pltpu.VMEM(tile, f32),
            pltpu.VMEM(tile, f32),
            pltpu.VMEM((2 * tile[0], tile[1]), bf16),
            pltpu.VMEM(tile, bf16),
            pltpu.VMEM((size_r, size_r), bf16),
            pltpu.VMEM((size_l, size_l), bf16),
            pltpu.SemaphoreType.DMA((len(args) + 1 + 2 * (tile[0] // LANES),)),
        ],
        compiler_params=pltpu.CompilerParams(vmem_limit_bytes=VMEM_LIMIT),
    )(me, *args)


def swap(x, axis, distance):
    count = lax.axis_size(axis)
    return lax.ppermute(x, axis, [(i, i ^ distance) for i in range(count)])


def distances(axis):
    count = lax.axis_size(axis)
    return [1 << b for b in range(count.bit_length() - 1)]


def spread(held, axis, steps):
    for distance in steps:
        held = held + [(at ^ distance, swap(piece, axis, distance)) for at, piece in held]
    return held


def sum_halves(x, axis):
    me, kind = lax.axis_index(axis), x.dtype
    if lax.axis_size(axis) == 1:
        return x, [(0, x)]
    rows = x.shape[0] // 2
    own = lax.rem(me, 2)
    keep = lax.dynamic_slice_in_dim(x, own * rows, rows, 0)
    other = lax.dynamic_slice_in_dim(x, (1 - own) * rows, rows, 0)
    total = keep.astype(jnp.float32) + swap(other, axis, 1).astype(jnp.float32)
    for distance in distances(axis)[1:]:
        total = total.astype(kind)
        total = total.astype(jnp.float32) + swap(total, axis, distance).astype(jnp.float32)
    total = total.astype(kind)
    return total, [(0, total), (1, swap(total, axis, 1))]


def gather_right(gram, basis, width):
    count = lax.axis_size("row")
    grams, bases = [(0, gram)], [(0, basis)]
    if count == 1:
        return grams, bases, [], gram
    window = half_window(gram.shape[1])
    half = lax.div(2 * lax.axis_index("row"), count)
    mine = lax.dynamic_slice_in_dim(gram, half * (gram.shape[1] - window), window, 1)
    mine = jnp.concatenate([mine, basis[:, :width]], axis=1)
    others = [(count // 2, swap(mine, "row", count // 2))]
    near = distances("row")[-2::-1]
    return spread(grams, "row", near), spread(bases, "row", near), spread(others, "row", near), mine


def body(grad, weight, moment, second, gram_left, basis_left, gram_right, basis_right):
    block_left, block_right = grad.shape
    first = max(block_right - block_left, LANES)
    count = lax.axis_size("row")
    me = jnp.stack([lax.axis_index("row"), lax.axis_index("col")])
    left = [lax.all_gather(x[0], "col", axis=0, tiled=True) for x in (gram_left, basis_left)]
    grams, bases, others, mine = gather_right(gram_right[0], basis_right[0], first)
    grad_after, _ = lax.optimization_barrier((grad, mine))
    terms_right, terms_left = terms(
        grad_after, 1.0 / (block_right * lax.axis_size("col")), 1.0 / (block_left * count)
    )
    sent, sums_right = sum_halves(terms_right, "row")
    _, sums_left = sum_halves(terms_left, "col")
    last, _ = lax.optimization_barrier((basis_right[0][:, first:], sent))
    last = [(d, swap(last, "row", d)) for d in range(count // 2, count)] if count > 1 else []
    new_gram_right, gh, gl, q_first = head(me, count, grams, bases, others, sums_right, first)
    new_weight, new_moment, new_second, basis_rows_right, basis_rows_left, new_gram_left = rest(
        me, gh, gl, q_first, (grad, weight, moment, second), bases, last, left, sums_left, gram_left.shape[1]
    )
    return (
        new_weight,
        new_moment,
        new_second,
        new_gram_left[None],
        basis_rows_left[None],
        new_gram_right[None],
        basis_rows_right[None],
    )


def solution(mesh):
    specs = (
        P("row", "col"),
        P("row", "col"),
        P("row", "col"),
        P("row", "col"),
        P("row", "col", None),
        P("row", "col", None),
        P("col", "row", None),
        P("col", "row", None),
    )
    out_specs = specs[:3] + specs[4:]
    return jax.shard_map(body, mesh=mesh, in_specs=specs, out_specs=out_specs, check_vma=False)
```

```python
import functools
import jax
import jax.numpy as jnp
from jax import lax
from jax.experimental import pallas as pl
from jax.experimental.pallas import tpu as pltpu
from jax.sharding import PartitionSpec as P

STAT_DECAY = 0.95
FIRST_DECAY = 0.9
SECOND_DECAY = 0.95
EPSILON = 1e-08
STEP_SIZE = 0.02
WEIGHT_DECAY = 0.01
LANES = 128
ROWS = 8
VMEM_LIMIT = 56 * 2**20


def sub_row(x, k):
    return jnp.broadcast_to(x[k : k + 1, :], (ROWS, LANES))


def lane_col(x, c):
    return jnp.broadcast_to(x[:, c : c + 1], (ROWS, LANES))


def reciprocal(p):
    guess = pl.reciprocal(p, approx=True)
    return guess * (2.0 - p * guess)


def inverse_factor(rows):
    count = LANES // ROWS
    rows = list(rows)
    subs = lax.broadcasted_iota(jnp.int32, (ROWS, LANES), 0)
    lanes = lax.broadcasted_iota(jnp.int32, (ROWS, LANES), 1)
    out = []
    for s in range(count):
        base = s * ROWS
        pivot = rows[s]
        here = (lanes >= base) & (lanes < base + ROWS)
        cols = [lane_col(pivot, base + k) for k in range(ROWS)]
        full = jnp.where(here, (lanes == subs + base).astype(jnp.float32), pivot)
        forward = full
        pivots = jnp.ones((ROWS, LANES), jnp.float32)
        yield
        for j in range(0, ROWS, 2):
            a, b, d = sub_row(cols[j], j), sub_row(cols[j], j + 1), sub_row(cols[j + 1], j + 1)
            det = a * d - b * b
            inv = reciprocal(det)
            pair = (subs == j) | (subs == j + 1)
            one = jnp.where(pair, jnp.where(subs == j, -1.0, 0.0), cols[j])
            two = jnp.where(pair, jnp.where(subs == j, 0.0, -1.0), cols[j + 1])
            for k in range(j + 2, min(j + 4, ROWS)):
                x, y = sub_row(cols[k], j), sub_row(cols[k], j + 1)
                change = one * (d * x - b * y) + two * (a * y - b * x)
                cols[k] = jnp.where(pair, 0.0, cols[k]) - change * inv
            yield
            one, two = (one * d - two * b) * inv, (two * a - one * b) * inv
            for k in range(j + 4, ROWS):
                x, y = sub_row(cols[k], j), sub_row(cols[k], j + 1)
                cols[k] = jnp.where(pair, 0.0, cols[k]) - (one * x + two * y)
            full = jnp.where(pair, 0.0, full) - (one * sub_row(full, j) + two * sub_row(full, j + 1))
            inner = b * reciprocal(a)
            below = subs > j + 1
            lower = jnp.where(below, one, jnp.where(subs == j + 1, inner, 0.0))
            change = lower * sub_row(forward, j)
            if j + 2 < ROWS:
                change = change + jnp.where(below, two, 0.0) * sub_row(forward, j + 1)
            forward = forward - change
            pivots = jnp.where(subs == j, a, jnp.where(subs == j + 1, d - inner * b, pivots))
            yield
        out.append(jnp.where(lanes < base + ROWS, forward * lax.rsqrt(pivots), 0.0))
        if s < count - 1:
            spread = [sub_row(full, k) for k in range(ROWS)]
            for i in range(s + 1, count):
                coeffs = [lane_col(rows[i], base + k) for k in range(ROWS)]
                terms = [coeffs[k] * spread[k] for k in range(ROWS)]
                while len(terms) > 1:
                    terms = [a + b for a, b in zip(terms[::2], terms[1::2])]
                rows[i] = jnp.where(here, 0.0, rows[i]) - terms[0]
                yield
    return out


def in_turns(generators, fills):
    results = [None] * len(generators)
    live = list(enumerate(generators))
    fills = list(fills)
    total, turn, done = 250, 0, 0
    while live:
        for at, generator in list(live):
            try:
                next(generator)
            except StopIteration as stop:
                results[at] = stop.value
                live.remove((at, generator))
        turn += 1
        while done < len(fills) and done * total <= turn * len(fills):
            fills[done]()
            done += 1
    for fill in fills[done:]:
        fill()
    return results


def split(x):
    hi = x.astype(jnp.bfloat16)
    return hi, (x - hi.astype(jnp.float32)).astype(jnp.bfloat16)


def stack_left(x, axis):
    hi, lo = split(x)
    return jnp.concatenate([hi, hi, lo], axis=axis)


def stack_right(x, axis):
    hi, lo = split(x)
    return jnp.concatenate([hi, lo, hi], axis=axis)


def mm(a, b, dims):
    return lax.dot_general(a, b, (dims, ((), ())), preferred_element_type=jnp.float32)


def mm_nn(a, b):
    return mm(stack_left(a, 1), stack_right(b, 0), ((1,), (0,)))


def mm_nt(a, b):
    return mm(stack_left(a, 1), stack_right(b, 1), ((1,), (1,)))


def product(ah, al, bh, bl, dims):
    return mm(ah, bh, dims) + (mm(ah, bl, dims) + mm(al, bh, dims))


def block(i):
    return pl.ds(i * LANES, LANES) if isinstance(i, int) else pl.ds(pl.multiple_of(i * LANES, LANES), LANES)


class Chain:
    def __init__(self, z_ref, w_ref, q_ref):
        self.z, self.w, self.q = z_ref, w_ref, q_ref
        self.width = z_ref.shape[1]
        self.blocks = self.width // LANES

    def cross(self):
        hi, lo = split(self.z[self.width :, :])
        dims = ((0,), (0,))
        self.z[: self.width, :] = product(hi, lo, hi, lo, dims)
        self.w[...] = jnp.zeros_like(self.w)

    def look(self, j):
        self.before = block(lax.max(j - 1, 0))
        self.w_nt = stack_right(self.w[...], 1)
        at = block(j)
        low = mm(stack_left(self.z[at, self.before], 1), self.w_nt, ((1,), (1,)))
        diagonal = self.z[at, at] - mm_nt(low, low)
        return [diagonal[i * ROWS : (i + 1) * ROWS, :] for i in range(LANES // ROWS)]

    def fills(self):
        def rows_of_u():
            self.u = stack_right(mm_nn(self.w[...], self.z[self.before, :]), 0)

        def rows(i):
            at = block(i)
            p = mm(stack_left(self.z[at, self.before], 1), self.w_nt, ((1,), (1,)))
            if i >= self.blocks:
                self.q[block(i - self.blocks), self.before] = p
            self.z[at, :] -= mm(stack_left(p, 1), self.u, ((1,), (0,)))

        return [rows_of_u] + [functools.partial(rows, i) for i in range(self.z.shape[0] // LANES)]

    def store(self, out):
        for i, row in enumerate(out):
            self.w[i * ROWS : (i + 1) * ROWS, :] = row

    def finish(self):
        last = block(self.blocks - 1)
        self.q[:, last] = mm_nt(self.z[self.width :, last], self.w[...])


def run_chains(chains):
    def step_of(members):
        def step(j, carry):
            rows = [chain.look(j) for chain in members]
            fills = [fill for chain in members for fill in chain.fills()]
            for chain, out in zip(members, in_turns([inverse_factor(r) for r in rows], fills)):
                chain.store(out)
            return carry

        return step

    start = 0
    for end in sorted({chain.blocks for chain in chains}):
        lax.fori_loop(start, end, step_of([chain for chain in chains if chain.blocks >= end]), 0)
        start = end
    for chain in chains:
        chain.finish()


class Copies:
    def __init__(self, semaphores):
        self.semaphores, self.used = semaphores, 0

    def start(self, source, target):
        copy = pltpu.make_async_copy(source, target, self.semaphores.at[self.used])
        self.used += 1
        copy.start()
        return copy


def wait(copies):
    for copy in copies:
        copy.wait()


def offsets(size):
    return size // LANES // 2 + 1


def pack_products(cols, out_ref, dims, scale):
    blocks = len(cols)
    for i in range(blocks):
        for o in range(offsets(blocks * LANES)):
            term = mm(cols[i], cols[(i + o) % blocks], dims)
            out_ref[block(i), block(o)] = (term * scale).astype(out_ref.dtype)


def terms_kernel(scale_left, scale_right, grad_ref, right_ref, left_ref):
    rows, columns = grad_ref.shape
    pack_products([grad_ref[:, block(i)] for i in range(columns // LANES)], right_ref, ((0,), (0,)), scale_right)
    pack_products([grad_ref[block(i), :] for i in range(rows // LANES)], left_ref, ((1,), (1,)), scale_left)


def terms(grad, scale_left, scale_right):
    rows, columns = grad.shape
    return pl.pallas_call(
        functools.partial(terms_kernel, scale_left, scale_right),
        out_shape=[
            jax.ShapeDtypeStruct((columns, offsets(columns) * LANES), jnp.bfloat16),
            jax.ShapeDtypeStruct((rows, offsets(rows) * LANES), jnp.bfloat16),
        ],
        compiler_params=pltpu.CompilerParams(vmem_limit_bytes=VMEM_LIMIT),
    )(grad)


def rows_at(me, distance, rows):
    return pl.ds(pl.multiple_of((me ^ distance) * rows, ROWS), rows)


def new_gram(gram_ref, packed_ref, gh_ref, gl_ref):
    blocks = gram_ref.shape[0] // LANES
    count = offsets(gram_ref.shape[0])

    def put(i, k, term):
        value = gram_ref[block(i), block(k)] * STAT_DECAY + term
        gram_ref[block(i), block(k)] = value
        gh_ref[block(i), block(k)], gl_ref[block(i), block(k)] = split(value)

    for i in range(blocks):
        for o in range(count):
            k = (i + o) % blocks
            term = packed_ref[block(i), block(o)].astype(jnp.float32) * (1.0 - STAT_DECAY)
            put(i, k, term)
            if o > 0 and not (blocks % 2 == 0 and o == count - 1):
                put(k, i, term.T)


def image(z_ref, gh_ref, gl_ref, basis_ref):
    width = z_ref.shape[1]
    bh, bl = split(basis_ref[...])
    for i in range(gh_ref.shape[0] // LANES):
        z_ref[pl.ds(width + i * LANES, LANES), :] = product(
            gh_ref[block(i), :], gl_ref[block(i), :], bh, bl, ((1,), (0,))
        )


def own_rows(ref, me, rows):
    return ref[pl.ds(pl.multiple_of(me * rows, ROWS), rows), :]


def half_window(size):
    return -(-size // 2 // LANES) * LANES


def fill_halves(gram, half):
    size = gram.shape[0]
    window = half_window(size)
    rest = size - window
    near = half * window
    far = pl.ds(pl.multiple_of((1 - half) * rest, LANES), window)
    for i in range(rest // LANES):
        at = pl.ds(pl.multiple_of(near + i * LANES, LANES), LANES)
        gram[far, at] = gram[at, far].T


def packed_copies(copies, me, sums, packed):
    side = lax.rem(me, 2) if len(sums) > 1 else 0
    return [copies.start(piece, packed.at[rows_at(side, d, piece.shape[0]), :]) for d, piece in sums]


def take(refs, distances_of):
    return [(d, refs.pop(0)) for d in distances_of]


def head_kernel(count, owns, others, sums, *refs):
    me_ref, refs = refs[0], list(refs[1:])
    gram_in, basis_in, other_in, sum_in = take(refs, owns), take(refs, owns), take(refs, others), take(refs, sums)
    rows_ref, gh_ref, gl_ref, q_ref, gram, packed, basis, gh, gl, rows_own, z, w, semaphores = refs
    me = me_ref[0]
    copies = Copies(semaphores)
    width = basis.shape[1]
    half = lax.div(2 * me, count)
    window = half_window(gram.shape[0])
    others_at = pl.ds(pl.multiple_of((1 - half) * (gram.shape[0] - window), LANES), window)
    first, second = [], []
    for d, piece in gram_in:
        first.append(copies.start(piece, gram.at[rows_at(me, d, piece.shape[0]), :]))
    for d, piece in other_in:
        at = rows_at(me, d, piece.shape[0])
        first.append(copies.start(piece.at[:, pl.ds(0, window)], gram.at[at, others_at]))
    first += packed_copies(copies, me, sum_in, packed)
    for d, piece in basis_in:
        at = rows_at(me, d, piece.shape[0])
        second.append(copies.start(piece.at[:, pl.ds(0, width)], basis.at[at, :]))
    for d, piece in other_in:
        at = rows_at(me, d, piece.shape[0])
        second.append(copies.start(piece.at[:, pl.ds(window, width)], basis.at[at, :]))
    wait(first)
    if other_in:
        fill_halves(gram, half)
    new_gram(gram, packed, gh, gl)
    rows_own[...] = own_rows(gram, me, rows_own.shape[0])
    out = [copies.start(gh, gh_ref), copies.start(gl, gl_ref), copies.start(rows_own, rows_ref)]
    wait(second)
    image(z, gh, gl, basis)
    chain = Chain(z, w, q_ref)
    chain.cross()
    run_chains([chain])
    wait(out)


def any_specs(count):
    return [pl.BlockSpec(memory_space=pltpu.SMEM)] + [pl.BlockSpec(memory_space=pl.ANY)] * count


def chain_scratch(width, rows):
    return [pltpu.VMEM((width + rows, width), jnp.float32), pltpu.VMEM((LANES, LANES), jnp.float32)]


def head(me, count, grams, bases, others, sums, width):
    args = [p for group in (grams, bases, others, sums) for _, p in group]
    rows, size = grams[0][1].shape
    f32, bf16 = jnp.float32, jnp.bfloat16
    return pl.pallas_call(
        functools.partial(head_kernel, count, *[[d for d, _ in group] for group in (grams, others, sums)]),
        out_shape=[
            jax.ShapeDtypeStruct((rows, size), f32),
            jax.ShapeDtypeStruct((size, size), bf16),
            jax.ShapeDtypeStruct((size, size), bf16),
            jax.ShapeDtypeStruct((size, width), f32),
        ],
        in_specs=any_specs(len(args)),
        out_specs=[pl.BlockSpec(memory_space=pl.ANY)] * 3 + [pl.BlockSpec(memory_space=pltpu.VMEM)],
        scratch_shapes=[
            pltpu.VMEM((size, size), f32),
            pltpu.VMEM((size, offsets(size) * LANES), bf16),
            pltpu.VMEM((size, width), f32),
            pltpu.VMEM((size, size), bf16),
            pltpu.VMEM((size, size), bf16),
            pltpu.VMEM((rows, size), f32),
            *chain_scratch(width, size),
            pltpu.SemaphoreType.DMA((len(args) + len(others) + 3,)),
        ],
        compiler_params=pltpu.CompilerParams(vmem_limit_bytes=VMEM_LIMIT),
    )(me, *args)


def rest_kernel(bases, others, lefts, *refs):
    me_ref, refs = refs[0], list(refs[1:])
    gh_in, gl_in, q_in, grad_in, weight_in, moment_in, second_in, sum_in = refs[:8]
    refs = refs[8:]
    basis_in, other_in, left_in = take(refs, bases), take(refs, others), take(refs, lefts)
    weight_out, moment_out, second_out, right_rows, left_rows, gram_rows = refs[:6]
    (gh, gl, q_first, basis, qr, ql, gram_l, packed_l, basis_l, glh, gll, zr, wr, zl, wl) = refs[6:21]
    (grad, weight, moment, second, inner, turn, right_half, left_half, semaphores) = refs[21:]
    row, col = me_ref[0], me_ref[1]
    copies = Copies(semaphores)
    first = q_first.shape[1]
    width = zr.shape[1]
    start = [copies.start(gh_in, gh), copies.start(gl_in, gl)]
    for d, piece in basis_in:
        at = rows_at(row, d, piece.shape[0])
        start.append(copies.start(piece.at[:, pl.ds(first, width)], basis.at[at, :]))
    for d, piece in other_in:
        start.append(copies.start(piece, basis.at[rows_at(row, d, piece.shape[0]), :]))
    project = [copies.start(q_in, q_first)]
    size = gram_l.shape[0]
    rows = left_rows.shape[0]
    left_copies = [copies.start(sum_in, packed_l)]
    for ats, pieces in left_in:
        for n, at in enumerate(ats):
            for i, ref in enumerate((gram_l, basis_l)):
                piece = pieces.at[pl.ds(n * rows, rows), pl.ds(i * size, size)]
                left_copies.append(copies.start(piece, ref.at[rows_at(col, at, rows), :]))
    tail = [copies.start(grad_in, grad), copies.start(moment_in, moment)]
    late = [copies.start(second_in, second), copies.start(weight_in, weight)]

    wait(start)
    image(zr, gh, gl, basis)
    wait(project)
    qh, qo = split(q_first[...])
    xh, xl = split(zr[width:, :])
    sh, sl = split(product(qh, qo, xh, xl, ((0,), (0,))))
    zr[width:, :] -= product(qh, qo, sh, sl, ((1,), (0,)))
    wait(left_copies)
    new_gram(gram_l, packed_l, glh, gll)
    gram_rows[...] = own_rows(gram_l, col, gram_rows.shape[0])
    image(zl, glh, gll, basis_l)
    right, left = Chain(zr, wr, qr), Chain(zl, wl, ql)
    right.cross()
    left.cross()
    right_half[:, :first] = q_first[...].astype(jnp.bfloat16)
    wait(tail)
    for i in range(grad.shape[0] // LANES):
        moment[block(i), :] = FIRST_DECAY * moment[block(i), :] + (1.0 - FIRST_DECAY) * grad[block(i), :].astype(
            jnp.float32
        )
    out = [copies.start(moment, moment_out)]
    run_chains([left, right] if left.blocks <= right.blocks else [right, left])
    left_half[...] = ql[...].astype(jnp.bfloat16)
    right_half[:, first:] = qr[...].astype(jnp.bfloat16)
    right_rows[:, :first] = own_rows(q_first, row, right_rows.shape[0])
    right_rows[:, first:] = own_rows(qr, row, right_rows.shape[0])
    left_rows[...] = own_rows(ql, col, left_rows.shape[0])

    wait(late)
    blocks = grad.shape[0] // LANES
    for i in range(blocks):
        part = left_half[:, block(i)]
        both = [grad[...], moment[...].astype(jnp.bfloat16)]
        for n, matrix in enumerate(both):
            inner[pl.ds(n * grad.shape[0] + i * LANES, LANES), :] = mm(part, matrix, ((0,), (0,))).astype(jnp.bfloat16)
    for i in range(blocks):
        rotated_grad = mm(inner[block(i), :], right_half[...], ((1,), (0,)))
        rotated_moment = mm(inner[pl.ds(grad.shape[0] + i * LANES, LANES), :], right_half[...], ((1,), (0,)))
        new_second = SECOND_DECAY * second[block(i), :] + (1.0 - SECOND_DECAY) * rotated_grad * rotated_grad
        second[block(i), :] = new_second
        out.append(copies.start(second.at[block(i), :], second_out.at[block(i), :]))
        turn[block(i), :] = (rotated_moment / (jnp.sqrt(new_second) + EPSILON)).astype(jnp.bfloat16)
    for i in range(blocks):
        turned = mm(left_half[block(i), :], turn[...], ((1,), (0,))).astype(jnp.bfloat16)
        update = mm(turned, right_half[...], ((1,), (1,)))
        old = weight[block(i), :]
        weight[block(i), :] = old - STEP_SIZE * (update + WEIGHT_DECAY * old)
        out.append(copies.start(weight.at[block(i), :], weight_out.at[block(i), :]))
    wait(out)


def rest(me, gh, gl, q_first, tiles, bases, others, lefts, sums_l):
    args = [gh, gl, q_first, *tiles, sums_l] + [p for _, p in bases + others + lefts]
    rows_r, size_r = bases[0][1].shape
    width = size_r - q_first.shape[1]
    rows_l, size_l = lefts[0][1].shape[0], sums_l.shape[0]
    tile = tiles[0].shape
    f32, bf16 = jnp.float32, jnp.bfloat16
    vmem, anywhere = pl.BlockSpec(memory_space=pltpu.VMEM), pl.BlockSpec(memory_space=pl.ANY)
    return pl.pallas_call(
        functools.partial(rest_kernel, *[[d for d, _ in group] for group in (bases, others, lefts)]),
        out_shape=[
            jax.ShapeDtypeStruct(tile, f32),
            jax.ShapeDtypeStruct(tile, f32),
            jax.ShapeDtypeStruct(tile, f32),
            jax.ShapeDtypeStruct((rows_r, size_r), f32),
            jax.ShapeDtypeStruct((rows_l, size_l), f32),
            jax.ShapeDtypeStruct((rows_l, size_l), f32),
        ],
        in_specs=any_specs(len(args)),
        out_specs=[anywhere] * 3 + [vmem] * 3,
        scratch_shapes=[
            pltpu.VMEM((size_r, size_r), bf16),
            pltpu.VMEM((size_r, size_r), bf16),
            pltpu.VMEM((size_r, size_r - width), f32),
            pltpu.VMEM((size_r, width), f32),
            pltpu.VMEM((size_r, width), f32),
            pltpu.VMEM((size_l, size_l), f32),
            pltpu.VMEM((size_l, size_l), f32),
            pltpu.VMEM((size_l, offsets(size_l) * LANES), bf16),
            pltpu.VMEM((size_l, size_l), f32),
            pltpu.VMEM((size_l, size_l), bf16),
            pltpu.VMEM((size_l, size_l), bf16),
            *chain_scratch(width, size_r),
            *chain_scratch(size_l, size_l),
            pltpu.VMEM(tile, bf16),
            pltpu.VMEM(tile, f32),
            pltpu.VMEM(tile, f32),
            pltpu.VMEM(tile, f32),
            pltpu.VMEM((2 * tile[0], tile[1]), bf16),
            pltpu.VMEM(tile, bf16),
            pltpu.VMEM((size_r, size_r), bf16),
            pltpu.VMEM((size_l, size_l), bf16),
            pltpu.SemaphoreType.DMA((len(args) + 1 + 2 * (size_l // rows_l) + 2 * (tile[0] // LANES),)),
        ],
        compiler_params=pltpu.CompilerParams(vmem_limit_bytes=VMEM_LIMIT),
    )(me, *args)


def swap(x, axis, distance):
    count = lax.axis_size(axis)
    return lax.ppermute(x, axis, [(i, i ^ distance) for i in range(count)])


def distances(axis):
    count = lax.axis_size(axis)
    return [1 << b for b in range(count.bit_length() - 1)]


def spread(held, axis, steps):
    for distance in steps:
        held = held + [(at ^ distance, swap(piece, axis, distance)) for at, piece in held]
    return held


def parts(x, axis, distance):
    rows = x.shape[0] // 2
    own = lax.rem(lax.div(lax.axis_index(axis), distance), 2)
    return (lax.dynamic_slice_in_dim(x, at * rows, rows, 0) for at in (own, 1 - own))


def gather_stacked(x, axis, after):
    held = [([0], x)]
    for distance in reversed(distances(axis)):
        sent = jnp.concatenate([piece for _, piece in held]) if len(held) > 1 else x
        if distance == 1:
            sent, _ = lax.optimization_barrier((sent, after))
        held.append(([at ^ distance for ats, _ in held for at in ats], swap(sent, axis, distance)))
    return held


def sum_halves(x, axis, after):
    kind = x.dtype
    if lax.axis_size(axis) == 1:
        return x, [(0, x)]
    keep, other = parts(x, axis, 1)
    total = keep.astype(jnp.float32) + swap(other, axis, 1).astype(jnp.float32)
    for distance in distances(axis)[1:]:
        total, _ = lax.optimization_barrier((total.astype(kind), after))
        total = total.astype(jnp.float32) + swap(total, axis, distance).astype(jnp.float32)
    total = total.astype(kind)
    return total, [(0, total), (1, swap(total, axis, 1))]


def gather_right(gram, basis, width):
    count = lax.axis_size("row")
    grams, bases = [(0, gram)], [(0, basis)]
    if count == 1:
        return grams, bases, [], gram
    window = half_window(gram.shape[1])
    half = lax.div(2 * lax.axis_index("row"), count)
    mine = lax.dynamic_slice_in_dim(gram, half * (gram.shape[1] - window), window, 1)
    mine = jnp.concatenate([mine, basis[:, :width]], axis=1)
    others = [(count // 2, swap(mine, "row", count // 2))]
    near = distances("row")[-2::-1]
    return spread(grams, "row", near), spread(bases, "row", near), spread(others, "row", near), mine


def body(grad, weight, moment, second, gram_left, basis_left, gram_right, basis_right):
    block_left, block_right = grad.shape
    first = max(block_right - block_left, LANES)
    count = lax.axis_size("row")
    me = jnp.stack([lax.axis_index("row"), lax.axis_index("col")])
    grams, bases, others, mine = gather_right(gram_right[0], basis_right[0], first)
    both, grad_after, _ = lax.optimization_barrier(((gram_left[0], basis_left[0]), grad, mine))
    terms_right, terms_left = terms(
        grad_after, 1.0 / (block_right * lax.axis_size("col")), 1.0 / (block_left * count)
    )
    arrived = others[0][1] if others else mine
    sent, sums_right = sum_halves(terms_right, "row", arrived)
    sums_left = lax.psum_scatter(terms_left, "col", scatter_dimension=0, tiled=True)
    left = gather_stacked(jnp.concatenate(both, axis=1), "col", sums_left)
    sums_left = lax.all_gather(sums_left, "col", axis=0, tiled=True)
    last, _ = lax.optimization_barrier((basis_right[0][:, first:], sent))
    last = [(d, swap(last, "row", d)) for d in range(count // 2, count)] if count > 1 else []
    new_gram_right, gh, gl, q_first = head(me, count, grams, bases, others, sums_right, first)
    new_weight, new_moment, new_second, basis_rows_right, basis_rows_left, new_gram_left = rest(
        me, gh, gl, q_first, (grad, weight, moment, second), bases, last, left, sums_left
    )
    return (
        new_weight,
        new_moment,
        new_second,
        new_gram_left[None],
        basis_rows_left[None],
        new_gram_right[None],
        basis_rows_right[None],
    )


def solution(mesh):
    specs = (
        P("row", "col"),
        P("row", "col"),
        P("row", "col"),
        P("row", "col"),
        P("row", "col", None),
        P("row", "col", None),
        P("col", "row", None),
        P("col", "row", None),
    )
    out_specs = specs[:3] + specs[4:]
    return jax.shard_map(body, mesh=mesh, in_specs=specs, out_specs=out_specs, check_vma=False)
```

```python
import functools
from itertools import zip_longest
import jax
import jax.numpy as jnp
from jax import lax
from jax.experimental import pallas as pl
from jax.experimental.pallas import tpu as pltpu
from jax.sharding import PartitionSpec as P

STAT_DECAY = 0.95
FIRST_DECAY = 0.9
SECOND_DECAY = 0.95
EPSILON = 1e-08
STEP_SIZE = 0.02
WEIGHT_DECAY = 0.01
LANES = 128
ROWS = 8
TILE = 256
VMEM_LIMIT = 56 * 2**20


def sub_row(x, k):
    return jnp.broadcast_to(x[k : k + 1, :], (ROWS, LANES))


def lane_col(x, c):
    return jnp.broadcast_to(x[:, c : c + 1], (ROWS, LANES))


def reciprocal(p):
    guess = pl.reciprocal(p, approx=True)
    return guess * (2.0 - p * guess)


def inverse_factor(rows):
    count = LANES // ROWS
    rows = list(rows)
    subs = lax.broadcasted_iota(jnp.int32, (ROWS, LANES), 0)
    lanes = lax.broadcasted_iota(jnp.int32, (ROWS, LANES), 1)
    out = []
    for s in range(count):
        base = s * ROWS
        pivot = rows[s]
        here = (lanes >= base) & (lanes < base + ROWS)
        cols = [lane_col(pivot, base + k) for k in range(ROWS)]
        full = jnp.where(here, (lanes == subs + base).astype(jnp.float32), pivot)
        forward = full
        pivots = jnp.ones((ROWS, LANES), jnp.float32)
        yield
        for j in range(0, ROWS, 2):
            a, b, d = sub_row(cols[j], j), sub_row(cols[j], j + 1), sub_row(cols[j + 1], j + 1)
            det = a * d - b * b
            inv = reciprocal(det)
            pair = (subs == j) | (subs == j + 1)
            one = jnp.where(pair, jnp.where(subs == j, -1.0, 0.0), cols[j])
            two = jnp.where(pair, jnp.where(subs == j, 0.0, -1.0), cols[j + 1])
            for k in range(j + 2, min(j + 4, ROWS)):
                x, y = sub_row(cols[k], j), sub_row(cols[k], j + 1)
                change = one * (d * x - b * y) + two * (a * y - b * x)
                cols[k] = jnp.where(pair, 0.0, cols[k]) - change * inv
            yield
            one, two = (one * d - two * b) * inv, (two * a - one * b) * inv
            for k in range(j + 4, ROWS):
                x, y = sub_row(cols[k], j), sub_row(cols[k], j + 1)
                cols[k] = jnp.where(pair, 0.0, cols[k]) - (one * x + two * y)
            full = jnp.where(pair, 0.0, full) - (one * sub_row(full, j) + two * sub_row(full, j + 1))
            inner = b * reciprocal(a)
            below = subs > j + 1
            lower = jnp.where(below, one, jnp.where(subs == j + 1, inner, 0.0))
            change = lower * sub_row(forward, j)
            if j + 2 < ROWS:
                change = change + jnp.where(below, two, 0.0) * sub_row(forward, j + 1)
            forward = forward - change
            pivots = jnp.where(subs == j, a, jnp.where(subs == j + 1, d - inner * b, pivots))
            yield
        out.append(jnp.where(lanes < base + ROWS, forward * lax.rsqrt(pivots), 0.0))
        if s < count - 1:
            spread = [sub_row(full, k) for k in range(ROWS)]
            for i in range(s + 1, count):
                coeffs = [lane_col(rows[i], base + k) for k in range(ROWS)]
                terms = [coeffs[k] * spread[k] for k in range(ROWS)]
                while len(terms) > 1:
                    terms = [a + b for a, b in zip(terms[::2], terms[1::2])]
                rows[i] = jnp.where(here, 0.0, rows[i]) - terms[0]
                yield
    return out


def in_turns(generators, fills):
    results = [None] * len(generators)
    live = list(enumerate(generators))
    fills = list(fills)
    total, turn, done = 250, 0, 0
    while live:
        for at, generator in list(live):
            try:
                next(generator)
            except StopIteration as stop:
                results[at] = stop.value
                live.remove((at, generator))
        turn += 1
        while done < len(fills) and done * total <= turn * len(fills):
            fills[done]()
            done += 1
    for fill in fills[done:]:
        fill()
    return results


def split(x):
    hi = x.astype(jnp.bfloat16)
    return hi, (x - hi.astype(jnp.float32)).astype(jnp.bfloat16)


def stack_left(x, axis):
    hi, lo = split(x)
    return jnp.concatenate([hi, hi, lo], axis=axis)


def stack_right(x, axis):
    hi, lo = split(x)
    return jnp.concatenate([hi, lo, hi], axis=axis)


def mm(a, b, dims):
    return lax.dot_general(a, b, (dims, ((), ())), preferred_element_type=jnp.float32)


def mm_nn(a, b):
    return mm(stack_left(a, 1), stack_right(b, 0), ((1,), (0,)))


def mm_nt(a, b):
    return mm(stack_left(a, 1), stack_right(b, 1), ((1,), (1,)))


def product(ah, al, bh, bl, dims):
    return mm(ah, bh, dims) + (mm(ah, bl, dims) + mm(al, bh, dims))


def block(i):
    return pl.ds(i * LANES, LANES) if isinstance(i, int) else pl.ds(pl.multiple_of(i * LANES, LANES), LANES)


class Chain:
    def __init__(self, z_ref, w_ref, q_ref):
        self.z, self.w, self.q = z_ref, w_ref, q_ref
        self.width = z_ref.shape[1]
        self.blocks = self.width // LANES

    def cross(self):
        hi, lo = split(self.z[self.width :, :])
        dims = ((0,), (0,))
        self.z[: self.width, :] = product(hi, lo, hi, lo, dims)
        self.w[...] = jnp.zeros_like(self.w)

    def look(self, j):
        self.before = block(lax.max(j - 1, 0))
        self.w_nt = stack_right(self.w[...], 1)
        at = block(j)
        low = mm(stack_left(self.z[at, self.before], 1), self.w_nt, ((1,), (1,)))
        diagonal = self.z[at, at] - mm_nt(low, low)
        return [diagonal[i * ROWS : (i + 1) * ROWS, :] for i in range(LANES // ROWS)]

    def fills(self):
        def rows_of_u():
            self.u = stack_right(mm_nn(self.w[...], self.z[self.before, :]), 0)

        def panel():
            p = mm(stack_left(self.z[:, self.before], 1), self.w_nt, ((1,), (1,)))
            self.q[:, self.before] = p[self.width :, :]
            self.p = stack_left(p, 1)

        def columns(at):
            stop = min(at + TILE, self.width)
            self.z[:, at:stop] -= mm(self.p, self.u[:, at:stop], ((1,), (0,)))

        return [rows_of_u, panel] + [functools.partial(columns, at) for at in range(0, self.width, TILE)]

    def store(self, out):
        for i, row in enumerate(out):
            self.w[i * ROWS : (i + 1) * ROWS, :] = row

    def finish(self):
        last = block(self.blocks - 1)
        self.q[:, last] = mm_nt(self.z[self.width :, last], self.w[...])


def run_chains(chains):
    def step_of(members):
        def step(j, carry):
            rows = [chain.look(j) for chain in members]
            fills = [fill for several in zip_longest(*[chain.fills() for chain in members]) for fill in several if fill]
            for chain, out in zip(members, in_turns([inverse_factor(r) for r in rows], fills)):
                chain.store(out)
            return carry

        return step

    start = 0
    for end in sorted({chain.blocks for chain in chains}):
        lax.fori_loop(start, end, step_of([chain for chain in chains if chain.blocks >= end]), 0)
        start = end
    for chain in chains:
        chain.finish()


class Copies:
    def __init__(self, semaphores):
        self.semaphores, self.used = semaphores, 0

    def start(self, source, target):
        copy = pltpu.make_async_copy(source, target, self.semaphores.at[self.used])
        self.used += 1
        copy.start()
        return copy


def wait(copies):
    for copy in copies:
        copy.wait()


def offsets(size):
    return size // LANES // 2 + 1


def pack_products(cols, out_ref, dims, scale):
    blocks = len(cols)
    for i in range(blocks):
        for o in range(offsets(blocks * LANES)):
            term = mm(cols[i], cols[(i + o) % blocks], dims)
            out_ref[block(i), block(o)] = (term * scale).astype(out_ref.dtype)


def terms_kernel(scale_left, scale_right, grad_ref, right_ref, left_ref):
    rows, columns = grad_ref.shape
    pack_products([grad_ref[:, block(i)] for i in range(columns // LANES)], right_ref, ((0,), (0,)), scale_right)
    pack_products([grad_ref[block(i), :] for i in range(rows // LANES)], left_ref, ((1,), (1,)), scale_left)


def terms(grad, scale_left, scale_right):
    rows, columns = grad.shape
    return pl.pallas_call(
        functools.partial(terms_kernel, scale_left, scale_right),
        out_shape=[
            jax.ShapeDtypeStruct((columns, offsets(columns) * LANES), jnp.bfloat16),
            jax.ShapeDtypeStruct((rows, offsets(rows) * LANES), jnp.bfloat16),
        ],
        compiler_params=pltpu.CompilerParams(vmem_limit_bytes=VMEM_LIMIT),
    )(grad)


def rows_at(me, distance, rows):
    return pl.ds(pl.multiple_of((me ^ distance) * rows, ROWS), rows)


def new_gram(gram_ref, packed_ref, gh_ref, gl_ref):
    blocks = gram_ref.shape[0] // LANES
    count = offsets(gram_ref.shape[0])

    def put(i, k, term):
        value = gram_ref[block(i), block(k)] * STAT_DECAY + term
        gram_ref[block(i), block(k)] = value
        gh_ref[block(i), block(k)], gl_ref[block(i), block(k)] = split(value)

    for i in range(blocks):
        for o in range(count):
            k = (i + o) % blocks
            term = packed_ref[block(i), block(o)].astype(jnp.float32) * (1.0 - STAT_DECAY)
            put(i, k, term)
            if o > 0 and not (blocks % 2 == 0 and o == count - 1):
                put(k, i, term.T)


def image(z_ref, gh_ref, gl_ref, basis_ref):
    width = z_ref.shape[1]
    for at in range(0, width, TILE):
        stop = min(at + TILE, width)
        bh, bl = split(basis_ref[:, at:stop])
        z_ref[width:, at:stop] = product(gh_ref[...], gl_ref[...], bh, bl, ((1,), (0,)))


def own_rows(ref, me, rows):
    return ref[pl.ds(pl.multiple_of(me * rows, ROWS), rows), :]


def half_window(size):
    return -(-size // 2 // LANES) * LANES


def fill_halves(gram, half):
    size = gram.shape[0]
    window = half_window(size)
    rest = size - window
    near = half * window
    far = pl.ds(pl.multiple_of((1 - half) * rest, LANES), window)
    for i in range(rest // LANES):
        at = pl.ds(pl.multiple_of(near + i * LANES, LANES), LANES)
        gram[far, at] = gram[at, far].T


def packed_copies(copies, me, sums, packed):
    side = lax.rem(me, 2) if len(sums) > 1 else 0
    return [copies.start(piece, packed.at[rows_at(side, d, piece.shape[0]), :]) for d, piece in sums]


def take(refs, distances_of):
    return [(d, refs.pop(0)) for d in distances_of]


def head_kernel(count, owns, others, sums, *refs):
    me_ref, refs = refs[0], list(refs[1:])
    gram_in, basis_in, other_in, sum_in = take(refs, owns), take(refs, owns), take(refs, others), take(refs, sums)
    rows_ref, gh_ref, gl_ref, q_ref, gram, packed, basis, gh, gl, rows_own, z, w, semaphores = refs
    me = me_ref[0]
    copies = Copies(semaphores)
    width = basis.shape[1]
    half = lax.div(2 * me, count)
    window = half_window(gram.shape[0])
    others_at = pl.ds(pl.multiple_of((1 - half) * (gram.shape[0] - window), LANES), window)
    first, second = [], []
    for d, piece in gram_in:
        first.append(copies.start(piece, gram.at[rows_at(me, d, piece.shape[0]), :]))
    for d, piece in other_in:
        at = rows_at(me, d, piece.shape[0])
        first.append(copies.start(piece.at[:, pl.ds(0, window)], gram.at[at, others_at]))
    first += packed_copies(copies, me, sum_in, packed)
    for d, piece in basis_in:
        at = rows_at(me, d, piece.shape[0])
        second.append(copies.start(piece.at[:, pl.ds(0, width)], basis.at[at, :]))
    for d, piece in other_in:
        at = rows_at(me, d, piece.shape[0])
        second.append(copies.start(piece.at[:, pl.ds(window, width)], basis.at[at, :]))
    wait(first)
    if other_in:
        fill_halves(gram, half)
    new_gram(gram, packed, gh, gl)
    rows_own[...] = own_rows(gram, me, rows_own.shape[0])
    out = [copies.start(gh, gh_ref), copies.start(gl, gl_ref), copies.start(rows_own, rows_ref)]
    wait(second)
    image(z, gh, gl, basis)
    chain = Chain(z, w, q_ref)
    chain.cross()
    run_chains([chain])
    wait(out)


def any_specs(count):
    return [pl.BlockSpec(memory_space=pltpu.SMEM)] + [pl.BlockSpec(memory_space=pl.ANY)] * count


def chain_scratch(width, rows):
    return [pltpu.VMEM((width + rows, width), jnp.float32), pltpu.VMEM((LANES, LANES), jnp.float32)]


def head(me, count, grams, bases, others, sums, width):
    args = [p for group in (grams, bases, others, sums) for _, p in group]
    rows, size = grams[0][1].shape
    f32, bf16 = jnp.float32, jnp.bfloat16
    return pl.pallas_call(
        functools.partial(head_kernel, count, *[[d for d, _ in group] for group in (grams, others, sums)]),
        out_shape=[
            jax.ShapeDtypeStruct((rows, size), f32),
            jax.ShapeDtypeStruct((size, size), bf16),
            jax.ShapeDtypeStruct((size, size), bf16),
            jax.ShapeDtypeStruct((size, width), f32),
        ],
        in_specs=any_specs(len(args)),
        out_specs=[pl.BlockSpec(memory_space=pl.ANY)] * 3 + [pl.BlockSpec(memory_space=pltpu.VMEM)],
        scratch_shapes=[
            pltpu.VMEM((size, size), f32),
            pltpu.VMEM((size, offsets(size) * LANES), bf16),
            pltpu.VMEM((size, width), f32),
            pltpu.VMEM((size, size), bf16),
            pltpu.VMEM((size, size), bf16),
            pltpu.VMEM((rows, size), f32),
            *chain_scratch(width, size),
            pltpu.SemaphoreType.DMA((len(args) + len(others) + 3,)),
        ],
        compiler_params=pltpu.CompilerParams(vmem_limit_bytes=VMEM_LIMIT),
    )(me, *args)


def rest_kernel(bases, others, lefts, sums, *refs):
    me_ref, refs = refs[0], list(refs[1:])
    gh_in, gl_in, q_in, grad_in, weight_in, moment_in, second_in = refs[:7]
    refs = refs[7:]
    basis_in, other_in, left_in, sum_in = take(refs, bases), take(refs, others), take(refs, lefts), take(refs, sums)
    weight_out, moment_out, second_out, right_rows, left_rows, gram_rows = refs[:6]
    (gh, gl, q_first, basis, qr, ql, gram_l, packed_l, basis_l, glh, gll, zr, wr, zl, wl) = refs[6:21]
    (grad, weight, moment, second, inner, turn, right_half, left_half, left_t, semaphores) = refs[21:]
    row, col = me_ref[0], me_ref[1]
    copies = Copies(semaphores)
    first = q_first.shape[1]
    width = zr.shape[1]
    start = [copies.start(gh_in, gh), copies.start(gl_in, gl)]
    for d, piece in basis_in:
        at = rows_at(row, d, piece.shape[0])
        start.append(copies.start(piece.at[:, pl.ds(first, width)], basis.at[at, :]))
    for d, piece in other_in:
        start.append(copies.start(piece, basis.at[rows_at(row, d, piece.shape[0]), :]))
    project = [copies.start(q_in, q_first)]
    size = gram_l.shape[0]
    left_copies = []
    for ats, pieces in sum_in:
        rows = pieces.shape[0] // len(ats)
        for n, at in enumerate(ats):
            piece = pieces.at[pl.ds(n * rows, rows), :]
            left_copies.append(copies.start(piece, packed_l.at[rows_at(me_ref[2], at, rows), :]))
    rows = left_rows.shape[0]
    for ats, pieces in left_in:
        for n, at in enumerate(ats):
            for i, ref in enumerate((gram_l, basis_l)):
                piece = pieces.at[pl.ds(n * rows, rows), pl.ds(i * size, size)]
                left_copies.append(copies.start(piece, ref.at[rows_at(col, at, rows), :]))
    tail = [copies.start(grad_in, grad), copies.start(moment_in, moment)]
    late = [copies.start(second_in, second), copies.start(weight_in, weight)]

    wait(start)
    image(zr, gh, gl, basis)
    wait(project)
    qh, qo = split(q_first[...])
    xh, xl = split(zr[width:, :])
    sh, sl = split(product(qh, qo, xh, xl, ((0,), (0,))))
    zr[width:, :] -= product(qh, qo, sh, sl, ((1,), (0,)))
    wait(left_copies)
    new_gram(gram_l, packed_l, glh, gll)
    gram_rows[...] = own_rows(gram_l, col, gram_rows.shape[0])
    image(zl, glh, gll, basis_l)
    right, left = Chain(zr, wr, qr), Chain(zl, wl, ql)
    right.cross()
    left.cross()
    right_half[:, :first] = q_first[...].astype(jnp.bfloat16)
    wait(tail)
    for i in range(grad.shape[0] // LANES):
        moment[block(i), :] = FIRST_DECAY * moment[block(i), :] + (1.0 - FIRST_DECAY) * grad[block(i), :].astype(
            jnp.float32
        )
    out = [copies.start(moment, moment_out)]
    run_chains([left, right] if left.blocks <= right.blocks else [right, left])
    left_half[...] = ql[...].astype(jnp.bfloat16)
    right_half[:, first:] = qr[...].astype(jnp.bfloat16)
    right_rows[:, :first] = own_rows(q_first, row, right_rows.shape[0])
    right_rows[:, first:] = own_rows(qr, row, right_rows.shape[0])
    left_rows[...] = own_rows(ql, col, left_rows.shape[0])

    rows, columns = grad.shape
    tiles = [pl.ds(at, min(TILE, columns - at)) for at in range(0, columns, TILE)]
    left_t[...] = left_half[...].T
    for tile in tiles:
        inner[:rows, tile] = mm(left_t[...], grad[:, tile], ((1,), (0,))).astype(jnp.bfloat16)
        half = moment[:, tile].astype(jnp.bfloat16)
        inner[rows:, tile] = mm(left_t[...], half, ((1,), (0,))).astype(jnp.bfloat16)
    wait(late)
    for tile in tiles:
        rotated = mm(inner[...], right_half[:, tile], ((1,), (0,)))
        rotated_grad, rotated_moment = rotated[:rows, :], rotated[rows:, :]
        new_second = SECOND_DECAY * second[:, tile] + (1.0 - SECOND_DECAY) * rotated_grad * rotated_grad
        second[:, tile] = new_second
        out.append(copies.start(second.at[:, tile], second_out.at[:, tile]))
        turn[:, tile] = (rotated_moment / (jnp.sqrt(new_second) + EPSILON)).astype(jnp.bfloat16)
    turned = mm(left_half[...], turn[...], ((1,), (0,))).astype(jnp.bfloat16)
    for tile in tiles:
        update = mm(turned, right_half[tile, :], ((1,), (1,)))
        old = weight[:, tile]
        weight[:, tile] = old - STEP_SIZE * (update + WEIGHT_DECAY * old)
        out.append(copies.start(weight.at[:, tile], weight_out.at[:, tile]))
    wait(out)


def rest(me, gh, gl, q_first, tiles, bases, others, lefts, sums):
    args = [gh, gl, q_first, *tiles] + [p for _, p in bases + others + lefts + sums]
    rows_r, size_r = bases[0][1].shape
    width = size_r - q_first.shape[1]
    rows_l, size_l = lefts[0][1].shape[0], lefts[0][1].shape[1] // 2
    tile = tiles[0].shape
    f32, bf16 = jnp.float32, jnp.bfloat16
    vmem, anywhere = pl.BlockSpec(memory_space=pltpu.VMEM), pl.BlockSpec(memory_space=pl.ANY)
    return pl.pallas_call(
        functools.partial(rest_kernel, *[[d for d, _ in group] for group in (bases, others, lefts, sums)]),
        out_shape=[
            jax.ShapeDtypeStruct(tile, f32),
            jax.ShapeDtypeStruct(tile, f32),
            jax.ShapeDtypeStruct(tile, f32),
            jax.ShapeDtypeStruct((rows_r, size_r), f32),
            jax.ShapeDtypeStruct((rows_l, size_l), f32),
            jax.ShapeDtypeStruct((rows_l, size_l), f32),
        ],
        in_specs=any_specs(len(args)),
        out_specs=[anywhere] * 3 + [vmem] * 3,
        scratch_shapes=[
            pltpu.VMEM((size_r, size_r), bf16),
            pltpu.VMEM((size_r, size_r), bf16),
            pltpu.VMEM((size_r, size_r - width), f32),
            pltpu.VMEM((size_r, width), f32),
            pltpu.VMEM((size_r, width), f32),
            pltpu.VMEM((size_l, size_l), f32),
            pltpu.VMEM((size_l, size_l), f32),
            pltpu.VMEM((size_l, offsets(size_l) * LANES), bf16),
            pltpu.VMEM((size_l, size_l), f32),
            pltpu.VMEM((size_l, size_l), bf16),
            pltpu.VMEM((size_l, size_l), bf16),
            *chain_scratch(width, size_r),
            *chain_scratch(size_l, size_l),
            pltpu.VMEM(tile, bf16),
            pltpu.VMEM(tile, f32),
            pltpu.VMEM(tile, f32),
            pltpu.VMEM(tile, f32),
            pltpu.VMEM((2 * tile[0], tile[1]), bf16),
            pltpu.VMEM(tile, bf16),
            pltpu.VMEM((size_r, size_r), bf16),
            pltpu.VMEM((size_l, size_l), bf16),
            pltpu.VMEM((size_l, size_l), bf16),
            pltpu.SemaphoreType.DMA((len(args) + 1 + 3 * (size_l // rows_l) + 2 * -(-tile[1] // TILE),)),
        ],
        compiler_params=pltpu.CompilerParams(vmem_limit_bytes=VMEM_LIMIT),
    )(me, *args)


def swap(x, axis, distance):
    count = lax.axis_size(axis)
    return lax.ppermute(x, axis, [(i, i ^ distance) for i in range(count)])


def distances(axis):
    count = lax.axis_size(axis)
    return [1 << b for b in range(count.bit_length() - 1)]


def spread(held, axis, steps):
    for distance in steps:
        held = held + [(at ^ distance, swap(piece, axis, distance)) for at, piece in held]
    return held


def parts(x, axis, distance):
    rows = x.shape[0] // 2
    own = lax.rem(lax.div(lax.axis_index(axis), distance), 2)
    return (lax.dynamic_slice_in_dim(x, at * rows, rows, 0) for at in (own, 1 - own))


def gather_stacked(x, axis):
    held = [([0], x)]
    for distance in reversed(distances(axis)):
        sent = jnp.concatenate([piece for _, piece in held]) if len(held) > 1 else x
        held.append(([at ^ distance for ats, _ in held for at in ats], swap(sent, axis, distance)))
    return held


def sum_stacked(x, axis):
    kind, steps = x.dtype, distances(axis)
    weights = [1 << n for n in reversed(range(len(steps) - 1))]
    index = 0
    for distance, weight in zip(steps, weights):
        keep, other = parts(x, axis, distance)
        index = index + weight * lax.rem(lax.div(lax.axis_index(axis), distance), 2)
        x = (keep.astype(jnp.float32) + swap(other, axis, distance).astype(jnp.float32)).astype(kind)
    if steps:
        x = (x.astype(jnp.float32) + swap(x, axis, steps[-1]).astype(jnp.float32)).astype(kind)
    held = [([0], x)]
    for distance, weight in reversed(list(zip(steps, weights))):
        sent = jnp.concatenate([piece for _, piece in held]) if len(held) > 1 else x
        held.append(([at ^ weight for ats, _ in held for at in ats], swap(sent, axis, distance)))
    return jnp.int32(index), held


def sum_halves(x, axis, after):
    kind = x.dtype
    if lax.axis_size(axis) == 1:
        return x, [(0, x)]
    keep, other = parts(x, axis, 1)
    total = keep.astype(jnp.float32) + swap(other, axis, 1).astype(jnp.float32)
    for distance in distances(axis)[1:]:
        total, _ = lax.optimization_barrier((total.astype(kind), after))
        total = total.astype(jnp.float32) + swap(total, axis, distance).astype(jnp.float32)
    total = total.astype(kind)
    return total, [(0, total), (1, swap(total, axis, 1))]


def gather_right(gram, basis, width):
    count = lax.axis_size("row")
    grams, bases = [(0, gram)], [(0, basis)]
    if count == 1:
        return grams, bases, [], gram
    window = half_window(gram.shape[1])
    half = lax.div(2 * lax.axis_index("row"), count)
    mine = lax.dynamic_slice_in_dim(gram, half * (gram.shape[1] - window), window, 1)
    mine = jnp.concatenate([mine, basis[:, :width]], axis=1)
    others = [(count // 2, swap(mine, "row", count // 2))]
    near = distances("row")[-2::-1]
    return spread(grams, "row", near), spread(bases, "row", near), spread(others, "row", near), mine


def body(grad, weight, moment, second, gram_left, basis_left, gram_right, basis_right):
    block_left, block_right = grad.shape
    first = max(block_right - block_left, LANES)
    count = lax.axis_size("row")
    grams, bases, others, mine = gather_right(gram_right[0], basis_right[0], first)
    both, grad_after, _ = lax.optimization_barrier(((gram_left[0], basis_left[0]), grad, mine))
    terms_right, terms_left = terms(
        grad_after, 1.0 / (block_right * lax.axis_size("col")), 1.0 / (block_left * count)
    )
    arrived = others[0][1] if others else mine
    sent, sums_right = sum_halves(terms_right, "row", arrived)
    left = gather_stacked(jnp.concatenate(both, axis=1), "col")
    piece, sums_left = sum_stacked(terms_left, "col")
    me = jnp.stack([lax.axis_index("row"), lax.axis_index("col"), piece])
    last, _ = lax.optimization_barrier((basis_right[0][:, first:], sent))
    last = [(d, swap(last, "row", d)) for d in range(count // 2, count)] if count > 1 else []
    new_gram_right, gh, gl, q_first = head(me, count, grams, bases, others, sums_right, first)
    new_weight, new_moment, new_second, basis_rows_right, basis_rows_left, new_gram_left = rest(
        me, gh, gl, q_first, (grad, weight, moment, second), bases, last, left, sums_left
    )
    return (
        new_weight,
        new_moment,
        new_second,
        new_gram_left[None],
        basis_rows_left[None],
        new_gram_right[None],
        basis_rows_right[None],
    )


def solution(mesh):
    specs = (
        P("row", "col"),
        P("row", "col"),
        P("row", "col"),
        P("row", "col"),
        P("row", "col", None),
        P("row", "col", None),
        P("col", "row", None),
        P("col", "row", None),
    )
    out_specs = specs[:3] + specs[4:]
    return jax.shard_map(body, mesh=mesh, in_specs=specs, out_specs=out_specs, check_vma=False)
```

```python
import functools
from itertools import zip_longest
import jax
import jax.numpy as jnp
from jax import lax
from jax.experimental import pallas as pl
from jax.experimental.pallas import tpu as pltpu
from jax.sharding import PartitionSpec as P

STAT_DECAY = 0.95
FIRST_DECAY = 0.9
SECOND_DECAY = 0.95
EPSILON = 1e-08
STEP_SIZE = 0.02
WEIGHT_DECAY = 0.01
LANES = 128
ROWS = 8
TILE = 256
VMEM_LIMIT = 56 * 2**20


def sub_row(x, k):
    return jnp.broadcast_to(x[k : k + 1, :], (ROWS, LANES))


def lane_col(x, c):
    return jnp.broadcast_to(x[:, c : c + 1], (ROWS, LANES))


def reciprocal(p):
    guess = pl.reciprocal(p, approx=True)
    return guess * (2.0 - p * guess)


def inverse_factor(rows):
    count = LANES // ROWS
    rows = list(rows)
    subs = lax.broadcasted_iota(jnp.int32, (ROWS, LANES), 0)
    lanes = lax.broadcasted_iota(jnp.int32, (ROWS, LANES), 1)
    out = []
    for s in range(count):
        base = s * ROWS
        pivot = rows[s]
        here = (lanes >= base) & (lanes < base + ROWS)
        cols = [lane_col(pivot, base + k) for k in range(ROWS)]
        full = jnp.where(here, (lanes == subs + base).astype(jnp.float32), pivot)
        forward = full
        pivots = jnp.ones((ROWS, LANES), jnp.float32)
        yield
        for j in range(0, ROWS, 2):
            a, b, d = sub_row(cols[j], j), sub_row(cols[j], j + 1), sub_row(cols[j + 1], j + 1)
            det = a * d - b * b
            inv = reciprocal(det)
            pair = (subs == j) | (subs == j + 1)
            one = jnp.where(pair, jnp.where(subs == j, -1.0, 0.0), cols[j])
            two = jnp.where(pair, jnp.where(subs == j, 0.0, -1.0), cols[j + 1])
            for k in range(j + 2, min(j + 4, ROWS)):
                x, y = sub_row(cols[k], j), sub_row(cols[k], j + 1)
                change = one * (d * x - b * y) + two * (a * y - b * x)
                cols[k] = jnp.where(pair, 0.0, cols[k]) - change * inv
            yield
            one, two = (one * d - two * b) * inv, (two * a - one * b) * inv
            for k in range(j + 4, ROWS):
                x, y = sub_row(cols[k], j), sub_row(cols[k], j + 1)
                cols[k] = jnp.where(pair, 0.0, cols[k]) - (one * x + two * y)
            full = jnp.where(pair, 0.0, full) - (one * sub_row(full, j) + two * sub_row(full, j + 1))
            inner = b * reciprocal(a)
            below = subs > j + 1
            lower = jnp.where(below, one, jnp.where(subs == j + 1, inner, 0.0))
            change = lower * sub_row(forward, j)
            if j + 2 < ROWS:
                change = change + jnp.where(below, two, 0.0) * sub_row(forward, j + 1)
            forward = forward - change
            pivots = jnp.where(subs == j, a, jnp.where(subs == j + 1, d - inner * b, pivots))
            yield
        out.append(jnp.where(lanes < base + ROWS, forward * lax.rsqrt(pivots), 0.0))
        if s < count - 1:
            spread = [sub_row(full, k) for k in range(ROWS)]
            for i in range(s + 1, count):
                coeffs = [lane_col(rows[i], base + k) for k in range(ROWS)]
                terms = [coeffs[k] * spread[k] for k in range(ROWS)]
                while len(terms) > 1:
                    terms = [a + b for a, b in zip(terms[::2], terms[1::2])]
                rows[i] = jnp.where(here, 0.0, rows[i]) - terms[0]
                yield
    return out


def in_turns(generators, fills):
    results = [None] * len(generators)
    live = list(enumerate(generators))
    fills = list(fills)
    total, turn, done = 250, 0, 0
    while live:
        for at, generator in list(live):
            try:
                next(generator)
            except StopIteration as stop:
                results[at] = stop.value
                live.remove((at, generator))
        turn += 1
        while done < len(fills) and done * total <= turn * len(fills):
            fills[done]()
            done += 1
    for fill in fills[done:]:
        fill()
    return results


def split(x):
    hi = x.astype(jnp.bfloat16)
    return hi, (x - hi.astype(jnp.float32)).astype(jnp.bfloat16)


def stack_left(x, axis):
    hi, lo = split(x)
    return jnp.concatenate([hi, hi, lo], axis=axis)


def stack_right(x, axis):
    hi, lo = split(x)
    return jnp.concatenate([hi, lo, hi], axis=axis)


def mm(a, b, dims):
    return lax.dot_general(a, b, (dims, ((), ())), preferred_element_type=jnp.float32)


def mm_nn(a, b):
    return mm(stack_left(a, 1), stack_right(b, 0), ((1,), (0,)))


def mm_nt(a, b):
    return mm(stack_left(a, 1), stack_right(b, 1), ((1,), (1,)))


def product(ah, al, bh, bl, dims):
    return mm(ah, bh, dims) + (mm(ah, bl, dims) + mm(al, bh, dims))


def block(i):
    return pl.ds(i * LANES, LANES) if isinstance(i, int) else pl.ds(pl.multiple_of(i * LANES, LANES), LANES)


class Chain:
    def __init__(self, z_ref, w_ref, q_ref):
        self.z, self.w, self.q = z_ref, w_ref, q_ref
        self.width = z_ref.shape[1]
        self.blocks = self.width // LANES

    def cross(self):
        hi, lo = split(self.z[self.width :, :])
        dims = ((0,), (0,))
        self.z[: self.width, :] = product(hi, lo, hi, lo, dims)
        self.w[...] = jnp.zeros_like(self.w)

    def look(self, j):
        self.before = block(lax.max(j - 1, 0))
        self.w_nt = stack_right(self.w[...], 1)
        at = block(j)
        low = mm(stack_left(self.z[at, self.before], 1), self.w_nt, ((1,), (1,)))
        diagonal = self.z[at, at] - mm_nt(low, low)
        return [diagonal[i * ROWS : (i + 1) * ROWS, :] for i in range(LANES // ROWS)]

    def fills(self):
        def rows_of_u():
            self.u = stack_right(mm_nn(self.w[...], self.z[self.before, :]), 0)

        def panel():
            p = mm(stack_left(self.z[:, self.before], 1), self.w_nt, ((1,), (1,)))
            self.q[:, self.before] = p[self.width :, :]
            self.p = stack_left(p, 1)

        def columns(at):
            stop = min(at + TILE, self.width)
            self.z[:, at:stop] -= mm(self.p, self.u[:, at:stop], ((1,), (0,)))

        return [rows_of_u, panel] + [functools.partial(columns, at) for at in range(0, self.width, TILE)]

    def store(self, out):
        for i, row in enumerate(out):
            self.w[i * ROWS : (i + 1) * ROWS, :] = row

    def finish(self):
        last = block(self.blocks - 1)
        self.q[:, last] = mm_nt(self.z[self.width :, last], self.w[...])


def run_chains(chains):
    def step_of(members):
        def step(j, carry):
            rows = [chain.look(j) for chain in members]
            fills = [fill for several in zip_longest(*[chain.fills() for chain in members]) for fill in several if fill]
            for chain, out in zip(members, in_turns([inverse_factor(r) for r in rows], fills)):
                chain.store(out)
            return carry

        return step

    start = 0
    for end in sorted({chain.blocks for chain in chains}):
        lax.fori_loop(start, end, step_of([chain for chain in chains if chain.blocks >= end]), 0)
        start = end
    for chain in chains:
        chain.finish()


class Copies:
    def __init__(self, semaphores):
        self.semaphores, self.used = semaphores, 0

    def start(self, source, target):
        copy = pltpu.make_async_copy(source, target, self.semaphores.at[self.used])
        self.used += 1
        copy.start()
        return copy


def wait(copies):
    for copy in copies:
        copy.wait()


def offsets(size):
    return size // LANES // 2 + 1


def pack_products(cols, out_ref, dims, scale):
    blocks = len(cols)
    for i in range(blocks):
        for o in range(offsets(blocks * LANES)):
            term = mm(cols[i], cols[(i + o) % blocks], dims)
            out_ref[block(i), block(o)] = (term * scale).astype(out_ref.dtype)


def terms_kernel(scale_left, scale_right, grad_ref, *refs):
    right_refs, left_refs, (right, left, semaphores) = refs[:2], refs[2:4], refs[4:]
    rows, columns = grad_ref.shape
    copies = Copies(semaphores)
    pack_products([grad_ref[:, block(i)] for i in range(columns // LANES)], right, ((0,), (0,)), scale_right)
    out = []
    for axis, packed, targets in (("row", right, right_refs), ("col", left, left_refs)):
        if axis == "col":
            pack_products([grad_ref[block(i), :] for i in range(rows // LANES)], left, ((1,), (1,)), scale_left)
        own = lax.rem(lax.axis_index(axis), 2)
        size = packed.shape[0] // 2
        for side, target in zip((own, 1 - own), targets):
            at = pl.ds(pl.multiple_of(side * size, 2 * ROWS), size)
            out.append(copies.start(packed.at[at, :], target))
    wait(out)


def terms(grad, scale_left, scale_right):
    rows, columns = grad.shape
    right, left = (columns, offsets(columns) * LANES), (rows, offsets(rows) * LANES)
    return pl.pallas_call(
        functools.partial(terms_kernel, scale_left, scale_right),
        out_shape=[
            jax.ShapeDtypeStruct((shape[0] // 2, shape[1]), jnp.bfloat16) for shape in (right, right, left, left)
        ],
        out_specs=any_specs(4),
        scratch_shapes=[
            pltpu.VMEM(right, jnp.bfloat16),
            pltpu.VMEM(left, jnp.bfloat16),
            pltpu.SemaphoreType.DMA((4,)),
        ],
        compiler_params=pltpu.CompilerParams(vmem_limit_bytes=VMEM_LIMIT),
    )(grad)


def pack_kernel(count, width, gram, basis, gram_left, basis_left, right_ref, left_ref, semaphores):
    copies = Copies(semaphores)
    window = half_window(gram.shape[1])
    half = lax.div(2 * lax.axis_index("row"), count)
    at = pl.ds(pl.multiple_of(half * (gram.shape[1] - window), LANES), window)
    size = gram_left.shape[1]
    wait(
        [
            copies.start(gram.at[:, at], right_ref.at[:, pl.ds(0, window)]),
            copies.start(basis.at[:, pl.ds(0, width)], right_ref.at[:, pl.ds(window, width)]),
            copies.start(gram_left, left_ref.at[:, pl.ds(0, size)]),
            copies.start(basis_left, left_ref.at[:, pl.ds(size, size)]),
        ]
    )


def pack(count, width, gram, basis, gram_left, basis_left):
    return pl.pallas_call(
        functools.partial(pack_kernel, count, width),
        out_shape=[
            jax.ShapeDtypeStruct((gram.shape[0], half_window(gram.shape[1]) + width), jnp.float32),
            jax.ShapeDtypeStruct((gram_left.shape[0], 2 * gram_left.shape[1]), jnp.float32),
        ],
        in_specs=any_specs(4),
        out_specs=any_specs(2),
        scratch_shapes=[pltpu.SemaphoreType.DMA((4,))],
        compiler_params=pltpu.CompilerParams(vmem_limit_bytes=VMEM_LIMIT),
    )(gram, basis, gram_left, basis_left)


def rows_at(me, distance, rows):
    return pl.ds(pl.multiple_of((me ^ distance) * rows, ROWS), rows)


def new_gram(gram_ref, packed_ref, gh_ref, gl_ref):
    blocks = gram_ref.shape[0] // LANES
    count = offsets(gram_ref.shape[0])

    def put(i, k, term):
        value = gram_ref[block(i), block(k)] * STAT_DECAY + term
        gram_ref[block(i), block(k)] = value
        gh_ref[block(i), block(k)], gl_ref[block(i), block(k)] = split(value)

    for i in range(blocks):
        for o in range(count):
            k = (i + o) % blocks
            term = packed_ref[block(i), block(o)].astype(jnp.float32) * (1.0 - STAT_DECAY)
            put(i, k, term)
            if o > 0 and not (blocks % 2 == 0 and o == count - 1):
                put(k, i, term.T)


def image(z_ref, gh_ref, gl_ref, basis_ref):
    width = z_ref.shape[1]
    for at in range(0, width, TILE):
        stop = min(at + TILE, width)
        bh, bl = split(basis_ref[:, at:stop])
        z_ref[width:, at:stop] = product(gh_ref[...], gl_ref[...], bh, bl, ((1,), (0,)))


def own_rows(ref, me, rows):
    return ref[pl.ds(pl.multiple_of(me * rows, ROWS), rows), :]


def half_window(size):
    return -(-size // 2 // LANES) * LANES


def fill_halves(gram, half):
    size = gram.shape[0]
    window = half_window(size)
    rest = size - window
    near = half * window
    far = pl.ds(pl.multiple_of((1 - half) * rest, LANES), window)
    for i in range(rest // LANES):
        at = pl.ds(pl.multiple_of(near + i * LANES, LANES), LANES)
        gram[far, at] = gram[at, far].T


def packed_copies(copies, me, sums, packed):
    side = lax.rem(me, 2) if len(sums) > 1 else 0
    return [copies.start(piece, packed.at[rows_at(side, d, piece.shape[0]), :]) for d, piece in sums]


def take(refs, distances_of):
    return [(d, refs.pop(0)) for d in distances_of]


def head_kernel(count, owns, others, sums, *refs):
    refs = list(refs)
    gram_in, basis_in, other_in, sum_in = take(refs, owns), take(refs, owns), take(refs, others), take(refs, sums)
    rows_ref, gh_ref, gl_ref, q_ref, gram, packed, basis, gh, gl, rows_own, z, w, semaphores = refs
    me = lax.axis_index("row")
    copies = Copies(semaphores)
    width = basis.shape[1]
    half = lax.div(2 * me, count)
    window = half_window(gram.shape[0])
    others_at = pl.ds(pl.multiple_of((1 - half) * (gram.shape[0] - window), LANES), window)
    first, second = [], []
    for d, piece in gram_in:
        first.append(copies.start(piece, gram.at[rows_at(me, d, piece.shape[0]), :]))
    for d, piece in other_in:
        at = rows_at(me, d, piece.shape[0])
        first.append(copies.start(piece.at[:, pl.ds(0, window)], gram.at[at, others_at]))
    first += packed_copies(copies, me, sum_in, packed)
    for d, piece in basis_in:
        at = rows_at(me, d, piece.shape[0])
        second.append(copies.start(piece.at[:, pl.ds(0, width)], basis.at[at, :]))
    for d, piece in other_in:
        at = rows_at(me, d, piece.shape[0])
        second.append(copies.start(piece.at[:, pl.ds(window, width)], basis.at[at, :]))
    wait(first)
    if other_in:
        fill_halves(gram, half)
    new_gram(gram, packed, gh, gl)
    rows_own[...] = own_rows(gram, me, rows_own.shape[0])
    out = [copies.start(gh, gh_ref), copies.start(gl, gl_ref), copies.start(rows_own, rows_ref)]
    wait(second)
    image(z, gh, gl, basis)
    chain = Chain(z, w, q_ref)
    chain.cross()
    run_chains([chain])
    wait(out)


def any_specs(count):
    return [pl.BlockSpec(memory_space=pl.ANY)] * count


def chain_scratch(width, rows):
    return [pltpu.VMEM((width + rows, width), jnp.float32), pltpu.VMEM((LANES, LANES), jnp.float32)]


def head(count, grams, bases, others, sums, width):
    args = [p for group in (grams, bases, others, sums) for _, p in group]
    rows, size = grams[0][1].shape
    f32, bf16 = jnp.float32, jnp.bfloat16
    return pl.pallas_call(
        functools.partial(head_kernel, count, *[[d for d, _ in group] for group in (grams, others, sums)]),
        out_shape=[
            jax.ShapeDtypeStruct((rows, size), f32),
            jax.ShapeDtypeStruct((size, size), bf16),
            jax.ShapeDtypeStruct((size, size), bf16),
            jax.ShapeDtypeStruct((size, width), f32),
        ],
        in_specs=any_specs(len(args)),
        out_specs=[pl.BlockSpec(memory_space=pl.ANY)] * 3 + [pl.BlockSpec(memory_space=pltpu.VMEM)],
        scratch_shapes=[
            pltpu.VMEM((size, size), f32),
            pltpu.VMEM((size, offsets(size) * LANES), bf16),
            pltpu.VMEM((size, width), f32),
            pltpu.VMEM((size, size), bf16),
            pltpu.VMEM((size, size), bf16),
            pltpu.VMEM((rows, size), f32),
            *chain_scratch(width, size),
            pltpu.SemaphoreType.DMA((len(args) + len(others) + 3,)),
        ],
        compiler_params=pltpu.CompilerParams(vmem_limit_bytes=VMEM_LIMIT),
    )(*args)


def rest_kernel(bases, others, lefts, sums, *refs):
    refs = list(refs)
    gh_in, gl_in, q_in, grad_in, weight_in, moment_in, second_in = refs[:7]
    refs = refs[7:]
    basis_in, other_in, left_in, sum_in = take(refs, bases), take(refs, others), take(refs, lefts), take(refs, sums)
    weight_out, moment_out, second_out, right_rows, left_rows, gram_rows = refs[:6]
    (gh, gl, q_first, basis, qr, ql, gram_l, packed_l, basis_l, glh, gll, zr, wr, zl, wl) = refs[6:21]
    (grad, weight, moment, second, inner, turn, right_half, left_half, left_t, semaphores) = refs[21:]
    row, col = lax.axis_index("row"), lax.axis_index("col")
    copies = Copies(semaphores)
    first = q_first.shape[1]
    width = zr.shape[1]
    start = [copies.start(gh_in, gh), copies.start(gl_in, gl)]
    for d, piece in basis_in:
        at = rows_at(row, d, piece.shape[0])
        start.append(copies.start(piece.at[:, pl.ds(first, width)], basis.at[at, :]))
    for d, piece in other_in:
        start.append(copies.start(piece, basis.at[rows_at(row, d, piece.shape[0]), :]))
    project = [copies.start(q_in, q_first)]
    size = gram_l.shape[0]
    left_copies = []
    for ats, pieces in sum_in:
        rows = pieces.shape[0] // len(ats)
        for n, at in enumerate(ats):
            piece = pieces.at[pl.ds(n * rows, rows), :]
            left_copies.append(copies.start(piece, packed_l.at[rows_at(piece_index("col"), at, rows), :]))
    rows = left_rows.shape[0]
    for ats, pieces in left_in:
        for n, at in enumerate(ats):
            for i, ref in enumerate((gram_l, basis_l)):
                piece = pieces.at[pl.ds(n * rows, rows), pl.ds(i * size, size)]
                left_copies.append(copies.start(piece, ref.at[rows_at(col, at, rows), :]))
    tail = [copies.start(grad_in, grad), copies.start(moment_in, moment)]
    late = [copies.start(second_in, second), copies.start(weight_in, weight)]

    wait(start)
    image(zr, gh, gl, basis)
    wait(project)
    qh, qo = split(q_first[...])
    xh, xl = split(zr[width:, :])
    sh, sl = split(product(qh, qo, xh, xl, ((0,), (0,))))
    zr[width:, :] -= product(qh, qo, sh, sl, ((1,), (0,)))
    wait(left_copies)
    new_gram(gram_l, packed_l, glh, gll)
    gram_rows[...] = own_rows(gram_l, col, gram_rows.shape[0])
    image(zl, glh, gll, basis_l)
    right, left = Chain(zr, wr, qr), Chain(zl, wl, ql)
    right.cross()
    left.cross()
    right_half[:, :first] = q_first[...].astype(jnp.bfloat16)
    wait(tail)
    for i in range(grad.shape[0] // LANES):
        moment[block(i), :] = FIRST_DECAY * moment[block(i), :] + (1.0 - FIRST_DECAY) * grad[block(i), :].astype(
            jnp.float32
        )
    out = [copies.start(moment, moment_out)]
    run_chains([left, right] if left.blocks <= right.blocks else [right, left])
    left_half[...] = ql[...].astype(jnp.bfloat16)
    right_half[:, first:] = qr[...].astype(jnp.bfloat16)
    right_rows[:, :first] = own_rows(q_first, row, right_rows.shape[0])
    right_rows[:, first:] = own_rows(qr, row, right_rows.shape[0])
    left_rows[...] = own_rows(ql, col, left_rows.shape[0])

    rows, columns = grad.shape
    tiles = [pl.ds(at, min(TILE, columns - at)) for at in range(0, columns, TILE)]
    left_t[...] = left_half[...].T
    for tile in tiles:
        inner[:rows, tile] = mm(left_t[...], grad[:, tile], ((1,), (0,))).astype(jnp.bfloat16)
        half = moment[:, tile].astype(jnp.bfloat16)
        inner[rows:, tile] = mm(left_t[...], half, ((1,), (0,))).astype(jnp.bfloat16)
    wait(late)
    for tile in tiles:
        rotated = mm(inner[...], right_half[:, tile], ((1,), (0,)))
        rotated_grad, rotated_moment = rotated[:rows, :], rotated[rows:, :]
        new_second = SECOND_DECAY * second[:, tile] + (1.0 - SECOND_DECAY) * rotated_grad * rotated_grad
        second[:, tile] = new_second
        out.append(copies.start(second.at[:, tile], second_out.at[:, tile]))
        turn[:, tile] = (rotated_moment / (jnp.sqrt(new_second) + EPSILON)).astype(jnp.bfloat16)
    turned = mm(left_half[...], turn[...], ((1,), (0,))).astype(jnp.bfloat16)
    for tile in tiles:
        update = mm(turned, right_half[tile, :], ((1,), (1,)))
        old = weight[:, tile]
        weight[:, tile] = old - STEP_SIZE * (update + WEIGHT_DECAY * old)
        out.append(copies.start(weight.at[:, tile], weight_out.at[:, tile]))
    wait(out)


def rest(gh, gl, q_first, tiles, bases, others, lefts, sums):
    args = [gh, gl, q_first, *tiles] + [p for _, p in bases + others + lefts + sums]
    rows_r, size_r = bases[0][1].shape
    width = size_r - q_first.shape[1]
    rows_l, size_l = lefts[0][1].shape[0], lefts[0][1].shape[1] // 2
    tile = tiles[0].shape
    f32, bf16 = jnp.float32, jnp.bfloat16
    vmem, anywhere = pl.BlockSpec(memory_space=pltpu.VMEM), pl.BlockSpec(memory_space=pl.ANY)
    return pl.pallas_call(
        functools.partial(rest_kernel, *[[d for d, _ in group] for group in (bases, others, lefts, sums)]),
        out_shape=[
            jax.ShapeDtypeStruct(tile, f32),
            jax.ShapeDtypeStruct(tile, f32),
            jax.ShapeDtypeStruct(tile, f32),
            jax.ShapeDtypeStruct((rows_r, size_r), f32),
            jax.ShapeDtypeStruct((rows_l, size_l), f32),
            jax.ShapeDtypeStruct((rows_l, size_l), f32),
        ],
        in_specs=any_specs(len(args)),
        out_specs=[anywhere] * 3 + [vmem] * 3,
        scratch_shapes=[
            pltpu.VMEM((size_r, size_r), bf16),
            pltpu.VMEM((size_r, size_r), bf16),
            pltpu.VMEM((size_r, size_r - width), f32),
            pltpu.VMEM((size_r, width), f32),
            pltpu.VMEM((size_r, width), f32),
            pltpu.VMEM((size_l, size_l), f32),
            pltpu.VMEM((size_l, size_l), f32),
            pltpu.VMEM((size_l, offsets(size_l) * LANES), bf16),
            pltpu.VMEM((size_l, size_l), f32),
            pltpu.VMEM((size_l, size_l), bf16),
            pltpu.VMEM((size_l, size_l), bf16),
            *chain_scratch(width, size_r),
            *chain_scratch(size_l, size_l),
            pltpu.VMEM(tile, bf16),
            pltpu.VMEM(tile, f32),
            pltpu.VMEM(tile, f32),
            pltpu.VMEM(tile, f32),
            pltpu.VMEM((2 * tile[0], tile[1]), bf16),
            pltpu.VMEM(tile, bf16),
            pltpu.VMEM((size_r, size_r), bf16),
            pltpu.VMEM((size_l, size_l), bf16),
            pltpu.VMEM((size_l, size_l), bf16),
            pltpu.SemaphoreType.DMA((len(args) + 1 + 3 * (size_l // rows_l) + 2 * -(-tile[1] // TILE),)),
        ],
        compiler_params=pltpu.CompilerParams(vmem_limit_bytes=VMEM_LIMIT),
    )(*args)


def swap(x, axis, distance):
    count = lax.axis_size(axis)
    return lax.ppermute(x, axis, [(i, i ^ distance) for i in range(count)])


def distances(axis):
    count = lax.axis_size(axis)
    return [1 << b for b in range(count.bit_length() - 1)]


def spread(held, axis, steps):
    for distance in steps:
        held = held + [(at ^ distance, swap(piece, axis, distance)) for at, piece in held]
    return held


def parts(x, axis, distance):
    rows = x.shape[0] // 2
    own = lax.rem(lax.div(lax.axis_index(axis), distance), 2)
    return tuple(lax.dynamic_slice_in_dim(x, at * rows, rows, 0) for at in (own, 1 - own))


def gather_stacked(x, axis):
    held = [([0], x)]
    for distance in reversed(distances(axis)):
        sent = jnp.concatenate([piece for _, piece in held]) if len(held) > 1 else x
        held.append(([at ^ distance for ats, _ in held for at in ats], swap(sent, axis, distance)))
    return held


def add(x, y):
    return (x.astype(jnp.float32) + y.astype(jnp.float32)).astype(x.dtype)


def piece_weights(axis):
    return [1 << n for n in reversed(range(len(distances(axis)) - 1))]


def piece_index(axis):
    me, index = lax.axis_index(axis), 0
    for distance, weight in zip(distances(axis), piece_weights(axis)):
        index = index + weight * lax.rem(lax.div(me, distance), 2)
    return index


def sum_stacked(keep, other, axis):
    steps, weights = distances(axis), piece_weights(axis)
    x = None
    for distance in steps[:-1]:
        if x is not None:
            keep, other = parts(x, axis, distance)
        x = add(keep, swap(other, axis, distance))
    x = add(x, swap(x, axis, steps[-1]))
    held = [([0], x)]
    for distance, weight in reversed(list(zip(steps, weights))):
        sent = jnp.concatenate([piece for _, piece in held]) if len(held) > 1 else x
        held.append(([at ^ weight for ats, _ in held for at in ats], swap(sent, axis, distance)))
    return held


def sum_halves(keep, other, axis, after):
    total, _ = lax.optimization_barrier((add(keep, swap(other, axis, 1)), after))
    for distance in distances(axis)[1:]:
        total = add(total, swap(total, axis, distance))
    return total, [(0, total), (1, swap(total, axis, 1))]


def body(grad, weight, moment, second, gram_left, basis_left, gram_right, basis_right):
    block_left, block_right = grad.shape
    first = max(block_right - block_left, LANES)
    count = lax.axis_size("row")
    gram_right, basis_right = gram_right[0], basis_right[0]
    window, left = pack(count, first, gram_right, basis_right, gram_left[0], basis_left[0])
    near = distances("row")[-2::-1]
    arrived = swap(window, "row", count // 2)
    gram_right, basis_right, _ = lax.optimization_barrier((gram_right, basis_right, arrived))
    grams, bases = spread([(0, gram_right)], "row", near), spread([(0, basis_right)], "row", near)
    others = spread([(count // 2, arrived)], "row", near)
    grad_after, left = lax.optimization_barrier((grad, left))
    keep_right, other_right, keep_left, other_left = terms(
        grad_after, 1.0 / (block_right * lax.axis_size("col")), 1.0 / (block_left * count)
    )
    left = gather_stacked(left, "col")
    sent, sums_right = sum_halves(keep_right, other_right, "row", arrived)
    sums_left = sum_stacked(keep_left, other_left, "col")
    last, _ = lax.optimization_barrier((basis_right[:, first:], sent))
    last = [(d, swap(last, "row", d)) for d in range(count // 2, count)]
    new_gram_right, gh, gl, q_first = head(count, grams, bases, others, sums_right, first)
    new_weight, new_moment, new_second, basis_rows_right, basis_rows_left, new_gram_left = rest(
        gh, gl, q_first, (grad, weight, moment, second), bases, last, left, sums_left
    )
    return (
        new_weight,
        new_moment,
        new_second,
        new_gram_left[None],
        basis_rows_left[None],
        new_gram_right[None],
        basis_rows_right[None],
    )


def solution(mesh):
    specs = (
        P("row", "col"),
        P("row", "col"),
        P("row", "col"),
        P("row", "col"),
        P("row", "col", None),
        P("row", "col", None),
        P("col", "row", None),
        P("col", "row", None),
    )
    out_specs = specs[:3] + specs[4:]
    return jax.shard_map(body, mesh=mesh, in_specs=specs, out_specs=out_specs, check_vma=False)
```

```python
import functools
from itertools import zip_longest
import jax
import jax.numpy as jnp
from jax import lax
from jax.experimental import pallas as pl
from jax.experimental.pallas import tpu as pltpu
from jax.sharding import PartitionSpec as P

STAT_DECAY = 0.95
FIRST_DECAY = 0.9
SECOND_DECAY = 0.95
EPSILON = 1e-08
STEP_SIZE = 0.02
WEIGHT_DECAY = 0.01
LANES = 128
ROWS = 8
TILE = 256
VMEM_LIMIT = 56 * 2**20


def sub_row(x, k):
    return jnp.broadcast_to(x[k : k + 1, :], (ROWS, LANES))


def lane_col(x, c):
    return jnp.broadcast_to(x[:, c : c + 1], (ROWS, LANES))


def reciprocal(p):
    guess = pl.reciprocal(p, approx=True)
    return guess * (2.0 - p * guess)


def inverse_factor(rows):
    count = LANES // ROWS
    rows = list(rows)
    subs = lax.broadcasted_iota(jnp.int32, (ROWS, LANES), 0)
    lanes = lax.broadcasted_iota(jnp.int32, (ROWS, LANES), 1)
    out = []
    for s in range(count):
        base = s * ROWS
        pivot = rows[s]
        here = (lanes >= base) & (lanes < base + ROWS)
        cols = [lane_col(pivot, base + k) for k in range(ROWS)]
        full = jnp.where(here, (lanes == subs + base).astype(jnp.float32), pivot)
        forward = full
        pivots = jnp.ones((ROWS, LANES), jnp.float32)
        yield
        for j in range(0, ROWS, 2):
            a, b, d = sub_row(cols[j], j), sub_row(cols[j], j + 1), sub_row(cols[j + 1], j + 1)
            det = a * d - b * b
            inv = reciprocal(det)
            pair = (subs == j) | (subs == j + 1)
            one = jnp.where(pair, jnp.where(subs == j, -1.0, 0.0), cols[j])
            two = jnp.where(pair, jnp.where(subs == j, 0.0, -1.0), cols[j + 1])
            for k in range(j + 2, min(j + 4, ROWS)):
                x, y = sub_row(cols[k], j), sub_row(cols[k], j + 1)
                change = one * (d * x - b * y) + two * (a * y - b * x)
                cols[k] = jnp.where(pair, 0.0, cols[k]) - change * inv
            yield
            one, two = (one * d - two * b) * inv, (two * a - one * b) * inv
            for k in range(j + 4, ROWS):
                x, y = sub_row(cols[k], j), sub_row(cols[k], j + 1)
                cols[k] = jnp.where(pair, 0.0, cols[k]) - (one * x + two * y)
            full = jnp.where(pair, 0.0, full) - (one * sub_row(full, j) + two * sub_row(full, j + 1))
            inner = b * reciprocal(a)
            below = subs > j + 1
            lower = jnp.where(below, one, jnp.where(subs == j + 1, inner, 0.0))
            change = lower * sub_row(forward, j)
            if j + 2 < ROWS:
                change = change + jnp.where(below, two, 0.0) * sub_row(forward, j + 1)
            forward = forward - change
            pivots = jnp.where(subs == j, a, jnp.where(subs == j + 1, d - inner * b, pivots))
            yield
        out.append(jnp.where(lanes < base + ROWS, forward * lax.rsqrt(pivots), 0.0))
        if s < count - 1:
            spread = [sub_row(full, k) for k in range(ROWS)]
            for i in range(s + 1, count):
                coeffs = [lane_col(rows[i], base + k) for k in range(ROWS)]
                terms = [coeffs[k] * spread[k] for k in range(ROWS)]
                while len(terms) > 1:
                    terms = [a + b for a, b in zip(terms[::2], terms[1::2])]
                rows[i] = jnp.where(here, 0.0, rows[i]) - terms[0]
                yield
    return out


def in_turns(generators, fills):
    results = [None] * len(generators)
    live = list(enumerate(generators))
    fills = list(fills)
    total, turn, done = 250, 0, 0
    while live:
        for at, generator in list(live):
            try:
                next(generator)
            except StopIteration as stop:
                results[at] = stop.value
                live.remove((at, generator))
        turn += 1
        while done < len(fills) and done * total <= turn * len(fills):
            fills[done]()
            done += 1
    for fill in fills[done:]:
        fill()
    return results


def split(x):
    hi = x.astype(jnp.bfloat16)
    return hi, (x - hi.astype(jnp.float32)).astype(jnp.bfloat16)


def stack_left(x, axis):
    hi, lo = split(x)
    return jnp.concatenate([hi, hi, lo], axis=axis)


def stack_right(x, axis):
    hi, lo = split(x)
    return jnp.concatenate([hi, lo, hi], axis=axis)


def mm(a, b, dims):
    return lax.dot_general(a, b, (dims, ((), ())), preferred_element_type=jnp.float32)


def mm_nn(a, b):
    return mm(stack_left(a, 1), stack_right(b, 0), ((1,), (0,)))


def mm_nt(a, b):
    return mm(stack_left(a, 1), stack_right(b, 1), ((1,), (1,)))


def product(ah, al, bh, bl, dims):
    return mm(ah, bh, dims) + (mm(ah, bl, dims) + mm(al, bh, dims))


def block(i):
    return pl.ds(i * LANES, LANES) if isinstance(i, int) else pl.ds(pl.multiple_of(i * LANES, LANES), LANES)


class Chain:
    def __init__(self, z_ref, w_ref, q_ref):
        self.z, self.w, self.q = z_ref, w_ref, q_ref
        self.width = z_ref.shape[1]
        self.blocks = self.width // LANES

    def cross(self):
        hi, lo = split(self.z[self.width :, :])
        dims = ((0,), (0,))
        self.z[: self.width, :] = product(hi, lo, hi, lo, dims)
        self.w[...] = jnp.zeros_like(self.w)

    def look(self, j):
        self.before = block(lax.max(j - 1, 0))
        self.w_nt = stack_right(self.w[...], 1)
        at = block(j)
        low = mm(stack_left(self.z[at, self.before], 1), self.w_nt, ((1,), (1,)))
        diagonal = self.z[at, at] - mm_nt(low, low)
        return [diagonal[i * ROWS : (i + 1) * ROWS, :] for i in range(LANES // ROWS)]

    def fills(self):
        def rows_of_u():
            self.u = stack_right(mm_nn(self.w[...], self.z[self.before, :]), 0)

        def panel():
            p = mm(stack_left(self.z[:, self.before], 1), self.w_nt, ((1,), (1,)))
            self.q[:, self.before] = p[self.width :, :]
            self.p = stack_left(p, 1)

        def columns(at):
            stop = min(at + TILE, self.width)
            self.z[:, at:stop] -= mm(self.p, self.u[:, at:stop], ((1,), (0,)))

        return [rows_of_u, panel] + [functools.partial(columns, at) for at in range(0, self.width, TILE)]

    def store(self, out):
        for i, row in enumerate(out):
            self.w[i * ROWS : (i + 1) * ROWS, :] = row

    def finish(self):
        last = block(self.blocks - 1)
        self.q[:, last] = mm_nt(self.z[self.width :, last], self.w[...])


def run_chains(chains):
    def step_of(members):
        def step(j, carry):
            rows = [chain.look(j) for chain in members]
            fills = [fill for several in zip_longest(*[chain.fills() for chain in members]) for fill in several if fill]
            for chain, out in zip(members, in_turns([inverse_factor(r) for r in rows], fills)):
                chain.store(out)
            return carry

        return step

    start = 0
    for end in sorted({chain.blocks for chain in chains}):
        lax.fori_loop(start, end, step_of([chain for chain in chains if chain.blocks >= end]), 0)
        start = end
    for chain in chains:
        chain.finish()


class Copies:
    def __init__(self, semaphores):
        self.semaphores, self.used = semaphores, 0

    def start(self, source, target):
        copy = pltpu.make_async_copy(source, target, self.semaphores.at[self.used])
        self.used += 1
        copy.start()
        return copy


def wait(copies):
    for copy in copies:
        copy.wait()


def offsets(size):
    return size // LANES // 2 + 1


def pack_products(cols, out_ref, dims, scale):
    blocks = len(cols)
    for i in range(blocks):
        for o in range(offsets(blocks * LANES)):
            term = mm(cols[i], cols[(i + o) % blocks], dims)
            out_ref[block(i), block(o)] = (term * scale).astype(out_ref.dtype)


def first_kernel(count, scale_left, scale_right, grad_in, gram, basis, gram_left, basis_left, *refs):
    window_ref, both_ref, right_refs, left_refs = refs[0], refs[1], refs[2:4], refs[4:6]
    grad_ref, window_vmem, both_vmem, right, left, semaphores = refs[6:]
    rows, columns = grad_ref.shape
    copies = Copies(semaphores)
    window = half_window(gram.shape[1])
    width = window_vmem.shape[1] - window
    half = lax.div(2 * lax.axis_index("row"), count)
    at = pl.ds(pl.multiple_of(half * (gram.shape[1] - window), LANES), window)
    size = gram_left.shape[1]
    packing = [
        copies.start(gram.at[:, at], window_vmem.at[:, pl.ds(0, window)]),
        copies.start(basis.at[:, pl.ds(0, width)], window_vmem.at[:, pl.ds(window, width)]),
        copies.start(gram_left, both_vmem.at[:, pl.ds(0, size)]),
        copies.start(basis_left, both_vmem.at[:, pl.ds(size, size)]),
    ]
    loading = [copies.start(grad_in, grad_ref)]
    wait(packing)
    out = [copies.start(window_vmem, window_ref), copies.start(both_vmem, both_ref)]
    wait(loading)
    pack_products([grad_ref[:, block(i)] for i in range(columns // LANES)], right, ((0,), (0,)), scale_right)
    for axis, packed, targets in (("row", right, right_refs), ("col", left, left_refs)):
        if axis == "col":
            pack_products([grad_ref[block(i), :] for i in range(rows // LANES)], left, ((1,), (1,)), scale_left)
        own = lax.rem(lax.axis_index(axis), 2)
        size = packed.shape[0] // 2
        for side, target in zip((own, 1 - own), targets):
            at = pl.ds(pl.multiple_of(side * size, 2 * ROWS), size)
            out.append(copies.start(packed.at[at, :], target))
    wait(out)


def first_sends(count, width, grad, gram, basis, gram_left, basis_left, scale_left, scale_right):
    rows, columns = grad.shape
    right, left = (columns, offsets(columns) * LANES), (rows, offsets(rows) * LANES)
    window = (gram.shape[0], half_window(gram.shape[1]) + width)
    both = (gram_left.shape[0], 2 * gram_left.shape[1])
    f32, bf16 = jnp.float32, jnp.bfloat16
    return pl.pallas_call(
        functools.partial(first_kernel, count, scale_left, scale_right),
        out_shape=[jax.ShapeDtypeStruct(shape, f32) for shape in (window, both)]
        + [jax.ShapeDtypeStruct((shape[0] // 2, shape[1]), bf16) for shape in (right, right, left, left)],
        in_specs=any_specs(5),
        out_specs=any_specs(6),
        scratch_shapes=[
            pltpu.VMEM(grad.shape, bf16),
            pltpu.VMEM(window, f32),
            pltpu.VMEM(both, f32),
            pltpu.VMEM(right, bf16),
            pltpu.VMEM(left, bf16),
            pltpu.SemaphoreType.DMA((11,)),
        ],
        compiler_params=pltpu.CompilerParams(vmem_limit_bytes=VMEM_LIMIT),
    )(grad, gram, basis, gram_left, basis_left)


def rows_at(me, distance, rows):
    return pl.ds(pl.multiple_of((me ^ distance) * rows, ROWS), rows)


def new_gram(gram_ref, packed_ref, gh_ref, gl_ref):
    blocks = gram_ref.shape[0] // LANES
    count = offsets(gram_ref.shape[0])

    def put(i, k, term):
        value = gram_ref[block(i), block(k)] * STAT_DECAY + term
        gram_ref[block(i), block(k)] = value
        gh_ref[block(i), block(k)], gl_ref[block(i), block(k)] = split(value)

    for i in range(blocks):
        for o in range(count):
            k = (i + o) % blocks
            term = packed_ref[block(i), block(o)].astype(jnp.float32) * (1.0 - STAT_DECAY)
            put(i, k, term)
            if o > 0 and not (blocks % 2 == 0 and o == count - 1):
                put(k, i, term.T)


def image(z_ref, gh_ref, gl_ref, basis_ref):
    width = z_ref.shape[1]
    for at in range(0, width, TILE):
        stop = min(at + TILE, width)
        bh, bl = split(basis_ref[:, at:stop])
        z_ref[width:, at:stop] = product(gh_ref[...], gl_ref[...], bh, bl, ((1,), (0,)))


def own_rows(ref, me, rows):
    return ref[pl.ds(pl.multiple_of(me * rows, ROWS), rows), :]


def half_window(size):
    return -(-size // 2 // LANES) * LANES


def fill_halves(gram, half):
    size = gram.shape[0]
    window = half_window(size)
    rest = size - window
    near = half * window
    far = pl.ds(pl.multiple_of((1 - half) * rest, LANES), window)
    for i in range(rest // LANES):
        at = pl.ds(pl.multiple_of(near + i * LANES, LANES), LANES)
        gram[far, at] = gram[at, far].T


def packed_copies(copies, me, sums, packed):
    side = lax.rem(me, 2) if len(sums) > 1 else 0
    return [copies.start(piece, packed.at[rows_at(side, d, piece.shape[0]), :]) for d, piece in sums]


def take(refs, distances_of):
    return [(d, refs.pop(0)) for d in distances_of]


def head_kernel(count, owns, others, sums, *refs):
    refs = list(refs)
    gram_in, basis_in, other_in, sum_in = take(refs, owns), take(refs, owns), take(refs, others), take(refs, sums)
    rows_ref, gh_ref, gl_ref, q_ref, gram, packed, basis, gh, gl, rows_own, z, w, semaphores = refs
    me = lax.axis_index("row")
    copies = Copies(semaphores)
    width = basis.shape[1]
    half = lax.div(2 * me, count)
    window = half_window(gram.shape[0])
    others_at = pl.ds(pl.multiple_of((1 - half) * (gram.shape[0] - window), LANES), window)
    first, second = [], []
    for d, piece in gram_in:
        first.append(copies.start(piece, gram.at[rows_at(me, d, piece.shape[0]), :]))
    for d, piece in other_in:
        at = rows_at(me, d, piece.shape[0])
        first.append(copies.start(piece.at[:, pl.ds(0, window)], gram.at[at, others_at]))
    first += packed_copies(copies, me, sum_in, packed)
    for d, piece in basis_in:
        at = rows_at(me, d, piece.shape[0])
        second.append(copies.start(piece.at[:, pl.ds(0, width)], basis.at[at, :]))
    for d, piece in other_in:
        at = rows_at(me, d, piece.shape[0])
        second.append(copies.start(piece.at[:, pl.ds(window, width)], basis.at[at, :]))
    wait(first)
    if other_in:
        fill_halves(gram, half)
    new_gram(gram, packed, gh, gl)
    rows_own[...] = own_rows(gram, me, rows_own.shape[0])
    out = [copies.start(gh, gh_ref), copies.start(gl, gl_ref), copies.start(rows_own, rows_ref)]
    wait(second)
    image(z, gh, gl, basis)
    chain = Chain(z, w, q_ref)
    chain.cross()
    run_chains([chain])
    wait(out)


def any_specs(count):
    return [pl.BlockSpec(memory_space=pl.ANY)] * count


def chain_scratch(width, rows):
    return [pltpu.VMEM((width + rows, width), jnp.float32), pltpu.VMEM((LANES, LANES), jnp.float32)]


def head(count, grams, bases, others, sums, width):
    args = [p for group in (grams, bases, others, sums) for _, p in group]
    rows, size = grams[0][1].shape
    f32, bf16 = jnp.float32, jnp.bfloat16
    return pl.pallas_call(
        functools.partial(head_kernel, count, *[[d for d, _ in group] for group in (grams, others, sums)]),
        out_shape=[
            jax.ShapeDtypeStruct((rows, size), f32),
            jax.ShapeDtypeStruct((size, size), bf16),
            jax.ShapeDtypeStruct((size, size), bf16),
            jax.ShapeDtypeStruct((size, width), f32),
        ],
        in_specs=any_specs(len(args)),
        out_specs=[pl.BlockSpec(memory_space=pl.ANY)] * 3 + [pl.BlockSpec(memory_space=pltpu.VMEM)],
        scratch_shapes=[
            pltpu.VMEM((size, size), f32),
            pltpu.VMEM((size, offsets(size) * LANES), bf16),
            pltpu.VMEM((size, width), f32),
            pltpu.VMEM((size, size), bf16),
            pltpu.VMEM((size, size), bf16),
            pltpu.VMEM((rows, size), f32),
            *chain_scratch(width, size),
            pltpu.SemaphoreType.DMA((len(args) + len(others) + 3,)),
        ],
        compiler_params=pltpu.CompilerParams(vmem_limit_bytes=VMEM_LIMIT),
    )(*args)


def rest_kernel(bases, others, lefts, sums, *refs):
    refs = list(refs)
    gh_in, gl_in, q_in, grad_in, weight_in, moment_in, second_in = refs[:7]
    refs = refs[7:]
    basis_in, other_in, left_in, sum_in = take(refs, bases), take(refs, others), take(refs, lefts), take(refs, sums)
    weight_out, moment_out, second_out, right_rows, left_rows, gram_rows = refs[:6]
    (gh, gl, q_first, basis, qr, ql, gram_l, packed_l, basis_l, glh, gll, zr, wr, zl, wl) = refs[6:21]
    (grad, weight, moment, second, inner, turn, right_half, left_half, left_t, semaphores) = refs[21:]
    row, col = lax.axis_index("row"), lax.axis_index("col")
    copies = Copies(semaphores)
    first = q_first.shape[1]
    width = zr.shape[1]
    start = [copies.start(gh_in, gh), copies.start(gl_in, gl)]
    for d, piece in basis_in:
        at = rows_at(row, d, piece.shape[0])
        start.append(copies.start(piece.at[:, pl.ds(first, width)], basis.at[at, :]))
    for d, piece in other_in:
        start.append(copies.start(piece, basis.at[rows_at(row, d, piece.shape[0]), :]))
    project = [copies.start(q_in, q_first)]
    size = gram_l.shape[0]
    left_copies = []
    for ats, pieces in sum_in:
        rows = pieces.shape[0] // len(ats)
        for n, at in enumerate(ats):
            piece = pieces.at[pl.ds(n * rows, rows), :]
            left_copies.append(copies.start(piece, packed_l.at[rows_at(piece_index("col"), at, rows), :]))
    rows = left_rows.shape[0]
    for ats, pieces in left_in:
        for n, at in enumerate(ats):
            for i, ref in enumerate((gram_l, basis_l)):
                piece = pieces.at[pl.ds(n * rows, rows), pl.ds(i * size, size)]
                left_copies.append(copies.start(piece, ref.at[rows_at(col, at, rows), :]))
    tail = [copies.start(grad_in, grad), copies.start(moment_in, moment)]
    late = [copies.start(second_in, second), copies.start(weight_in, weight)]

    wait(start)
    image(zr, gh, gl, basis)
    wait(project)
    qh, qo = split(q_first[...])
    xh, xl = split(zr[width:, :])
    sh, sl = split(product(qh, qo, xh, xl, ((0,), (0,))))
    zr[width:, :] -= product(qh, qo, sh, sl, ((1,), (0,)))
    wait(left_copies)
    new_gram(gram_l, packed_l, glh, gll)
    gram_rows[...] = own_rows(gram_l, col, gram_rows.shape[0])
    image(zl, glh, gll, basis_l)
    right, left = Chain(zr, wr, qr), Chain(zl, wl, ql)
    right.cross()
    left.cross()
    right_half[:, :first] = q_first[...].astype(jnp.bfloat16)
    wait(tail)
    for i in range(grad.shape[0] // LANES):
        moment[block(i), :] = FIRST_DECAY * moment[block(i), :] + (1.0 - FIRST_DECAY) * grad[block(i), :].astype(
            jnp.float32
        )
    out = [copies.start(moment, moment_out)]
    run_chains([left, right] if left.blocks <= right.blocks else [right, left])
    left_half[...] = ql[...].astype(jnp.bfloat16)
    right_half[:, first:] = qr[...].astype(jnp.bfloat16)
    right_rows[:, :first] = own_rows(q_first, row, right_rows.shape[0])
    right_rows[:, first:] = own_rows(qr, row, right_rows.shape[0])
    left_rows[...] = own_rows(ql, col, left_rows.shape[0])

    rows, columns = grad.shape
    tiles = [pl.ds(at, min(TILE, columns - at)) for at in range(0, columns, TILE)]
    left_t[...] = left_half[...].T
    for tile in tiles:
        inner[:rows, tile] = mm(left_t[...], grad[:, tile], ((1,), (0,))).astype(jnp.bfloat16)
        half = moment[:, tile].astype(jnp.bfloat16)
        inner[rows:, tile] = mm(left_t[...], half, ((1,), (0,))).astype(jnp.bfloat16)
    wait(late)
    for tile in tiles:
        rotated = mm(inner[...], right_half[:, tile], ((1,), (0,)))
        rotated_grad, rotated_moment = rotated[:rows, :], rotated[rows:, :]
        new_second = SECOND_DECAY * second[:, tile] + (1.0 - SECOND_DECAY) * rotated_grad * rotated_grad
        second[:, tile] = new_second
        out.append(copies.start(second.at[:, tile], second_out.at[:, tile]))
        turn[:, tile] = (rotated_moment / (jnp.sqrt(new_second) + EPSILON)).astype(jnp.bfloat16)
    turned = mm(left_half[...], turn[...], ((1,), (0,))).astype(jnp.bfloat16)
    for tile in tiles:
        update = mm(turned, right_half[tile, :], ((1,), (1,)))
        old = weight[:, tile]
        weight[:, tile] = old - STEP_SIZE * (update + WEIGHT_DECAY * old)
        out.append(copies.start(weight.at[:, tile], weight_out.at[:, tile]))
    wait(out)


def rest(gh, gl, q_first, tiles, bases, others, lefts, sums):
    args = [gh, gl, q_first, *tiles] + [p for _, p in bases + others + lefts + sums]
    rows_r, size_r = bases[0][1].shape
    width = size_r - q_first.shape[1]
    rows_l, size_l = lefts[0][1].shape[0], lefts[0][1].shape[1] // 2
    tile = tiles[0].shape
    f32, bf16 = jnp.float32, jnp.bfloat16
    vmem, anywhere = pl.BlockSpec(memory_space=pltpu.VMEM), pl.BlockSpec(memory_space=pl.ANY)
    return pl.pallas_call(
        functools.partial(rest_kernel, *[[d for d, _ in group] for group in (bases, others, lefts, sums)]),
        out_shape=[
            jax.ShapeDtypeStruct(tile, f32),
            jax.ShapeDtypeStruct(tile, f32),
            jax.ShapeDtypeStruct(tile, f32),
            jax.ShapeDtypeStruct((rows_r, size_r), f32),
            jax.ShapeDtypeStruct((rows_l, size_l), f32),
            jax.ShapeDtypeStruct((rows_l, size_l), f32),
        ],
        in_specs=any_specs(len(args)),
        out_specs=[anywhere] * 3 + [vmem] * 3,
        scratch_shapes=[
            pltpu.VMEM((size_r, size_r), bf16),
            pltpu.VMEM((size_r, size_r), bf16),
            pltpu.VMEM((size_r, size_r - width), f32),
            pltpu.VMEM((size_r, width), f32),
            pltpu.VMEM((size_r, width), f32),
            pltpu.VMEM((size_l, size_l), f32),
            pltpu.VMEM((size_l, size_l), f32),
            pltpu.VMEM((size_l, offsets(size_l) * LANES), bf16),
            pltpu.VMEM((size_l, size_l), f32),
            pltpu.VMEM((size_l, size_l), bf16),
            pltpu.VMEM((size_l, size_l), bf16),
            *chain_scratch(width, size_r),
            *chain_scratch(size_l, size_l),
            pltpu.VMEM(tile, bf16),
            pltpu.VMEM(tile, f32),
            pltpu.VMEM(tile, f32),
            pltpu.VMEM(tile, f32),
            pltpu.VMEM((2 * tile[0], tile[1]), bf16),
            pltpu.VMEM(tile, bf16),
            pltpu.VMEM((size_r, size_r), bf16),
            pltpu.VMEM((size_l, size_l), bf16),
            pltpu.VMEM((size_l, size_l), bf16),
            pltpu.SemaphoreType.DMA((len(args) + 1 + 3 * (size_l // rows_l) + 2 * -(-tile[1] // TILE),)),
        ],
        compiler_params=pltpu.CompilerParams(vmem_limit_bytes=VMEM_LIMIT),
    )(*args)


def swap(x, axis, distance):
    count = lax.axis_size(axis)
    return lax.ppermute(x, axis, [(i, i ^ distance) for i in range(count)])


def distances(axis):
    count = lax.axis_size(axis)
    return [1 << b for b in range(count.bit_length() - 1)]


def spread(held, axis, steps):
    for distance in steps:
        held = held + [(at ^ distance, swap(piece, axis, distance)) for at, piece in held]
    return held


def parts(x, axis, distance):
    rows = x.shape[0] // 2
    own = lax.rem(lax.div(lax.axis_index(axis), distance), 2)
    return tuple(lax.dynamic_slice_in_dim(x, at * rows, rows, 0) for at in (own, 1 - own))


def gather_stacked(x, axis):
    held = [([0], x)]
    for distance in reversed(distances(axis)):
        sent = jnp.concatenate([piece for _, piece in held]) if len(held) > 1 else x
        held.append(([at ^ distance for ats, _ in held for at in ats], swap(sent, axis, distance)))
    return held


def add(x, y):
    return (x.astype(jnp.float32) + y.astype(jnp.float32)).astype(x.dtype)


def piece_weights(axis):
    return [1 << n for n in reversed(range(len(distances(axis)) - 1))]


def piece_index(axis):
    me, index = lax.axis_index(axis), 0
    for distance, weight in zip(distances(axis), piece_weights(axis)):
        index = index + weight * lax.rem(lax.div(me, distance), 2)
    return index


def sum_stacked(keep, other, axis):
    steps, weights = distances(axis), piece_weights(axis)
    x = None
    for distance in steps[:-1]:
        if x is not None:
            keep, other = parts(x, axis, distance)
        x = add(keep, swap(other, axis, distance))
    x = add(x, swap(x, axis, steps[-1]))
    held = [([0], x)]
    for distance, weight in reversed(list(zip(steps, weights))):
        sent = jnp.concatenate([piece for _, piece in held]) if len(held) > 1 else x
        held.append(([at ^ weight for ats, _ in held for at in ats], swap(sent, axis, distance)))
    return held


def sum_halves(keep, other, axis):
    total = add(keep, swap(other, axis, 1))
    for distance in distances(axis)[1:]:
        total = add(total, swap(total, axis, distance))
    return total, [(0, total), (1, swap(total, axis, 1))]


def body(grad, weight, moment, second, gram_left, basis_left, gram_right, basis_right):
    block_left, block_right = grad.shape
    first = max(block_right - block_left, LANES)
    count = lax.axis_size("row")
    gram_right, basis_right = gram_right[0], basis_right[0]
    window, left, keep_right, other_right, keep_left, other_left = first_sends(
        count,
        first,
        grad,
        gram_right,
        basis_right,
        gram_left[0],
        basis_left[0],
        1.0 / (block_right * lax.axis_size("col")),
        1.0 / (block_left * count),
    )
    near = distances("row")[-2::-1]
    arrived = swap(window, "row", count // 2)
    gram_right, basis_right, _ = lax.optimization_barrier((gram_right, basis_right, arrived))
    grams, bases = spread([(0, gram_right)], "row", near), spread([(0, basis_right)], "row", near)
    others = spread([(count // 2, arrived)], "row", near)
    left = gather_stacked(left, "col")
    sent, sums_right = sum_halves(keep_right, other_right, "row")
    sums_left = sum_stacked(keep_left, other_left, "col")
    last, _ = lax.optimization_barrier((basis_right[:, first:], sent))
    last = [(d, swap(last, "row", d)) for d in range(count // 2, count)]
    new_gram_right, gh, gl, q_first = head(count, grams, bases, others, sums_right, first)
    new_weight, new_moment, new_second, basis_rows_right, basis_rows_left, new_gram_left = rest(
        gh, gl, q_first, (grad, weight, moment, second), bases, last, left, sums_left
    )
    return (
        new_weight,
        new_moment,
        new_second,
        new_gram_left[None],
        basis_rows_left[None],
        new_gram_right[None],
        basis_rows_right[None],
    )


def solution(mesh):
    specs = (
        P("row", "col"),
        P("row", "col"),
        P("row", "col"),
        P("row", "col"),
        P("row", "col", None),
        P("row", "col", None),
        P("col", "row", None),
        P("col", "row", None),
    )
    out_specs = specs[:3] + specs[4:]
    return jax.shard_map(body, mesh=mesh, in_specs=specs, out_specs=out_specs, check_vma=False)
```

```python
import functools
from itertools import zip_longest
import jax
import jax.numpy as jnp
from jax import lax
from jax.experimental import pallas as pl
from jax.experimental.pallas import tpu as pltpu
from jax.sharding import PartitionSpec as P

STAT_DECAY = 0.95
FIRST_DECAY = 0.9
SECOND_DECAY = 0.95
EPSILON = 1e-08
STEP_SIZE = 0.02
WEIGHT_DECAY = 0.01
LANES = 128
ROWS = 8
TILE = 256
VMEM_LIMIT = 56 * 2**20


def sub_row(x, k):
    return jnp.broadcast_to(x[k : k + 1, :], (ROWS, LANES))


def lane_col(x, c):
    return jnp.broadcast_to(x[:, c : c + 1], (ROWS, LANES))


def reciprocal(p):
    guess = pl.reciprocal(p, approx=True)
    return guess * (2.0 - p * guess)


def sum_tree(terms):
    while len(terms) > 1:
        terms = [a + b for a, b in zip(terms[::2], terms[1::2])]
    return terms[0]


def inverse_factor(rows):
    count = LANES // ROWS
    rows = list(rows)
    subs = lax.broadcasted_iota(jnp.int32, (ROWS, LANES), 0)
    lanes = lax.broadcasted_iota(jnp.int32, (ROWS, LANES), 1)
    out = []
    for s in range(count):
        base = s * ROWS
        pivot = rows[s]
        here = (lanes >= base) & (lanes < base + ROWS)
        if s == 0:
            cols = [lane_col(pivot, k) for k in range(ROWS)]
        ahead = range(base + ROWS, base + 2 * ROWS) if s < count - 1 else ()
        across = [lane_col(pivot, c) for c in ahead]
        next_cols = [lane_col(rows[s + 1], c) for c in ahead]
        next_coeffs = [lane_col(rows[s + 1], base + k) for k in range(ROWS)] if ahead else None
        full = jnp.where(here, (lanes == subs + base).astype(jnp.float32), pivot)
        forward = full
        pivots = jnp.ones((ROWS, LANES), jnp.float32)
        yield
        for j in range(0, ROWS, 2):
            a, b, d = sub_row(cols[j], j), sub_row(cols[j], j + 1), sub_row(cols[j + 1], j + 1)
            det = a * d - b * b
            inv = reciprocal(det)
            pair = (subs == j) | (subs == j + 1)
            one = jnp.where(pair, jnp.where(subs == j, -1.0, 0.0), cols[j])
            two = jnp.where(pair, jnp.where(subs == j, 0.0, -1.0), cols[j + 1])
            for k in range(j + 2, min(j + 4, ROWS)):
                x, y = sub_row(cols[k], j), sub_row(cols[k], j + 1)
                change = one * (d * x - b * y) + two * (a * y - b * x)
                cols[k] = jnp.where(pair, 0.0, cols[k]) - change * inv
            yield
            one, two = (one * d - two * b) * inv, (two * a - one * b) * inv
            for k in range(j + 4, ROWS):
                x, y = sub_row(cols[k], j), sub_row(cols[k], j + 1)
                cols[k] = jnp.where(pair, 0.0, cols[k]) - (one * x + two * y)
            yield
            across = [
                jnp.where(pair, 0.0, c) - (one * sub_row(c, j) + two * sub_row(c, j + 1)) for c in across
            ]
            yield
            full = jnp.where(pair, 0.0, full) - (one * sub_row(full, j) + two * sub_row(full, j + 1))
            inner = b * reciprocal(a)
            below = subs > j + 1
            lower = jnp.where(below, one, jnp.where(subs == j + 1, inner, 0.0))
            change = lower * sub_row(forward, j)
            if j + 2 < ROWS:
                change = change + jnp.where(below, two, 0.0) * sub_row(forward, j + 1)
            forward = forward - change
            pivots = jnp.where(subs == j, a, jnp.where(subs == j + 1, d - inner * b, pivots))
            yield
        out.append(jnp.where(lanes < base + ROWS, forward * lax.rsqrt(pivots), 0.0))
        if s < count - 1:
            cols = [
                own - sum_tree([next_coeffs[k] * sub_row(c, k) for k in range(ROWS)])
                for own, c in zip(next_cols, across)
            ]
            yield
            spread = [sub_row(full, k) for k in range(ROWS)]
            for i in range(s + 1, count):
                coeffs = next_coeffs if i == s + 1 else [lane_col(rows[i], base + k) for k in range(ROWS)]
                rows[i] = jnp.where(here, 0.0, rows[i]) - sum_tree([coeffs[k] * spread[k] for k in range(ROWS)])
                yield
    return out


def in_turns(generators, fills):
    results = [None] * len(generators)
    live = list(enumerate(generators))
    fills = list(fills)
    total, turn, done = 350, 0, 0
    while live:
        for at, generator in list(live):
            try:
                next(generator)
            except StopIteration as stop:
                results[at] = stop.value
                live.remove((at, generator))
        turn += 1
        while done < len(fills) and done * total <= turn * len(fills):
            fills[done]()
            done += 1
    for fill in fills[done:]:
        fill()
    return results


def split(x):
    hi = x.astype(jnp.bfloat16)
    return hi, (x - hi.astype(jnp.float32)).astype(jnp.bfloat16)


def stack_left(x, axis):
    hi, lo = split(x)
    return jnp.concatenate([hi, hi, lo], axis=axis)


def stack_right(x, axis):
    hi, lo = split(x)
    return jnp.concatenate([hi, lo, hi], axis=axis)


def mm(a, b, dims):
    return lax.dot_general(a, b, (dims, ((), ())), preferred_element_type=jnp.float32)


def mm_nn(a, b):
    return mm(stack_left(a, 1), stack_right(b, 0), ((1,), (0,)))


def mm_nt(a, b):
    return mm(stack_left(a, 1), stack_right(b, 1), ((1,), (1,)))


def product(ah, al, bh, bl, dims):
    return mm(ah, bh, dims) + (mm(ah, bl, dims) + mm(al, bh, dims))


def block(i):
    return pl.ds(i * LANES, LANES) if isinstance(i, int) else pl.ds(pl.multiple_of(i * LANES, LANES), LANES)


class Chain:
    def __init__(self, z_ref, w_ref, q_ref):
        self.z, self.w, self.q = z_ref, w_ref, q_ref
        self.width = z_ref.shape[1]
        self.blocks = self.width // LANES

    def cross(self):
        hi, lo = split(self.z[self.width :, :])
        dims = ((0,), (0,))
        self.z[: self.width, :] = product(hi, lo, hi, lo, dims)
        self.w[...] = jnp.zeros_like(self.w)

    def look(self, j):
        self.before = block(lax.max(j - 1, 0))
        self.w_nt = stack_right(self.w[...], 1)
        at = block(j)
        low = mm(stack_left(self.z[at, self.before], 1), self.w_nt, ((1,), (1,)))
        diagonal = self.z[at, at] - mm_nt(low, low)
        return [diagonal[i * ROWS : (i + 1) * ROWS, :] for i in range(LANES // ROWS)]

    def fills(self):
        def rows_of_u():
            self.u = stack_right(mm_nn(self.w[...], self.z[self.before, :]), 0)

        def panel():
            p = mm(stack_left(self.z[:, self.before], 1), self.w_nt, ((1,), (1,)))
            self.q[:, self.before] = p[self.width :, :]
            self.p = stack_left(p, 1)

        def columns(at):
            stop = min(at + TILE, self.width)
            self.z[:, at:stop] -= mm(self.p, self.u[:, at:stop], ((1,), (0,)))

        return [rows_of_u, panel] + [functools.partial(columns, at) for at in range(0, self.width, TILE)]

    def store(self, out):
        for i, row in enumerate(out):
            self.w[i * ROWS : (i + 1) * ROWS, :] = row

    def finish(self):
        last = block(self.blocks - 1)
        self.q[:, last] = mm_nt(self.z[self.width :, last], self.w[...])


def run_chains(chains):
    def step_of(members):
        def step(j, carry):
            rows = [chain.look(j) for chain in members]
            fills = [fill for several in zip_longest(*[chain.fills() for chain in members]) for fill in several if fill]
            for chain, out in zip(members, in_turns([inverse_factor(r) for r in rows], fills)):
                chain.store(out)
            return carry

        return step

    start = 0
    for end in sorted({chain.blocks for chain in chains}):
        lax.fori_loop(start, end, step_of([chain for chain in chains if chain.blocks >= end]), 0)
        start = end
    for chain in chains:
        chain.finish()


class Copies:
    def __init__(self, semaphores):
        self.semaphores, self.used = semaphores, 0

    def start(self, source, target):
        copy = pltpu.make_async_copy(source, target, self.semaphores.at[self.used])
        self.used += 1
        copy.start()
        return copy


def wait(copies):
    for copy in copies:
        copy.wait()


def offsets(size):
    return size // LANES // 2 + 1


def pack_products(cols, out_ref, dims, scale):
    blocks = len(cols)
    for i in range(blocks):
        for o in range(offsets(blocks * LANES)):
            term = mm(cols[i], cols[(i + o) % blocks], dims)
            out_ref[block(i), block(o)] = (term * scale).astype(out_ref.dtype)


def first_kernel(count, scale_left, scale_right, grad_in, gram, basis, gram_left, basis_left, *refs):
    window_ref, both_ref, right_refs, left_refs = refs[0], refs[1], refs[2:4], refs[4:6]
    grad_ref, window_vmem, both_vmem, right, left, semaphores = refs[6:]
    rows, columns = grad_ref.shape
    copies = Copies(semaphores)
    window = half_window(gram.shape[1])
    width = window_vmem.shape[1] - window
    half = lax.div(2 * lax.axis_index("row"), count)
    at = pl.ds(pl.multiple_of(half * (gram.shape[1] - window), LANES), window)
    size = gram_left.shape[1]
    packing = [
        copies.start(gram.at[:, at], window_vmem.at[:, pl.ds(0, window)]),
        copies.start(basis.at[:, pl.ds(0, width)], window_vmem.at[:, pl.ds(window, width)]),
        copies.start(gram_left, both_vmem.at[:, pl.ds(0, size)]),
        copies.start(basis_left, both_vmem.at[:, pl.ds(size, size)]),
    ]
    loading = [copies.start(grad_in, grad_ref)]
    wait(packing)
    out = [copies.start(window_vmem, window_ref), copies.start(both_vmem, both_ref)]
    wait(loading)
    pack_products([grad_ref[:, block(i)] for i in range(columns // LANES)], right, ((0,), (0,)), scale_right)
    for axis, packed, targets in (("row", right, right_refs), ("col", left, left_refs)):
        if axis == "col":
            pack_products([grad_ref[block(i), :] for i in range(rows // LANES)], left, ((1,), (1,)), scale_left)
        own = lax.rem(lax.axis_index(axis), 2)
        size = packed.shape[0] // 2
        for side, target in zip((own, 1 - own), targets):
            at = pl.ds(pl.multiple_of(side * size, 2 * ROWS), size)
            out.append(copies.start(packed.at[at, :], target))
    wait(out)


def first_sends(count, width, grad, gram, basis, gram_left, basis_left, scale_left, scale_right):
    rows, columns = grad.shape
    right, left = (columns, offsets(columns) * LANES), (rows, offsets(rows) * LANES)
    window = (gram.shape[0], half_window(gram.shape[1]) + width)
    both = (gram_left.shape[0], 2 * gram_left.shape[1])
    f32, bf16 = jnp.float32, jnp.bfloat16
    return pl.pallas_call(
        functools.partial(first_kernel, count, scale_left, scale_right),
        out_shape=[jax.ShapeDtypeStruct(shape, f32) for shape in (window, both)]
        + [jax.ShapeDtypeStruct((shape[0] // 2, shape[1]), bf16) for shape in (right, right, left, left)],
        in_specs=any_specs(5),
        out_specs=any_specs(6),
        scratch_shapes=[
            pltpu.VMEM(grad.shape, bf16),
            pltpu.VMEM(window, f32),
            pltpu.VMEM(both, f32),
            pltpu.VMEM(right, bf16),
            pltpu.VMEM(left, bf16),
            pltpu.SemaphoreType.DMA((11,)),
        ],
        compiler_params=pltpu.CompilerParams(vmem_limit_bytes=VMEM_LIMIT),
    )(grad, gram, basis, gram_left, basis_left)


def rows_at(me, distance, rows):
    return pl.ds(pl.multiple_of((me ^ distance) * rows, ROWS), rows)


def new_gram(gram_ref, packed_ref, gh_ref, gl_ref):
    blocks = gram_ref.shape[0] // LANES
    count = offsets(gram_ref.shape[0])

    def put(i, k, term):
        value = gram_ref[block(i), block(k)] * STAT_DECAY + term
        gram_ref[block(i), block(k)] = value
        gh_ref[block(i), block(k)], gl_ref[block(i), block(k)] = split(value)

    for i in range(blocks):
        for o in range(count):
            k = (i + o) % blocks
            term = packed_ref[block(i), block(o)].astype(jnp.float32) * (1.0 - STAT_DECAY)
            put(i, k, term)
            if o > 0 and not (blocks % 2 == 0 and o == count - 1):
                put(k, i, term.T)


def image(z_ref, gh_ref, gl_ref, basis_ref):
    width = z_ref.shape[1]
    for at in range(0, width, TILE):
        stop = min(at + TILE, width)
        bh, bl = split(basis_ref[:, at:stop])
        z_ref[width:, at:stop] = product(gh_ref[...], gl_ref[...], bh, bl, ((1,), (0,)))


def own_rows(ref, me, rows):
    return ref[pl.ds(pl.multiple_of(me * rows, ROWS), rows), :]


def half_window(size):
    return -(-size // 2 // LANES) * LANES


def fill_halves(gram, half):
    size = gram.shape[0]
    window = half_window(size)
    rest = size - window
    near = half * window
    far = pl.ds(pl.multiple_of((1 - half) * rest, LANES), window)
    for i in range(rest // LANES):
        at = pl.ds(pl.multiple_of(near + i * LANES, LANES), LANES)
        gram[far, at] = gram[at, far].T


def packed_copies(copies, me, sums, packed):
    side = lax.rem(me, 2) if len(sums) > 1 else 0
    return [copies.start(piece, packed.at[rows_at(side, d, piece.shape[0]), :]) for d, piece in sums]


def take(refs, distances_of):
    return [(d, refs.pop(0)) for d in distances_of]


def head_kernel(count, owns, others, sums, *refs):
    refs = list(refs)
    gram_in, basis_in, other_in, sum_in = take(refs, owns), take(refs, owns), take(refs, others), take(refs, sums)
    rows_ref, gh_ref, gl_ref, q_ref, gram, packed, basis, gh, gl, rows_own, z, w, semaphores = refs
    me = lax.axis_index("row")
    copies = Copies(semaphores)
    width = basis.shape[1]
    half = lax.div(2 * me, count)
    window = half_window(gram.shape[0])
    others_at = pl.ds(pl.multiple_of((1 - half) * (gram.shape[0] - window), LANES), window)
    first, second = [], []
    for d, piece in gram_in:
        first.append(copies.start(piece, gram.at[rows_at(me, d, piece.shape[0]), :]))
    for d, piece in other_in:
        at = rows_at(me, d, piece.shape[0])
        first.append(copies.start(piece.at[:, pl.ds(0, window)], gram.at[at, others_at]))
    first += packed_copies(copies, me, sum_in, packed)
    for d, piece in basis_in:
        at = rows_at(me, d, piece.shape[0])
        second.append(copies.start(piece.at[:, pl.ds(0, width)], basis.at[at, :]))
    for d, piece in other_in:
        at = rows_at(me, d, piece.shape[0])
        second.append(copies.start(piece.at[:, pl.ds(window, width)], basis.at[at, :]))
    wait(first)
    if other_in:
        fill_halves(gram, half)
    new_gram(gram, packed, gh, gl)
    rows_own[...] = own_rows(gram, me, rows_own.shape[0])
    out = [copies.start(gh, gh_ref), copies.start(gl, gl_ref), copies.start(rows_own, rows_ref)]
    wait(second)
    image(z, gh, gl, basis)
    chain = Chain(z, w, q_ref)
    chain.cross()
    run_chains([chain])
    wait(out)


def any_specs(count):
    return [pl.BlockSpec(memory_space=pl.ANY)] * count


def chain_scratch(width, rows):
    return [pltpu.VMEM((width + rows, width), jnp.float32), pltpu.VMEM((LANES, LANES), jnp.float32)]


def head(count, grams, bases, others, sums, width):
    args = [p for group in (grams, bases, others, sums) for _, p in group]
    rows, size = grams[0][1].shape
    f32, bf16 = jnp.float32, jnp.bfloat16
    return pl.pallas_call(
        functools.partial(head_kernel, count, *[[d for d, _ in group] for group in (grams, others, sums)]),
        out_shape=[
            jax.ShapeDtypeStruct((rows, size), f32),
            jax.ShapeDtypeStruct((size, size), bf16),
            jax.ShapeDtypeStruct((size, size), bf16),
            jax.ShapeDtypeStruct((size, width), f32),
        ],
        in_specs=any_specs(len(args)),
        out_specs=[pl.BlockSpec(memory_space=pl.ANY)] * 3 + [pl.BlockSpec(memory_space=pltpu.VMEM)],
        scratch_shapes=[
            pltpu.VMEM((size, size), f32),
            pltpu.VMEM((size, offsets(size) * LANES), bf16),
            pltpu.VMEM((size, width), f32),
            pltpu.VMEM((size, size), bf16),
            pltpu.VMEM((size, size), bf16),
            pltpu.VMEM((rows, size), f32),
            *chain_scratch(width, size),
            pltpu.SemaphoreType.DMA((len(args) + len(others) + 3,)),
        ],
        compiler_params=pltpu.CompilerParams(vmem_limit_bytes=VMEM_LIMIT),
    )(*args)


def rest_kernel(bases, others, lefts, sums, *refs):
    refs = list(refs)
    gh_in, gl_in, q_in, grad_in, weight_in, moment_in, second_in = refs[:7]
    refs = refs[7:]
    basis_in, other_in, left_in, sum_in = take(refs, bases), take(refs, others), take(refs, lefts), take(refs, sums)
    weight_out, moment_out, second_out, right_rows, left_rows, gram_rows = refs[:6]
    (gh, gl, q_first, basis, qr, ql, gram_l, packed_l, basis_l, glh, gll, zr, wr, zl, wl) = refs[6:21]
    (grad, weight, moment, second, inner, turn, right_half, left_half, left_t, semaphores) = refs[21:]
    row, col = lax.axis_index("row"), lax.axis_index("col")
    copies = Copies(semaphores)
    first = q_first.shape[1]
    width = zr.shape[1]
    start = [copies.start(gh_in, gh), copies.start(gl_in, gl)]
    for d, piece in basis_in:
        at = rows_at(row, d, piece.shape[0])
        start.append(copies.start(piece.at[:, pl.ds(first, width)], basis.at[at, :]))
    for d, piece in other_in:
        start.append(copies.start(piece, basis.at[rows_at(row, d, piece.shape[0]), :]))
    project = [copies.start(q_in, q_first)]
    size = gram_l.shape[0]
    left_copies = []
    for ats, pieces in sum_in:
        rows = pieces.shape[0] // len(ats)
        for n, at in enumerate(ats):
            piece = pieces.at[pl.ds(n * rows, rows), :]
            left_copies.append(copies.start(piece, packed_l.at[rows_at(piece_index("col"), at, rows), :]))
    rows = left_rows.shape[0]
    for ats, pieces in left_in:
        for n, at in enumerate(ats):
            for i, ref in enumerate((gram_l, basis_l)):
                piece = pieces.at[pl.ds(n * rows, rows), pl.ds(i * size, size)]
                left_copies.append(copies.start(piece, ref.at[rows_at(col, at, rows), :]))
    tail = [copies.start(grad_in, grad), copies.start(moment_in, moment)]
    late = [copies.start(second_in, second), copies.start(weight_in, weight)]

    wait(start)
    image(zr, gh, gl, basis)
    wait(project)
    qh, qo = split(q_first[...])
    xh, xl = split(zr[width:, :])
    sh, sl = split(product(qh, qo, xh, xl, ((0,), (0,))))
    zr[width:, :] -= product(qh, qo, sh, sl, ((1,), (0,)))
    wait(left_copies)
    new_gram(gram_l, packed_l, glh, gll)
    gram_rows[...] = own_rows(gram_l, col, gram_rows.shape[0])
    image(zl, glh, gll, basis_l)
    right, left = Chain(zr, wr, qr), Chain(zl, wl, ql)
    right.cross()
    left.cross()
    right_half[:, :first] = q_first[...].astype(jnp.bfloat16)
    wait(tail)
    for i in range(grad.shape[0] // LANES):
        moment[block(i), :] = FIRST_DECAY * moment[block(i), :] + (1.0 - FIRST_DECAY) * grad[block(i), :].astype(
            jnp.float32
        )
    out = [copies.start(moment, moment_out)]
    run_chains([left, right] if left.blocks <= right.blocks else [right, left])
    left_half[...] = ql[...].astype(jnp.bfloat16)
    right_half[:, first:] = qr[...].astype(jnp.bfloat16)
    right_rows[:, :first] = own_rows(q_first, row, right_rows.shape[0])
    right_rows[:, first:] = own_rows(qr, row, right_rows.shape[0])
    left_rows[...] = own_rows(ql, col, left_rows.shape[0])

    rows, columns = grad.shape
    tiles = [pl.ds(at, min(TILE, columns - at)) for at in range(0, columns, TILE)]
    left_t[...] = left_half[...].T
    for tile in tiles:
        inner[:rows, tile] = mm(left_t[...], grad[:, tile], ((1,), (0,))).astype(jnp.bfloat16)
        half = moment[:, tile].astype(jnp.bfloat16)
        inner[rows:, tile] = mm(left_t[...], half, ((1,), (0,))).astype(jnp.bfloat16)
    wait(late)
    for tile in tiles:
        rotated = mm(inner[...], right_half[:, tile], ((1,), (0,)))
        rotated_grad, rotated_moment = rotated[:rows, :], rotated[rows:, :]
        new_second = SECOND_DECAY * second[:, tile] + (1.0 - SECOND_DECAY) * rotated_grad * rotated_grad
        second[:, tile] = new_second
        out.append(copies.start(second.at[:, tile], second_out.at[:, tile]))
        turn[:, tile] = (rotated_moment / (jnp.sqrt(new_second) + EPSILON)).astype(jnp.bfloat16)
    turned = mm(left_half[...], turn[...], ((1,), (0,))).astype(jnp.bfloat16)
    for tile in tiles:
        update = mm(turned, right_half[tile, :], ((1,), (1,)))
        old = weight[:, tile]
        weight[:, tile] = old - STEP_SIZE * (update + WEIGHT_DECAY * old)
        out.append(copies.start(weight.at[:, tile], weight_out.at[:, tile]))
    wait(out)


def rest(gh, gl, q_first, tiles, bases, others, lefts, sums):
    args = [gh, gl, q_first, *tiles] + [p for _, p in bases + others + lefts + sums]
    rows_r, size_r = bases[0][1].shape
    width = size_r - q_first.shape[1]
    rows_l, size_l = lefts[0][1].shape[0], lefts[0][1].shape[1] // 2
    tile = tiles[0].shape
    f32, bf16 = jnp.float32, jnp.bfloat16
    vmem, anywhere = pl.BlockSpec(memory_space=pltpu.VMEM), pl.BlockSpec(memory_space=pl.ANY)
    return pl.pallas_call(
        functools.partial(rest_kernel, *[[d for d, _ in group] for group in (bases, others, lefts, sums)]),
        out_shape=[
            jax.ShapeDtypeStruct(tile, f32),
            jax.ShapeDtypeStruct(tile, f32),
            jax.ShapeDtypeStruct(tile, f32),
            jax.ShapeDtypeStruct((rows_r, size_r), f32),
            jax.ShapeDtypeStruct((rows_l, size_l), f32),
            jax.ShapeDtypeStruct((rows_l, size_l), f32),
        ],
        in_specs=any_specs(len(args)),
        out_specs=[anywhere] * 3 + [vmem] * 3,
        scratch_shapes=[
            pltpu.VMEM((size_r, size_r), bf16),
            pltpu.VMEM((size_r, size_r), bf16),
            pltpu.VMEM((size_r, size_r - width), f32),
            pltpu.VMEM((size_r, width), f32),
            pltpu.VMEM((size_r, width), f32),
            pltpu.VMEM((size_l, size_l), f32),
            pltpu.VMEM((size_l, size_l), f32),
            pltpu.VMEM((size_l, offsets(size_l) * LANES), bf16),
            pltpu.VMEM((size_l, size_l), f32),
            pltpu.VMEM((size_l, size_l), bf16),
            pltpu.VMEM((size_l, size_l), bf16),
            *chain_scratch(width, size_r),
            *chain_scratch(size_l, size_l),
            pltpu.VMEM(tile, bf16),
            pltpu.VMEM(tile, f32),
            pltpu.VMEM(tile, f32),
            pltpu.VMEM(tile, f32),
            pltpu.VMEM((2 * tile[0], tile[1]), bf16),
            pltpu.VMEM(tile, bf16),
            pltpu.VMEM((size_r, size_r), bf16),
            pltpu.VMEM((size_l, size_l), bf16),
            pltpu.VMEM((size_l, size_l), bf16),
            pltpu.SemaphoreType.DMA((len(args) + 1 + 3 * (size_l // rows_l) + 2 * -(-tile[1] // TILE),)),
        ],
        compiler_params=pltpu.CompilerParams(vmem_limit_bytes=VMEM_LIMIT),
    )(*args)


def swap(x, axis, distance):
    count = lax.axis_size(axis)
    return lax.ppermute(x, axis, [(i, i ^ distance) for i in range(count)])


def distances(axis):
    count = lax.axis_size(axis)
    return [1 << b for b in range(count.bit_length() - 1)]


def spread(held, axis, steps):
    for distance in steps:
        held = held + [(at ^ distance, swap(piece, axis, distance)) for at, piece in held]
    return held


def parts(x, axis, distance):
    rows = x.shape[0] // 2
    own = lax.rem(lax.div(lax.axis_index(axis), distance), 2)
    return tuple(lax.dynamic_slice_in_dim(x, at * rows, rows, 0) for at in (own, 1 - own))


def gather_stacked(x, axis, after):
    held = [([0], x)]
    for n, distance in enumerate(reversed(distances(axis))):
        if 0 < n <= len(after):
            (ats, piece), (piece_after, _) = held[-1], lax.optimization_barrier((held[-1][1], after[n - 1]))
            held[-1] = (ats, piece_after)
        sent = jnp.concatenate([piece for _, piece in held]) if len(held) > 1 else x
        held.append(([at ^ distance for ats, _ in held for at in ats], swap(sent, axis, distance)))
    return held


def add(x, y):
    return (x.astype(jnp.float32) + y.astype(jnp.float32)).astype(x.dtype)


def piece_weights(axis):
    return [1 << n for n in reversed(range(len(distances(axis)) - 1))]


def piece_index(axis):
    me, index = lax.axis_index(axis), 0
    for distance, weight in zip(distances(axis), piece_weights(axis)):
        index = index + weight * lax.rem(lax.div(me, distance), 2)
    return index


def sum_stacked(keep, other, axis):
    steps, weights = distances(axis), piece_weights(axis)
    x = None
    sums = []
    for distance in steps[:-1]:
        if x is not None:
            keep, other = parts(x, axis, distance)
        x = add(keep, swap(other, axis, distance))
        sums.append(x)
    x = add(x, swap(x, axis, steps[-1]))
    held = [([0], x)]
    for distance, weight in reversed(list(zip(steps, weights))):
        sent = jnp.concatenate([piece for _, piece in held]) if len(held) > 1 else x
        held.append(([at ^ weight for ats, _ in held for at in ats], swap(sent, axis, distance)))
    return sums + [x], held


def sum_halves(keep, other, axis):
    total = add(keep, swap(other, axis, 1))
    steps = [total]
    for distance in distances(axis)[1:]:
        total = add(total, swap(total, axis, distance))
        steps.append(total)
    return steps, [(0, total), (1, swap(total, axis, 1))]


def body(grad, weight, moment, second, gram_left, basis_left, gram_right, basis_right):
    block_left, block_right = grad.shape
    first = max(block_right - block_left, LANES)
    count = lax.axis_size("row")
    gram_right, basis_right = gram_right[0], basis_right[0]
    window, left, keep_right, other_right, keep_left, other_left = first_sends(
        count,
        first,
        grad,
        gram_right,
        basis_right,
        gram_left[0],
        basis_left[0],
        1.0 / (block_right * lax.axis_size("col")),
        1.0 / (block_left * count),
    )
    near = distances("row")[-2::-1]
    arrived = swap(window, "row", count // 2)
    gram_right, basis_right, _ = lax.optimization_barrier((gram_right, basis_right, arrived))
    grams, bases = spread([(0, gram_right)], "row", near), spread([(0, basis_right)], "row", near)
    others = spread([(count // 2, arrived)], "row", near)
    steps_right, sums_right = sum_halves(keep_right, other_right, "row")
    steps_left, sums_left = sum_stacked(keep_left, other_left, "col")
    left = gather_stacked(left, "col", [(steps_right[0], steps_left[-2]), (steps_right[-1], sums_left[min(1, len(sums_left) - 1)][1])])
    last, _ = lax.optimization_barrier((basis_right[:, first:], steps_right[-1]))
    last = [(d, swap(last, "row", d)) for d in range(count // 2, count)]
    new_gram_right, gh, gl, q_first = head(count, grams, bases, others, sums_right, first)
    new_weight, new_moment, new_second, basis_rows_right, basis_rows_left, new_gram_left = rest(
        gh, gl, q_first, (grad, weight, moment, second), bases, last, left, sums_left
    )
    return (
        new_weight,
        new_moment,
        new_second,
        new_gram_left[None],
        basis_rows_left[None],
        new_gram_right[None],
        basis_rows_right[None],
    )


def solution(mesh):
    specs = (
        P("row", "col"),
        P("row", "col"),
        P("row", "col"),
        P("row", "col"),
        P("row", "col", None),
        P("row", "col", None),
        P("col", "row", None),
        P("col", "row", None),
    )
    out_specs = specs[:3] + specs[4:]
    return jax.shard_map(body, mesh=mesh, in_specs=specs, out_specs=out_specs, check_vma=False)
```

```python
import functools
from itertools import zip_longest
import jax
import jax.numpy as jnp
from jax import lax
from jax.experimental import pallas as pl
from jax.experimental.pallas import tpu as pltpu
from jax.sharding import PartitionSpec as P

STAT_DECAY = 0.95
FIRST_DECAY = 0.9
SECOND_DECAY = 0.95
EPSILON = 1e-08
STEP_SIZE = 0.02
WEIGHT_DECAY = 0.01
LANES = 128
ROWS = 8
TILE = 256
VMEM_LIMIT = 56 * 2**20


def sub_row(x, k):
    return jnp.broadcast_to(x[k : k + 1, :], (ROWS, LANES))


def lane_col(x, c):
    return jnp.broadcast_to(x[:, c : c + 1], (ROWS, LANES))


def reciprocal(p):
    guess = pl.reciprocal(p, approx=True)
    return guess * (2.0 - p * guess)


def sum_tree(terms):
    while len(terms) > 1:
        terms = [a + b for a, b in zip(terms[::2], terms[1::2])]
    return terms[0]


def inverse_factor(rows, carry):
    count = LANES // ROWS
    rows = list(rows)
    subs = lax.broadcasted_iota(jnp.int32, (ROWS, LANES), 0)
    lanes = lax.broadcasted_iota(jnp.int32, (ROWS, LANES), 1)
    out = []
    for s in range(count):
        base = s * ROWS
        pivot = rows[s]
        here = (lanes >= base) & (lanes < base + ROWS)
        if s == 0 or not carry:
            cols = [lane_col(pivot, base + k) for k in range(ROWS)]
        ahead = range(base + ROWS, base + 2 * ROWS) if carry and s < count - 1 else ()
        across = [lane_col(pivot, c) for c in ahead]
        next_cols = [lane_col(rows[s + 1], c) for c in ahead]
        next_coeffs = [lane_col(rows[s + 1], base + k) for k in range(ROWS)] if ahead else None
        full = jnp.where(here, (lanes == subs + base).astype(jnp.float32), pivot)
        forward = full
        pivots = jnp.ones((ROWS, LANES), jnp.float32)
        yield
        for j in range(0, ROWS, 2):
            a, b, d = sub_row(cols[j], j), sub_row(cols[j], j + 1), sub_row(cols[j + 1], j + 1)
            det = a * d - b * b
            inv = reciprocal(det)
            pair = (subs == j) | (subs == j + 1)
            one = jnp.where(pair, jnp.where(subs == j, -1.0, 0.0), cols[j])
            two = jnp.where(pair, jnp.where(subs == j, 0.0, -1.0), cols[j + 1])
            for k in range(j + 2, min(j + 4, ROWS)):
                x, y = sub_row(cols[k], j), sub_row(cols[k], j + 1)
                change = one * (d * x - b * y) + two * (a * y - b * x)
                cols[k] = jnp.where(pair, 0.0, cols[k]) - change * inv
            yield
            one, two = (one * d - two * b) * inv, (two * a - one * b) * inv
            for k in range(j + 4, ROWS):
                x, y = sub_row(cols[k], j), sub_row(cols[k], j + 1)
                cols[k] = jnp.where(pair, 0.0, cols[k]) - (one * x + two * y)
            if carry:
                yield
                across = [
                    jnp.where(pair, 0.0, c) - (one * sub_row(c, j) + two * sub_row(c, j + 1)) for c in across
                ]
                yield
            full = jnp.where(pair, 0.0, full) - (one * sub_row(full, j) + two * sub_row(full, j + 1))
            inner = b * reciprocal(a)
            below = subs > j + 1
            lower = jnp.where(below, one, jnp.where(subs == j + 1, inner, 0.0))
            change = lower * sub_row(forward, j)
            if j + 2 < ROWS:
                change = change + jnp.where(below, two, 0.0) * sub_row(forward, j + 1)
            forward = forward - change
            pivots = jnp.where(subs == j, a, jnp.where(subs == j + 1, d - inner * b, pivots))
            yield
        out.append(jnp.where(lanes < base + ROWS, forward * lax.rsqrt(pivots), 0.0))
        if s < count - 1:
            if carry:
                cols = [
                    own - sum_tree([next_coeffs[k] * sub_row(c, k) for k in range(ROWS)])
                    for own, c in zip(next_cols, across)
                ]
            yield
            spread = [sub_row(full, k) for k in range(ROWS)]
            for i in range(s + 1, count):
                coeffs = next_coeffs if carry and i == s + 1 else [lane_col(rows[i], base + k) for k in range(ROWS)]
                rows[i] = jnp.where(here, 0.0, rows[i]) - sum_tree([coeffs[k] * spread[k] for k in range(ROWS)])
                yield
    return out


def in_turns(generators, fills):
    results = [None] * len(generators)
    live = list(enumerate(generators))
    fills = list(fills)
    total, turn, done = 250, 0, 0
    while live:
        for at, generator in list(live):
            try:
                next(generator)
            except StopIteration as stop:
                results[at] = stop.value
                live.remove((at, generator))
        turn += 1
        while done < len(fills) and done * total <= turn * len(fills):
            fills[done]()
            done += 1
    for fill in fills[done:]:
        fill()
    return results


def split(x):
    hi = x.astype(jnp.bfloat16)
    return hi, (x - hi.astype(jnp.float32)).astype(jnp.bfloat16)


def stack_left(x, axis):
    hi, lo = split(x)
    return jnp.concatenate([hi, hi, lo], axis=axis)


def stack_right(x, axis):
    hi, lo = split(x)
    return jnp.concatenate([hi, lo, hi], axis=axis)


def mm(a, b, dims):
    return lax.dot_general(a, b, (dims, ((), ())), preferred_element_type=jnp.float32)


def mm_nn(a, b):
    return mm(stack_left(a, 1), stack_right(b, 0), ((1,), (0,)))


def mm_nt(a, b):
    return mm(stack_left(a, 1), stack_right(b, 1), ((1,), (1,)))


def product(ah, al, bh, bl, dims):
    return mm(ah, bh, dims) + (mm(ah, bl, dims) + mm(al, bh, dims))


def block(i):
    return pl.ds(i * LANES, LANES) if isinstance(i, int) else pl.ds(pl.multiple_of(i * LANES, LANES), LANES)


class Chain:
    def __init__(self, z_ref, w_ref, q_ref):
        self.z, self.w, self.q = z_ref, w_ref, q_ref
        self.width = z_ref.shape[1]
        self.blocks = self.width // LANES

    def cross(self):
        hi, lo = split(self.z[self.width :, :])
        dims = ((0,), (0,))
        self.z[: self.width, :] = product(hi, lo, hi, lo, dims)
        self.w[...] = jnp.zeros_like(self.w)

    def look(self, j):
        self.before = block(lax.max(j - 1, 0))
        self.w_nt = stack_right(self.w[...], 1)
        at = block(j)
        low = mm(stack_left(self.z[at, self.before], 1), self.w_nt, ((1,), (1,)))
        diagonal = self.z[at, at] - mm_nt(low, low)
        return [diagonal[i * ROWS : (i + 1) * ROWS, :] for i in range(LANES // ROWS)]

    def fills(self):
        def rows_of_u():
            self.u = stack_right(mm_nn(self.w[...], self.z[self.before, :]), 0)

        def panel():
            p = mm(stack_left(self.z[:, self.before], 1), self.w_nt, ((1,), (1,)))
            self.q[:, self.before] = p[self.width :, :]
            self.p = stack_left(p, 1)

        def columns(at):
            stop = min(at + TILE, self.width)
            self.z[:, at:stop] -= mm(self.p, self.u[:, at:stop], ((1,), (0,)))

        return [rows_of_u, panel] + [functools.partial(columns, at) for at in range(0, self.width, TILE)]

    def store(self, out):
        for i, row in enumerate(out):
            self.w[i * ROWS : (i + 1) * ROWS, :] = row

    def finish(self):
        last = block(self.blocks - 1)
        self.q[:, last] = mm_nt(self.z[self.width :, last], self.w[...])


def run_chains(chains):
    def step_of(members):
        def step(j, carry):
            rows = [chain.look(j) for chain in members]
            fills = [fill for several in zip_longest(*[chain.fills() for chain in members]) for fill in several if fill]
            for chain, out in zip(members, in_turns([inverse_factor(r, len(members) == 1) for r in rows], fills)):
                chain.store(out)
            return carry

        return step

    start = 0
    for end in sorted({chain.blocks for chain in chains}):
        lax.fori_loop(start, end, step_of([chain for chain in chains if chain.blocks >= end]), 0)
        start = end
    for chain in chains:
        chain.finish()


class Copies:
    def __init__(self, semaphores):
        self.semaphores, self.used = semaphores, 0

    def start(self, source, target):
        copy = pltpu.make_async_copy(source, target, self.semaphores.at[self.used])
        self.used += 1
        copy.start()
        return copy


def wait(copies):
    for copy in copies:
        copy.wait()


def offsets(size):
    return size // LANES // 2 + 1


def pack_products(cols, out_ref, dims, scale):
    blocks = len(cols)
    for i in range(blocks):
        for o in range(offsets(blocks * LANES)):
            term = mm(cols[i], cols[(i + o) % blocks], dims)
            out_ref[block(i), block(o)] = (term * scale).astype(out_ref.dtype)


def first_kernel(count, scale_left, scale_right, grad_in, gram, basis, gram_left, basis_left, *refs):
    window_ref, both_ref, right_refs, left_refs = refs[0], refs[1], refs[2:4], refs[4:6]
    grad_ref, window_vmem, both_vmem, right, left, semaphores = refs[6:]
    rows, columns = grad_ref.shape
    copies = Copies(semaphores)
    window = half_window(gram.shape[1])
    width = window_vmem.shape[1] - window
    half = lax.div(2 * lax.axis_index("row"), count)
    at = pl.ds(pl.multiple_of(half * (gram.shape[1] - window), LANES), window)
    size = gram_left.shape[1]
    packing = [
        copies.start(gram.at[:, at], window_vmem.at[:, pl.ds(0, window)]),
        copies.start(basis.at[:, pl.ds(0, width)], window_vmem.at[:, pl.ds(window, width)]),
        copies.start(gram_left, both_vmem.at[:, pl.ds(0, size)]),
        copies.start(basis_left, both_vmem.at[:, pl.ds(size, size)]),
    ]
    loading = [copies.start(grad_in, grad_ref)]
    wait(packing)
    out = [copies.start(window_vmem, window_ref), copies.start(both_vmem, both_ref)]
    wait(loading)
    pack_products([grad_ref[:, block(i)] for i in range(columns // LANES)], right, ((0,), (0,)), scale_right)
    for axis, packed, targets in (("row", right, right_refs), ("col", left, left_refs)):
        if axis == "col":
            pack_products([grad_ref[block(i), :] for i in range(rows // LANES)], left, ((1,), (1,)), scale_left)
        own = lax.rem(lax.axis_index(axis), 2)
        size = packed.shape[0] // 2
        for side, target in zip((own, 1 - own), targets):
            at = pl.ds(pl.multiple_of(side * size, 2 * ROWS), size)
            out.append(copies.start(packed.at[at, :], target))
    wait(out)


def first_sends(count, width, grad, gram, basis, gram_left, basis_left, scale_left, scale_right):
    rows, columns = grad.shape
    right, left = (columns, offsets(columns) * LANES), (rows, offsets(rows) * LANES)
    window = (gram.shape[0], half_window(gram.shape[1]) + width)
    both = (gram_left.shape[0], 2 * gram_left.shape[1])
    f32, bf16 = jnp.float32, jnp.bfloat16
    return pl.pallas_call(
        functools.partial(first_kernel, count, scale_left, scale_right),
        out_shape=[jax.ShapeDtypeStruct(shape, f32) for shape in (window, both)]
        + [jax.ShapeDtypeStruct((shape[0] // 2, shape[1]), bf16) for shape in (right, right, left, left)],
        in_specs=any_specs(5),
        out_specs=any_specs(6),
        scratch_shapes=[
            pltpu.VMEM(grad.shape, bf16),
            pltpu.VMEM(window, f32),
            pltpu.VMEM(both, f32),
            pltpu.VMEM(right, bf16),
            pltpu.VMEM(left, bf16),
            pltpu.SemaphoreType.DMA((11,)),
        ],
        compiler_params=pltpu.CompilerParams(vmem_limit_bytes=VMEM_LIMIT),
    )(grad, gram, basis, gram_left, basis_left)


def rows_at(me, distance, rows):
    return pl.ds(pl.multiple_of((me ^ distance) * rows, ROWS), rows)


def new_gram(gram_ref, packed_ref, gh_ref, gl_ref):
    blocks = gram_ref.shape[0] // LANES
    count = offsets(gram_ref.shape[0])

    def put(i, k, term):
        value = gram_ref[block(i), block(k)] * STAT_DECAY + term
        gram_ref[block(i), block(k)] = value
        gh_ref[block(i), block(k)], gl_ref[block(i), block(k)] = split(value)

    for i in range(blocks):
        for o in range(count):
            k = (i + o) % blocks
            term = packed_ref[block(i), block(o)].astype(jnp.float32) * (1.0 - STAT_DECAY)
            put(i, k, term)
            if o > 0 and not (blocks % 2 == 0 and o == count - 1):
                put(k, i, term.T)


def image(z_ref, gh_ref, gl_ref, basis_ref):
    width = z_ref.shape[1]
    for at in range(0, width, TILE):
        stop = min(at + TILE, width)
        bh, bl = split(basis_ref[:, at:stop])
        z_ref[width:, at:stop] = product(gh_ref[...], gl_ref[...], bh, bl, ((1,), (0,)))


def own_rows(ref, me, rows):
    return ref[pl.ds(pl.multiple_of(me * rows, ROWS), rows), :]


def half_window(size):
    return -(-size // 2 // LANES) * LANES


def fill_halves(gram, half):
    size = gram.shape[0]
    window = half_window(size)
    rest = size - window
    near = half * window
    far = pl.ds(pl.multiple_of((1 - half) * rest, LANES), window)
    for i in range(rest // LANES):
        at = pl.ds(pl.multiple_of(near + i * LANES, LANES), LANES)
        gram[far, at] = gram[at, far].T


def packed_copies(copies, me, sums, packed):
    side = lax.rem(me, 2) if len(sums) > 1 else 0
    return [copies.start(piece, packed.at[rows_at(side, d, piece.shape[0]), :]) for d, piece in sums]


def take(refs, distances_of):
    return [(d, refs.pop(0)) for d in distances_of]


def head_kernel(count, owns, others, sums, *refs):
    refs = list(refs)
    gram_in, basis_in, other_in, sum_in = take(refs, owns), take(refs, owns), take(refs, others), take(refs, sums)
    rows_ref, gh_ref, gl_ref, q_ref, gram, packed, basis, gh, gl, rows_own, z, w, semaphores = refs
    me = lax.axis_index("row")
    copies = Copies(semaphores)
    width = basis.shape[1]
    half = lax.div(2 * me, count)
    window = half_window(gram.shape[0])
    others_at = pl.ds(pl.multiple_of((1 - half) * (gram.shape[0] - window), LANES), window)
    first, second = [], []
    for d, piece in gram_in:
        first.append(copies.start(piece, gram.at[rows_at(me, d, piece.shape[0]), :]))
    for d, piece in other_in:
        at = rows_at(me, d, piece.shape[0])
        first.append(copies.start(piece.at[:, pl.ds(0, window)], gram.at[at, others_at]))
    first += packed_copies(copies, me, sum_in, packed)
    for d, piece in basis_in:
        at = rows_at(me, d, piece.shape[0])
        second.append(copies.start(piece.at[:, pl.ds(0, width)], basis.at[at, :]))
    for d, piece in other_in:
        at = rows_at(me, d, piece.shape[0])
        second.append(copies.start(piece.at[:, pl.ds(window, width)], basis.at[at, :]))
    wait(first)
    if other_in:
        fill_halves(gram, half)
    new_gram(gram, packed, gh, gl)
    rows_own[...] = own_rows(gram, me, rows_own.shape[0])
    out = [copies.start(gh, gh_ref), copies.start(gl, gl_ref), copies.start(rows_own, rows_ref)]
    wait(second)
    image(z, gh, gl, basis)
    chain = Chain(z, w, q_ref)
    chain.cross()
    run_chains([chain])
    wait(out)


def any_specs(count):
    return [pl.BlockSpec(memory_space=pl.ANY)] * count


def chain_scratch(width, rows):
    return [pltpu.VMEM((width + rows, width), jnp.float32), pltpu.VMEM((LANES, LANES), jnp.float32)]


def head(count, grams, bases, others, sums, width):
    args = [p for group in (grams, bases, others, sums) for _, p in group]
    rows, size = grams[0][1].shape
    f32, bf16 = jnp.float32, jnp.bfloat16
    return pl.pallas_call(
        functools.partial(head_kernel, count, *[[d for d, _ in group] for group in (grams, others, sums)]),
        out_shape=[
            jax.ShapeDtypeStruct((rows, size), f32),
            jax.ShapeDtypeStruct((size, size), bf16),
            jax.ShapeDtypeStruct((size, size), bf16),
            jax.ShapeDtypeStruct((size, width), f32),
        ],
        in_specs=any_specs(len(args)),
        out_specs=[pl.BlockSpec(memory_space=pl.ANY)] * 3 + [pl.BlockSpec(memory_space=pltpu.VMEM)],
        scratch_shapes=[
            pltpu.VMEM((size, size), f32),
            pltpu.VMEM((size, offsets(size) * LANES), bf16),
            pltpu.VMEM((size, width), f32),
            pltpu.VMEM((size, size), bf16),
            pltpu.VMEM((size, size), bf16),
            pltpu.VMEM((rows, size), f32),
            *chain_scratch(width, size),
            pltpu.SemaphoreType.DMA((len(args) + len(others) + 3,)),
        ],
        compiler_params=pltpu.CompilerParams(vmem_limit_bytes=VMEM_LIMIT),
    )(*args)


def rest_kernel(bases, others, lefts, sums, *refs):
    refs = list(refs)
    gh_in, gl_in, q_in, grad_in, weight_in, moment_in, second_in = refs[:7]
    refs = refs[7:]
    basis_in, other_in, left_in, sum_in = take(refs, bases), take(refs, others), take(refs, lefts), take(refs, sums)
    weight_out, moment_out, second_out, right_rows, left_rows, gram_rows = refs[:6]
    (gh, gl, q_first, basis, qr, ql, gram_l, packed_l, basis_l, glh, gll, zr, wr, zl, wl) = refs[6:21]
    (grad, weight, moment, second, inner, turn, right_half, left_half, left_t, semaphores) = refs[21:]
    row, col = lax.axis_index("row"), lax.axis_index("col")
    copies = Copies(semaphores)
    first = q_first.shape[1]
    width = zr.shape[1]
    start = [copies.start(gh_in, gh), copies.start(gl_in, gl)]
    for d, piece in basis_in:
        at = rows_at(row, d, piece.shape[0])
        start.append(copies.start(piece.at[:, pl.ds(first, width)], basis.at[at, :]))
    for d, piece in other_in:
        start.append(copies.start(piece, basis.at[rows_at(row, d, piece.shape[0]), :]))
    project = [copies.start(q_in, q_first)]
    size = gram_l.shape[0]
    left_copies = []
    for ats, pieces in sum_in:
        rows = pieces.shape[0] // len(ats)
        for n, at in enumerate(ats):
            piece = pieces.at[pl.ds(n * rows, rows), :]
            left_copies.append(copies.start(piece, packed_l.at[rows_at(piece_index("col"), at, rows), :]))
    rows = left_rows.shape[0]
    for ats, pieces in left_in:
        for n, at in enumerate(ats):
            for i, ref in enumerate((gram_l, basis_l)):
                piece = pieces.at[pl.ds(n * rows, rows), pl.ds(i * size, size)]
                left_copies.append(copies.start(piece, ref.at[rows_at(col, at, rows), :]))
    tail = [copies.start(grad_in, grad), copies.start(moment_in, moment)]
    late = [copies.start(second_in, second), copies.start(weight_in, weight)]

    wait(start)
    image(zr, gh, gl, basis)
    wait(project)
    qh, qo = split(q_first[...])
    xh, xl = split(zr[width:, :])
    sh, sl = split(product(qh, qo, xh, xl, ((0,), (0,))))
    zr[width:, :] -= product(qh, qo, sh, sl, ((1,), (0,)))
    wait(left_copies)
    new_gram(gram_l, packed_l, glh, gll)
    gram_rows[...] = own_rows(gram_l, col, gram_rows.shape[0])
    image(zl, glh, gll, basis_l)
    right, left = Chain(zr, wr, qr), Chain(zl, wl, ql)
    right.cross()
    left.cross()
    right_half[:, :first] = q_first[...].astype(jnp.bfloat16)
    wait(tail)
    for i in range(grad.shape[0] // LANES):
        moment[block(i), :] = FIRST_DECAY * moment[block(i), :] + (1.0 - FIRST_DECAY) * grad[block(i), :].astype(
            jnp.float32
        )
    out = [copies.start(moment, moment_out)]
    run_chains([left, right] if left.blocks <= right.blocks else [right, left])
    left_half[...] = ql[...].astype(jnp.bfloat16)
    right_half[:, first:] = qr[...].astype(jnp.bfloat16)
    right_rows[:, :first] = own_rows(q_first, row, right_rows.shape[0])
    right_rows[:, first:] = own_rows(qr, row, right_rows.shape[0])
    left_rows[...] = own_rows(ql, col, left_rows.shape[0])

    rows, columns = grad.shape
    tiles = [pl.ds(at, min(TILE, columns - at)) for at in range(0, columns, TILE)]
    left_t[...] = left_half[...].T
    for tile in tiles:
        inner[:rows, tile] = mm(left_t[...], grad[:, tile], ((1,), (0,))).astype(jnp.bfloat16)
        half = moment[:, tile].astype(jnp.bfloat16)
        inner[rows:, tile] = mm(left_t[...], half, ((1,), (0,))).astype(jnp.bfloat16)
    wait(late)
    for tile in tiles:
        rotated = mm(inner[...], right_half[:, tile], ((1,), (0,)))
        rotated_grad, rotated_moment = rotated[:rows, :], rotated[rows:, :]
        new_second = SECOND_DECAY * second[:, tile] + (1.0 - SECOND_DECAY) * rotated_grad * rotated_grad
        second[:, tile] = new_second
        out.append(copies.start(second.at[:, tile], second_out.at[:, tile]))
        turn[:, tile] = (rotated_moment / (jnp.sqrt(new_second) + EPSILON)).astype(jnp.bfloat16)
    turned = mm(left_half[...], turn[...], ((1,), (0,))).astype(jnp.bfloat16)
    for tile in tiles:
        update = mm(turned, right_half[tile, :], ((1,), (1,)))
        old = weight[:, tile]
        weight[:, tile] = old - STEP_SIZE * (update + WEIGHT_DECAY * old)
        out.append(copies.start(weight.at[:, tile], weight_out.at[:, tile]))
    wait(out)


def rest(gh, gl, q_first, tiles, bases, others, lefts, sums):
    args = [gh, gl, q_first, *tiles] + [p for _, p in bases + others + lefts + sums]
    rows_r, size_r = bases[0][1].shape
    width = size_r - q_first.shape[1]
    rows_l, size_l = lefts[0][1].shape[0], lefts[0][1].shape[1] // 2
    tile = tiles[0].shape
    f32, bf16 = jnp.float32, jnp.bfloat16
    vmem, anywhere = pl.BlockSpec(memory_space=pltpu.VMEM), pl.BlockSpec(memory_space=pl.ANY)
    return pl.pallas_call(
        functools.partial(rest_kernel, *[[d for d, _ in group] for group in (bases, others, lefts, sums)]),
        out_shape=[
            jax.ShapeDtypeStruct(tile, f32),
            jax.ShapeDtypeStruct(tile, f32),
            jax.ShapeDtypeStruct(tile, f32),
            jax.ShapeDtypeStruct((rows_r, size_r), f32),
            jax.ShapeDtypeStruct((rows_l, size_l), f32),
            jax.ShapeDtypeStruct((rows_l, size_l), f32),
        ],
        in_specs=any_specs(len(args)),
        out_specs=[anywhere] * 3 + [vmem] * 3,
        scratch_shapes=[
            pltpu.VMEM((size_r, size_r), bf16),
            pltpu.VMEM((size_r, size_r), bf16),
            pltpu.VMEM((size_r, size_r - width), f32),
            pltpu.VMEM((size_r, width), f32),
            pltpu.VMEM((size_r, width), f32),
            pltpu.VMEM((size_l, size_l), f32),
            pltpu.VMEM((size_l, size_l), f32),
            pltpu.VMEM((size_l, offsets(size_l) * LANES), bf16),
            pltpu.VMEM((size_l, size_l), f32),
            pltpu.VMEM((size_l, size_l), bf16),
            pltpu.VMEM((size_l, size_l), bf16),
            *chain_scratch(width, size_r),
            *chain_scratch(size_l, size_l),
            pltpu.VMEM(tile, bf16),
            pltpu.VMEM(tile, f32),
            pltpu.VMEM(tile, f32),
            pltpu.VMEM(tile, f32),
            pltpu.VMEM((2 * tile[0], tile[1]), bf16),
            pltpu.VMEM(tile, bf16),
            pltpu.VMEM((size_r, size_r), bf16),
            pltpu.VMEM((size_l, size_l), bf16),
            pltpu.VMEM((size_l, size_l), bf16),
            pltpu.SemaphoreType.DMA((len(args) + 1 + 3 * (size_l // rows_l) + 2 * -(-tile[1] // TILE),)),
        ],
        compiler_params=pltpu.CompilerParams(vmem_limit_bytes=VMEM_LIMIT),
    )(*args)


def swap(x, axis, distance):
    count = lax.axis_size(axis)
    return lax.ppermute(x, axis, [(i, i ^ distance) for i in range(count)])


def distances(axis):
    count = lax.axis_size(axis)
    return [1 << b for b in range(count.bit_length() - 1)]


def spread(held, axis, steps):
    for distance in steps:
        held = held + [(at ^ distance, swap(piece, axis, distance)) for at, piece in held]
    return held


def parts(x, axis, distance):
    rows = x.shape[0] // 2
    own = lax.rem(lax.div(lax.axis_index(axis), distance), 2)
    return tuple(lax.dynamic_slice_in_dim(x, at * rows, rows, 0) for at in (own, 1 - own))


def gather_stacked(x, axis, after):
    held = [([0], x)]
    for n, distance in enumerate(reversed(distances(axis))):
        if 0 < n <= len(after):
            (ats, piece), (piece_after, _) = held[-1], lax.optimization_barrier((held[-1][1], after[n - 1]))
            held[-1] = (ats, piece_after)
        sent = jnp.concatenate([piece for _, piece in held]) if len(held) > 1 else x
        held.append(([at ^ distance for ats, _ in held for at in ats], swap(sent, axis, distance)))
    return held


def add(x, y):
    return (x.astype(jnp.float32) + y.astype(jnp.float32)).astype(x.dtype)


def piece_weights(axis):
    return [1 << n for n in reversed(range(len(distances(axis)) - 1))]


def piece_index(axis):
    me, index = lax.axis_index(axis), 0
    for distance, weight in zip(distances(axis), piece_weights(axis)):
        index = index + weight * lax.rem(lax.div(me, distance), 2)
    return index


def sum_stacked(keep, other, axis):
    steps, weights = distances(axis), piece_weights(axis)
    x = None
    sums = []
    for distance in steps[:-1]:
        if x is not None:
            keep, other = parts(x, axis, distance)
        x = add(keep, swap(other, axis, distance))
        sums.append(x)
    x = add(x, swap(x, axis, steps[-1]))
    held = [([0], x)]
    for distance, weight in reversed(list(zip(steps, weights))):
        sent = jnp.concatenate([piece for _, piece in held]) if len(held) > 1 else x
        held.append(([at ^ weight for ats, _ in held for at in ats], swap(sent, axis, distance)))
    return sums + [x], held


def sum_halves(keep, other, axis):
    total = add(keep, swap(other, axis, 1))
    steps = [total]
    for distance in distances(axis)[1:]:
        total = add(total, swap(total, axis, distance))
        steps.append(total)
    return steps, [(0, total), (1, swap(total, axis, 1))]


def body(grad, weight, moment, second, gram_left, basis_left, gram_right, basis_right):
    block_left, block_right = grad.shape
    first = max(block_right - block_left, LANES)
    count = lax.axis_size("row")
    gram_right, basis_right = gram_right[0], basis_right[0]
    window, left, keep_right, other_right, keep_left, other_left = first_sends(
        count,
        first,
        grad,
        gram_right,
        basis_right,
        gram_left[0],
        basis_left[0],
        1.0 / (block_right * lax.axis_size("col")),
        1.0 / (block_left * count),
    )
    near = distances("row")[-2::-1]
    arrived = swap(window, "row", count // 2)
    gram_right, basis_right, _ = lax.optimization_barrier((gram_right, basis_right, arrived))
    grams, bases = spread([(0, gram_right)], "row", near), spread([(0, basis_right)], "row", near)
    others = spread([(count // 2, arrived)], "row", near)
    steps_right, sums_right = sum_halves(keep_right, other_right, "row")
    steps_left, sums_left = sum_stacked(keep_left, other_left, "col")
    left = gather_stacked(left, "col", [(steps_right[0], steps_left[-2]), (steps_right[-1], sums_left[min(1, len(sums_left) - 1)][1])])
    last, _ = lax.optimization_barrier((basis_right[:, first:], steps_right[-1]))
    last = [(d, swap(last, "row", d)) for d in range(count // 2, count)]
    new_gram_right, gh, gl, q_first = head(count, grams, bases, others, sums_right, first)
    new_weight, new_moment, new_second, basis_rows_right, basis_rows_left, new_gram_left = rest(
        gh, gl, q_first, (grad, weight, moment, second), bases, last, left, sums_left
    )
    return (
        new_weight,
        new_moment,
        new_second,
        new_gram_left[None],
        basis_rows_left[None],
        new_gram_right[None],
        basis_rows_right[None],
    )


def solution(mesh):
    specs = (
        P("row", "col"),
        P("row", "col"),
        P("row", "col"),
        P("row", "col"),
        P("row", "col", None),
        P("row", "col", None),
        P("col", "row", None),
        P("col", "row", None),
    )
    out_specs = specs[:3] + specs[4:]
    return jax.shard_map(body, mesh=mesh, in_specs=specs, out_specs=out_specs, check_vma=False)
```

```python
import functools
from itertools import zip_longest
import jax
import jax.numpy as jnp
from jax import lax
from jax.experimental import pallas as pl
from jax.experimental.pallas import tpu as pltpu
from jax.sharding import PartitionSpec as P

STAT_DECAY = 0.95
FIRST_DECAY = 0.9
SECOND_DECAY = 0.95
EPSILON = 1e-08
STEP_SIZE = 0.02
WEIGHT_DECAY = 0.01
LANES = 128
ROWS = 8
TILE = 256
VMEM_LIMIT = 56 * 2**20


def sub_row(x, k):
    return jnp.broadcast_to(x[k : k + 1, :], (ROWS, LANES))


def lane_col(x, c):
    return jnp.broadcast_to(x[:, c : c + 1], (ROWS, LANES))


def reciprocal(p):
    guess = pl.reciprocal(p, approx=True)
    return guess * (2.0 - p * guess)


def sum_tree(terms):
    while len(terms) > 1:
        terms = [a + b for a, b in zip(terms[::2], terms[1::2])]
    return terms[0]


def inverse_factor(rows, carry):
    count = LANES // ROWS
    rows = list(rows)
    subs = lax.broadcasted_iota(jnp.int32, (ROWS, LANES), 0)
    lanes = lax.broadcasted_iota(jnp.int32, (ROWS, LANES), 1)
    out = []
    for s in range(count):
        base = s * ROWS
        pivot = rows[s]
        here = (lanes >= base) & (lanes < base + ROWS)
        if s == 0 or not carry:
            cols = [lane_col(pivot, base + k) for k in range(ROWS)]
        ahead = range(base + ROWS, base + 2 * ROWS) if carry and s < count - 1 else ()
        across = [lane_col(pivot, c) for c in ahead]
        next_cols = [lane_col(rows[s + 1], c) for c in ahead]
        next_coeffs = [lane_col(rows[s + 1], base + k) for k in range(ROWS)] if ahead else None
        full = jnp.where(here, (lanes == subs + base).astype(jnp.float32), pivot)
        forward = full
        pivots = jnp.ones((ROWS, LANES), jnp.float32)
        yield
        for j in range(0, ROWS, 2):
            a, b, d = sub_row(cols[j], j), sub_row(cols[j], j + 1), sub_row(cols[j + 1], j + 1)
            det = a * d - b * b
            guess = pl.reciprocal(det, approx=True)
            refine = 2.0 - det * guess
            inv = guess * refine
            pair = (subs == j) | (subs == j + 1)
            one = jnp.where(pair, jnp.where(subs == j, -1.0, 0.0), cols[j])
            two = jnp.where(pair, jnp.where(subs == j, 0.0, -1.0), cols[j + 1])
            for k in range(j + 2, min(j + 4, ROWS)):
                x, y = sub_row(cols[k], j), sub_row(cols[k], j + 1)
                change = one * (d * x - b * y) + two * (a * y - b * x)
                cols[k] = jnp.where(pair, 0.0, cols[k]) - (change * guess) * refine
            yield
            one, two = (one * d - two * b) * inv, (two * a - one * b) * inv
            for k in range(j + 4, ROWS):
                x, y = sub_row(cols[k], j), sub_row(cols[k], j + 1)
                cols[k] = jnp.where(pair, 0.0, cols[k]) - (one * x + two * y)
            if carry:
                yield
                across = [
                    jnp.where(pair, 0.0, c) - (one * sub_row(c, j) + two * sub_row(c, j + 1)) for c in across
                ]
                yield
            full = jnp.where(pair, 0.0, full) - (one * sub_row(full, j) + two * sub_row(full, j + 1))
            inner = b * reciprocal(a)
            below = subs > j + 1
            lower = jnp.where(below, one, jnp.where(subs == j + 1, inner, 0.0))
            change = lower * sub_row(forward, j)
            if j + 2 < ROWS:
                change = change + jnp.where(below, two, 0.0) * sub_row(forward, j + 1)
            forward = forward - change
            pivots = jnp.where(subs == j, a, jnp.where(subs == j + 1, d - inner * b, pivots))
            yield
        out.append(jnp.where(lanes < base + ROWS, forward * lax.rsqrt(pivots), 0.0))
        if s < count - 1:
            if carry:
                cols = [
                    own - sum_tree([next_coeffs[k] * sub_row(c, k) for k in range(ROWS)])
                    for own, c in zip(next_cols, across)
                ]
            yield
            spread = [sub_row(full, k) for k in range(ROWS)]
            for i in range(s + 1, count):
                coeffs = next_coeffs if carry and i == s + 1 else [lane_col(rows[i], base + k) for k in range(ROWS)]
                rows[i] = jnp.where(here, 0.0, rows[i]) - sum_tree([coeffs[k] * spread[k] for k in range(ROWS)])
                yield
    return out


def in_turns(generators, fills):
    results = [None] * len(generators)
    live = list(enumerate(generators))
    fills = list(fills)
    total, turn, done = 250, 0, 0
    while live:
        for at, generator in list(live):
            try:
                next(generator)
            except StopIteration as stop:
                results[at] = stop.value
                live.remove((at, generator))
        turn += 1
        while done < len(fills) and done * total <= turn * len(fills):
            fills[done]()
            done += 1
    for fill in fills[done:]:
        fill()
    return results


def split(x):
    hi = x.astype(jnp.bfloat16)
    return hi, (x - hi.astype(jnp.float32)).astype(jnp.bfloat16)


def stack_left(x, axis):
    hi, lo = split(x)
    return jnp.concatenate([hi, hi, lo], axis=axis)


def stack_right(x, axis):
    hi, lo = split(x)
    return jnp.concatenate([hi, lo, hi], axis=axis)


def mm(a, b, dims):
    return lax.dot_general(a, b, (dims, ((), ())), preferred_element_type=jnp.float32)


def mm_nn(a, b):
    return mm(stack_left(a, 1), stack_right(b, 0), ((1,), (0,)))


def mm_nt(a, b):
    return mm(stack_left(a, 1), stack_right(b, 1), ((1,), (1,)))


def product(ah, al, bh, bl, dims):
    return mm(ah, bh, dims) + (mm(ah, bl, dims) + mm(al, bh, dims))


def block(i):
    return pl.ds(i * LANES, LANES) if isinstance(i, int) else pl.ds(pl.multiple_of(i * LANES, LANES), LANES)


class Chain:
    def __init__(self, z_ref, w_ref, q_ref):
        self.z, self.w, self.q = z_ref, w_ref, q_ref
        self.width = z_ref.shape[1]
        self.blocks = self.width // LANES

    def cross(self):
        hi, lo = split(self.z[self.width :, :])
        dims = ((0,), (0,))
        self.z[: self.width, :] = product(hi, lo, hi, lo, dims)
        self.w[...] = jnp.zeros_like(self.w)

    def look(self, j):
        self.before = block(lax.max(j - 1, 0))
        self.w_nt = stack_right(self.w[...], 1)
        at = block(j)
        low = mm(stack_left(self.z[at, self.before], 1), self.w_nt, ((1,), (1,)))
        diagonal = self.z[at, at] - mm_nt(low, low)
        return [diagonal[i * ROWS : (i + 1) * ROWS, :] for i in range(LANES // ROWS)]

    def fills(self):
        def rows_of_u():
            self.u = stack_right(mm_nn(self.w[...], self.z[self.before, :]), 0)

        def panel():
            p = mm(stack_left(self.z[:, self.before], 1), self.w_nt, ((1,), (1,)))
            self.q[:, self.before] = p[self.width :, :]
            self.p = stack_left(p, 1)

        def columns(at):
            stop = min(at + TILE, self.width)
            self.z[:, at:stop] -= mm(self.p, self.u[:, at:stop], ((1,), (0,)))

        return [rows_of_u, panel] + [functools.partial(columns, at) for at in range(0, self.width, TILE)]

    def store(self, out):
        for i, row in enumerate(out):
            self.w[i * ROWS : (i + 1) * ROWS, :] = row

    def finish(self):
        last = block(self.blocks - 1)
        self.q[:, last] = mm_nt(self.z[self.width :, last], self.w[...])


def run_chains(chains):
    def step_of(members):
        def step(j, carry):
            rows = [chain.look(j) for chain in members]
            fills = [fill for several in zip_longest(*[chain.fills() for chain in members]) for fill in several if fill]
            for chain, out in zip(members, in_turns([inverse_factor(r, len(members) == 1) for r in rows], fills)):
                chain.store(out)
            return carry

        return step

    start = 0
    for end in sorted({chain.blocks for chain in chains}):
        lax.fori_loop(start, end, step_of([chain for chain in chains if chain.blocks >= end]), 0)
        start = end
    for chain in chains:
        chain.finish()


class Copies:
    def __init__(self, semaphores):
        self.semaphores, self.used = semaphores, 0

    def start(self, source, target):
        copy = pltpu.make_async_copy(source, target, self.semaphores.at[self.used])
        self.used += 1
        copy.start()
        return copy


def wait(copies):
    for copy in copies:
        copy.wait()


def offsets(size):
    return size // LANES // 2 + 1


def pack_products(cols, out_ref, dims, scale):
    blocks = len(cols)
    for i in range(blocks):
        for o in range(offsets(blocks * LANES)):
            term = mm(cols[i], cols[(i + o) % blocks], dims)
            out_ref[block(i), block(o)] = (term * scale).astype(out_ref.dtype)


def first_kernel(count, scale_left, scale_right, grad_in, gram, basis, gram_left, basis_left, *refs):
    window_ref, both_ref, right_refs, left_refs = refs[0], refs[1], refs[2:4], refs[4:6]
    grad_ref, window_vmem, both_vmem, right, left, semaphores = refs[6:]
    rows, columns = grad_ref.shape
    copies = Copies(semaphores)
    window = half_window(gram.shape[1])
    width = window_vmem.shape[1] - window
    half = lax.div(2 * lax.axis_index("row"), count)
    at = pl.ds(pl.multiple_of(half * (gram.shape[1] - window), LANES), window)
    size = gram_left.shape[1]
    packing = [
        copies.start(gram.at[:, at], window_vmem.at[:, pl.ds(0, window)]),
        copies.start(basis.at[:, pl.ds(0, width)], window_vmem.at[:, pl.ds(window, width)]),
        copies.start(gram_left, both_vmem.at[:, pl.ds(0, size)]),
        copies.start(basis_left, both_vmem.at[:, pl.ds(size, size)]),
    ]
    loading = [copies.start(grad_in, grad_ref)]
    wait(packing)
    out = [copies.start(window_vmem, window_ref), copies.start(both_vmem, both_ref)]
    wait(loading)
    pack_products([grad_ref[:, block(i)] for i in range(columns // LANES)], right, ((0,), (0,)), scale_right)
    for axis, packed, targets in (("row", right, right_refs), ("col", left, left_refs)):
        if axis == "col":
            pack_products([grad_ref[block(i), :] for i in range(rows // LANES)], left, ((1,), (1,)), scale_left)
        own = lax.rem(lax.axis_index(axis), 2)
        size = packed.shape[0] // 2
        for side, target in zip((own, 1 - own), targets):
            at = pl.ds(pl.multiple_of(side * size, 2 * ROWS), size)
            out.append(copies.start(packed.at[at, :], target))
    wait(out)


def first_sends(count, width, grad, gram, basis, gram_left, basis_left, scale_left, scale_right):
    rows, columns = grad.shape
    right, left = (columns, offsets(columns) * LANES), (rows, offsets(rows) * LANES)
    window = (gram.shape[0], half_window(gram.shape[1]) + width)
    both = (gram_left.shape[0], 2 * gram_left.shape[1])
    f32, bf16 = jnp.float32, jnp.bfloat16
    return pl.pallas_call(
        functools.partial(first_kernel, count, scale_left, scale_right),
        out_shape=[jax.ShapeDtypeStruct(shape, f32) for shape in (window, both)]
        + [jax.ShapeDtypeStruct((shape[0] // 2, shape[1]), bf16) for shape in (right, right, left, left)],
        in_specs=any_specs(5),
        out_specs=any_specs(6),
        scratch_shapes=[
            pltpu.VMEM(grad.shape, bf16),
            pltpu.VMEM(window, f32),
            pltpu.VMEM(both, f32),
            pltpu.VMEM(right, bf16),
            pltpu.VMEM(left, bf16),
            pltpu.SemaphoreType.DMA((11,)),
        ],
        compiler_params=pltpu.CompilerParams(vmem_limit_bytes=VMEM_LIMIT),
    )(grad, gram, basis, gram_left, basis_left)


def rows_at(me, distance, rows):
    return pl.ds(pl.multiple_of((me ^ distance) * rows, ROWS), rows)


def new_gram(gram_ref, packed_ref, gh_ref, gl_ref):
    blocks = gram_ref.shape[0] // LANES
    count = offsets(gram_ref.shape[0])

    def put(i, k, term):
        value = gram_ref[block(i), block(k)] * STAT_DECAY + term
        gram_ref[block(i), block(k)] = value
        gh_ref[block(i), block(k)], gl_ref[block(i), block(k)] = split(value)

    for i in range(blocks):
        for o in range(count):
            k = (i + o) % blocks
            term = packed_ref[block(i), block(o)].astype(jnp.float32) * (1.0 - STAT_DECAY)
            put(i, k, term)
            if o > 0 and not (blocks % 2 == 0 and o == count - 1):
                put(k, i, term.T)


def image(z_ref, gh_ref, gl_ref, basis_ref):
    width = z_ref.shape[1]
    for at in range(0, width, TILE):
        stop = min(at + TILE, width)
        bh, bl = split(basis_ref[:, at:stop])
        z_ref[width:, at:stop] = product(gh_ref[...], gl_ref[...], bh, bl, ((1,), (0,)))


def own_rows(ref, me, rows):
    return ref[pl.ds(pl.multiple_of(me * rows, ROWS), rows), :]


def half_window(size):
    return -(-size // 2 // LANES) * LANES


def fill_halves(gram, half):
    size = gram.shape[0]
    window = half_window(size)
    rest = size - window
    near = half * window
    far = pl.ds(pl.multiple_of((1 - half) * rest, LANES), window)
    for i in range(rest // LANES):
        at = pl.ds(pl.multiple_of(near + i * LANES, LANES), LANES)
        gram[far, at] = gram[at, far].T


def packed_copies(copies, me, sums, packed):
    side = lax.rem(me, 2) if len(sums) > 1 else 0
    return [copies.start(piece, packed.at[rows_at(side, d, piece.shape[0]), :]) for d, piece in sums]


def take(refs, distances_of):
    return [(d, refs.pop(0)) for d in distances_of]


def head_kernel(count, owns, others, sums, *refs):
    refs = list(refs)
    gram_in, basis_in, other_in, sum_in = take(refs, owns), take(refs, owns), take(refs, others), take(refs, sums)
    rows_ref, gh_ref, gl_ref, q_ref, gram, packed, basis, gh, gl, rows_own, z, w, semaphores = refs
    me = lax.axis_index("row")
    copies = Copies(semaphores)
    width = basis.shape[1]
    half = lax.div(2 * me, count)
    window = half_window(gram.shape[0])
    others_at = pl.ds(pl.multiple_of((1 - half) * (gram.shape[0] - window), LANES), window)
    first, second = [], []
    for d, piece in gram_in:
        first.append(copies.start(piece, gram.at[rows_at(me, d, piece.shape[0]), :]))
    for d, piece in other_in:
        at = rows_at(me, d, piece.shape[0])
        first.append(copies.start(piece.at[:, pl.ds(0, window)], gram.at[at, others_at]))
    first += packed_copies(copies, me, sum_in, packed)
    for d, piece in basis_in:
        at = rows_at(me, d, piece.shape[0])
        second.append(copies.start(piece.at[:, pl.ds(0, width)], basis.at[at, :]))
    for d, piece in other_in:
        at = rows_at(me, d, piece.shape[0])
        second.append(copies.start(piece.at[:, pl.ds(window, width)], basis.at[at, :]))
    wait(first)
    if other_in:
        fill_halves(gram, half)
    new_gram(gram, packed, gh, gl)
    rows_own[...] = own_rows(gram, me, rows_own.shape[0])
    out = [copies.start(gh, gh_ref), copies.start(gl, gl_ref), copies.start(rows_own, rows_ref)]
    wait(second)
    image(z, gh, gl, basis)
    chain = Chain(z, w, q_ref)
    chain.cross()
    run_chains([chain])
    wait(out)


def any_specs(count):
    return [pl.BlockSpec(memory_space=pl.ANY)] * count


def chain_scratch(width, rows):
    return [pltpu.VMEM((width + rows, width), jnp.float32), pltpu.VMEM((LANES, LANES), jnp.float32)]


def head(count, grams, bases, others, sums, width):
    args = [p for group in (grams, bases, others, sums) for _, p in group]
    rows, size = grams[0][1].shape
    f32, bf16 = jnp.float32, jnp.bfloat16
    return pl.pallas_call(
        functools.partial(head_kernel, count, *[[d for d, _ in group] for group in (grams, others, sums)]),
        out_shape=[
            jax.ShapeDtypeStruct((rows, size), f32),
            jax.ShapeDtypeStruct((size, size), bf16),
            jax.ShapeDtypeStruct((size, size), bf16),
            jax.ShapeDtypeStruct((size, width), f32),
        ],
        in_specs=any_specs(len(args)),
        out_specs=[pl.BlockSpec(memory_space=pl.ANY)] * 3 + [pl.BlockSpec(memory_space=pltpu.VMEM)],
        scratch_shapes=[
            pltpu.VMEM((size, size), f32),
            pltpu.VMEM((size, offsets(size) * LANES), bf16),
            pltpu.VMEM((size, width), f32),
            pltpu.VMEM((size, size), bf16),
            pltpu.VMEM((size, size), bf16),
            pltpu.VMEM((rows, size), f32),
            *chain_scratch(width, size),
            pltpu.SemaphoreType.DMA((len(args) + len(others) + 3,)),
        ],
        compiler_params=pltpu.CompilerParams(vmem_limit_bytes=VMEM_LIMIT),
    )(*args)


def rest_kernel(bases, others, lefts, sums, *refs):
    refs = list(refs)
    gh_in, gl_in, q_in, grad_in, weight_in, moment_in, second_in = refs[:7]
    refs = refs[7:]
    basis_in, other_in, left_in, sum_in = take(refs, bases), take(refs, others), take(refs, lefts), take(refs, sums)
    weight_out, moment_out, second_out, right_rows, left_rows, gram_rows = refs[:6]
    (gh, gl, q_first, basis, qr, ql, gram_l, packed_l, basis_l, glh, gll, zr, wr, zl, wl) = refs[6:21]
    (grad, weight, moment, second, inner, turn, right_half, left_half, left_t, semaphores) = refs[21:]
    row, col = lax.axis_index("row"), lax.axis_index("col")
    copies = Copies(semaphores)
    first = q_first.shape[1]
    width = zr.shape[1]
    start = [copies.start(gh_in, gh), copies.start(gl_in, gl)]
    for d, piece in basis_in:
        at = rows_at(row, d, piece.shape[0])
        start.append(copies.start(piece.at[:, pl.ds(first, width)], basis.at[at, :]))
    for d, piece in other_in:
        start.append(copies.start(piece, basis.at[rows_at(row, d, piece.shape[0]), :]))
    project = [copies.start(q_in, q_first)]
    size = gram_l.shape[0]
    left_copies = []
    for ats, pieces in sum_in:
        rows = pieces.shape[0] // len(ats)
        for n, at in enumerate(ats):
            piece = pieces.at[pl.ds(n * rows, rows), :]
            left_copies.append(copies.start(piece, packed_l.at[rows_at(piece_index("col"), at, rows), :]))
    rows = left_rows.shape[0]
    for ats, pieces in left_in:
        for n, at in enumerate(ats):
            for i, ref in enumerate((gram_l, basis_l)):
                piece = pieces.at[pl.ds(n * rows, rows), pl.ds(i * size, size)]
                left_copies.append(copies.start(piece, ref.at[rows_at(col, at, rows), :]))
    tail = [copies.start(grad_in, grad), copies.start(moment_in, moment)]
    late = [copies.start(second_in, second), copies.start(weight_in, weight)]

    wait(start)
    image(zr, gh, gl, basis)
    wait(project)
    qh, qo = split(q_first[...])
    xh, xl = split(zr[width:, :])
    sh, sl = split(product(qh, qo, xh, xl, ((0,), (0,))))
    zr[width:, :] -= product(qh, qo, sh, sl, ((1,), (0,)))
    wait(left_copies)
    new_gram(gram_l, packed_l, glh, gll)
    gram_rows[...] = own_rows(gram_l, col, gram_rows.shape[0])
    image(zl, glh, gll, basis_l)
    right, left = Chain(zr, wr, qr), Chain(zl, wl, ql)
    right.cross()
    left.cross()
    right_half[:, :first] = q_first[...].astype(jnp.bfloat16)
    wait(tail)
    for i in range(grad.shape[0] // LANES):
        moment[block(i), :] = FIRST_DECAY * moment[block(i), :] + (1.0 - FIRST_DECAY) * grad[block(i), :].astype(
            jnp.float32
        )
    out = [copies.start(moment, moment_out)]
    run_chains([left, right] if left.blocks <= right.blocks else [right, left])
    left_half[...] = ql[...].astype(jnp.bfloat16)
    right_half[:, first:] = qr[...].astype(jnp.bfloat16)
    right_rows[:, :first] = own_rows(q_first, row, right_rows.shape[0])
    right_rows[:, first:] = own_rows(qr, row, right_rows.shape[0])
    left_rows[...] = own_rows(ql, col, left_rows.shape[0])

    rows, columns = grad.shape
    tiles = [pl.ds(at, min(TILE, columns - at)) for at in range(0, columns, TILE)]
    left_t[...] = left_half[...].T
    for tile in tiles:
        inner[:rows, tile] = mm(left_t[...], grad[:, tile], ((1,), (0,))).astype(jnp.bfloat16)
        half = moment[:, tile].astype(jnp.bfloat16)
        inner[rows:, tile] = mm(left_t[...], half, ((1,), (0,))).astype(jnp.bfloat16)
    wait(late)
    for tile in tiles:
        rotated = mm(inner[...], right_half[:, tile], ((1,), (0,)))
        rotated_grad, rotated_moment = rotated[:rows, :], rotated[rows:, :]
        new_second = SECOND_DECAY * second[:, tile] + (1.0 - SECOND_DECAY) * rotated_grad * rotated_grad
        second[:, tile] = new_second
        out.append(copies.start(second.at[:, tile], second_out.at[:, tile]))
        turn[:, tile] = (rotated_moment / (jnp.sqrt(new_second) + EPSILON)).astype(jnp.bfloat16)
    turned = mm(left_half[...], turn[...], ((1,), (0,))).astype(jnp.bfloat16)
    for tile in tiles:
        update = mm(turned, right_half[tile, :], ((1,), (1,)))
        old = weight[:, tile]
        weight[:, tile] = old - STEP_SIZE * (update + WEIGHT_DECAY * old)
        out.append(copies.start(weight.at[:, tile], weight_out.at[:, tile]))
    wait(out)


def rest(gh, gl, q_first, tiles, bases, others, lefts, sums):
    args = [gh, gl, q_first, *tiles] + [p for _, p in bases + others + lefts + sums]
    rows_r, size_r = bases[0][1].shape
    width = size_r - q_first.shape[1]
    rows_l, size_l = lefts[0][1].shape[0], lefts[0][1].shape[1] // 2
    tile = tiles[0].shape
    f32, bf16 = jnp.float32, jnp.bfloat16
    vmem, anywhere = pl.BlockSpec(memory_space=pltpu.VMEM), pl.BlockSpec(memory_space=pl.ANY)
    return pl.pallas_call(
        functools.partial(rest_kernel, *[[d for d, _ in group] for group in (bases, others, lefts, sums)]),
        out_shape=[
            jax.ShapeDtypeStruct(tile, f32),
            jax.ShapeDtypeStruct(tile, f32),
            jax.ShapeDtypeStruct(tile, f32),
            jax.ShapeDtypeStruct((rows_r, size_r), f32),
            jax.ShapeDtypeStruct((rows_l, size_l), f32),
            jax.ShapeDtypeStruct((rows_l, size_l), f32),
        ],
        in_specs=any_specs(len(args)),
        out_specs=[anywhere] * 3 + [vmem] * 3,
        scratch_shapes=[
            pltpu.VMEM((size_r, size_r), bf16),
            pltpu.VMEM((size_r, size_r), bf16),
            pltpu.VMEM((size_r, size_r - width), f32),
            pltpu.VMEM((size_r, width), f32),
            pltpu.VMEM((size_r, width), f32),
            pltpu.VMEM((size_l, size_l), f32),
            pltpu.VMEM((size_l, size_l), f32),
            pltpu.VMEM((size_l, offsets(size_l) * LANES), bf16),
            pltpu.VMEM((size_l, size_l), f32),
            pltpu.VMEM((size_l, size_l), bf16),
            pltpu.VMEM((size_l, size_l), bf16),
            *chain_scratch(width, size_r),
            *chain_scratch(size_l, size_l),
            pltpu.VMEM(tile, bf16),
            pltpu.VMEM(tile, f32),
            pltpu.VMEM(tile, f32),
            pltpu.VMEM(tile, f32),
            pltpu.VMEM((2 * tile[0], tile[1]), bf16),
            pltpu.VMEM(tile, bf16),
            pltpu.VMEM((size_r, size_r), bf16),
            pltpu.VMEM((size_l, size_l), bf16),
            pltpu.VMEM((size_l, size_l), bf16),
            pltpu.SemaphoreType.DMA((len(args) + 1 + 3 * (size_l // rows_l) + 2 * -(-tile[1] // TILE),)),
        ],
        compiler_params=pltpu.CompilerParams(vmem_limit_bytes=VMEM_LIMIT),
    )(*args)


def swap(x, axis, distance):
    count = lax.axis_size(axis)
    return lax.ppermute(x, axis, [(i, i ^ distance) for i in range(count)])


def distances(axis):
    count = lax.axis_size(axis)
    return [1 << b for b in range(count.bit_length() - 1)]


def spread(held, axis, steps):
    for distance in steps:
        held = held + [(at ^ distance, swap(piece, axis, distance)) for at, piece in held]
    return held


def parts(x, axis, distance):
    rows = x.shape[0] // 2
    own = lax.rem(lax.div(lax.axis_index(axis), distance), 2)
    return tuple(lax.dynamic_slice_in_dim(x, at * rows, rows, 0) for at in (own, 1 - own))


def gather_stacked(x, axis, after):
    held = [([0], x)]
    for n, distance in enumerate(reversed(distances(axis))):
        if 0 < n <= len(after):
            (ats, piece), (piece_after, _) = held[-1], lax.optimization_barrier((held[-1][1], after[n - 1]))
            held[-1] = (ats, piece_after)
        sent = jnp.concatenate([piece for _, piece in held]) if len(held) > 1 else x
        held.append(([at ^ distance for ats, _ in held for at in ats], swap(sent, axis, distance)))
    return held


def add(x, y):
    return (x.astype(jnp.float32) + y.astype(jnp.float32)).astype(x.dtype)


def piece_weights(axis):
    return [1 << n for n in reversed(range(len(distances(axis)) - 1))]


def piece_index(axis):
    me, index = lax.axis_index(axis), 0
    for distance, weight in zip(distances(axis), piece_weights(axis)):
        index = index + weight * lax.rem(lax.div(me, distance), 2)
    return index


def sum_stacked(keep, other, axis):
    steps, weights = distances(axis), piece_weights(axis)
    x = None
    sums = []
    for distance in steps[:-1]:
        if x is not None:
            keep, other = parts(x, axis, distance)
        x = add(keep, swap(other, axis, distance))
        sums.append(x)
    x = add(x, swap(x, axis, steps[-1]))
    held = [([0], x)]
    for distance, weight in reversed(list(zip(steps, weights))):
        sent = jnp.concatenate([piece for _, piece in held]) if len(held) > 1 else x
        held.append(([at ^ weight for ats, _ in held for at in ats], swap(sent, axis, distance)))
    return sums + [x], held


def sum_halves(keep, other, axis):
    total = add(keep, swap(other, axis, 1))
    steps = [total]
    for distance in distances(axis)[1:]:
        total = add(total, swap(total, axis, distance))
        steps.append(total)
    return steps, [(0, total), (1, swap(total, axis, 1))]


def body(grad, weight, moment, second, gram_left, basis_left, gram_right, basis_right):
    block_left, block_right = grad.shape
    first = max(block_right - block_left, LANES)
    count = lax.axis_size("row")
    gram_right, basis_right = gram_right[0], basis_right[0]
    window, left, keep_right, other_right, keep_left, other_left = first_sends(
        count,
        first,
        grad,
        gram_right,
        basis_right,
        gram_left[0],
        basis_left[0],
        1.0 / (block_right * lax.axis_size("col")),
        1.0 / (block_left * count),
    )
    near = distances("row")[-2::-1]
    arrived = swap(window, "row", count // 2)
    gram_right, basis_right, _ = lax.optimization_barrier((gram_right, basis_right, arrived))
    grams, bases = spread([(0, gram_right)], "row", near), spread([(0, basis_right)], "row", near)
    others = spread([(count // 2, arrived)], "row", near)
    steps_right, sums_right = sum_halves(keep_right, other_right, "row")
    steps_left, sums_left = sum_stacked(keep_left, other_left, "col")
    left = gather_stacked(left, "col", [(steps_right[0], steps_left[-2]), (steps_right[-1], sums_left[min(1, len(sums_left) - 1)][1])])
    last, _ = lax.optimization_barrier((basis_right[:, first:], steps_right[-1]))
    last = [(d, swap(last, "row", d)) for d in range(count // 2, count)]
    new_gram_right, gh, gl, q_first = head(count, grams, bases, others, sums_right, first)
    new_weight, new_moment, new_second, basis_rows_right, basis_rows_left, new_gram_left = rest(
        gh, gl, q_first, (grad, weight, moment, second), bases, last, left, sums_left
    )
    return (
        new_weight,
        new_moment,
        new_second,
        new_gram_left[None],
        basis_rows_left[None],
        new_gram_right[None],
        basis_rows_right[None],
    )


def solution(mesh):
    specs = (
        P("row", "col"),
        P("row", "col"),
        P("row", "col"),
        P("row", "col"),
        P("row", "col", None),
        P("row", "col", None),
        P("col", "row", None),
        P("col", "row", None),
    )
    out_specs = specs[:3] + specs[4:]
    return jax.shard_map(body, mesh=mesh, in_specs=specs, out_specs=out_specs, check_vma=False)
```
